32 devices in a mesh: fsdp: 32 (over z, y, x, core).
Axes of the slice: x: 2, y: 2, z: 4, core: 2. Of those that a mesh axis runs over, the one named last changes fastest.
Arguments:
- tokens: bfloat16 [12608, 768], P('fsdp'), may hold values from -6 to 6
- ln1_gain: bfloat16 [768], P('fsdp'), may hold values from 0.5 to 1.5
- ln1_shift: bfloat16 [768], P('fsdp'), may hold values from -3 to 3
- qkv_weight: bfloat16 [768, 2304], P('fsdp'), may hold values from -0.21875 to 0.21875
- qv_bias: bfloat16 [2, 768], P(None, 'fsdp'), may hold values from -3 to 3
- proj_weight: bfloat16 [768, 768], P('fsdp'), may hold values from -1 to 1
- proj_bias: bfloat16 [768], P('fsdp'), may hold values from -3 to 3
- ln2_gain: bfloat16 [768], P('fsdp'), may hold values from 0.5 to 1.5
- ln2_shift: bfloat16 [768], P('fsdp'), may hold values from -3 to 3
- router_weight: bfloat16 [768, 4], P('fsdp'), may hold values from -0.15625 to 0.15625
- expert_in: bfloat16 [3072, 4, 768], P('fsdp'), may hold values from -0.21875 to 0.21875
- expert_in_bias: bfloat16 [3072, 4], P('fsdp'), may hold values from -3 to 3
- expert_out: bfloat16 [3072, 4, 768], P('fsdp'), may hold values from -0.3125 to 0.3125
- expert_out_bias: bfloat16 [4, 768], P(None, 'fsdp'), may hold values from -3 to 3
- routes: int32 [12608, 2], P('fsdp'), may hold values from 0 to 3, all different within a row; in each aligned block of 394 rows (0 to 393, 394 to 787, ...) at most 246 rows name the same one
- out_grad: bfloat16 [12608, 768], P('fsdp'), may hold values from -6 to 6
Outputs:
- block_out: bfloat16 [12608, 768], P('fsdp')
- tokens_grad: float32 [12608, 768], P('fsdp')
- ln1_gain_grad: float32 [768], P('fsdp')
- ln1_shift_grad: float32 [768], P('fsdp')
- qkv_weight_grad: float32 [768, 2304], P('fsdp')
- qv_bias_grad: float32 [2, 768], P(None, 'fsdp')
- proj_weight_grad: float32 [768, 768], P('fsdp')
- proj_bias_grad: float32 [768], P('fsdp')
- ln2_gain_grad: float32 [768], P('fsdp')
- ln2_shift_grad: float32 [768], P('fsdp')
- router_weight_grad: float32 [768, 4], P('fsdp')
- expert_in_grad: float32 [3072, 4, 768], P('fsdp')
- expert_in_bias_grad: float32 [3072, 4], P('fsdp')
- expert_out_grad: float32 [3072, 4, 768], P('fsdp')
- expert_out_bias_grad: float32 [4, 768], P(None, 'fsdp')
The draws below stay inside these ranges and needn't reach their ends.
Inputs may be any that keep to these rules, and one draw needn't show every extreme that they name: `routes`: each row names 2 different experts. Within the rows of one device no expert is named more than 246 times, and in some blocks one expert is named exactly 246 times.
All inputs are finite; a program needn't handle non-finite values.
Results may differ from the reference program's by a relative error of at most 0.015.
Values may be sent and summed in bfloat16 or wider, within the bound.
A program may use at most 320 MiB of HBM per device.

```python
import math
import jax
import jax.numpy as jnp
import numpy as np
from jax import lax

D = 768
HEADS = 12
HD = 64
FF = 3072
EXPERTS = 4
TOP = 2
LEN = 197
SEQ_DEV = 2
TOK_DEV = 394
CAP = 246
TOKENS = 12608
N_FSDP = 32


def strengthened(values, stream_key, source, target, parts, factor):
    owner, partner = [(jnp.arange(values.shape[position]) // (values.shape[position] // parts)).reshape([-1 if axis == position else 1 for axis in range(values.ndim)]) for position in (source, target)]
    chosen = jax.random.permutation(stream_key, parts)[partner]
    strong = (owner == chosen) | (owner == (partner + parts // 2) % parts)
    return jnp.where(strong, factor * values, values)


def levels(own_key, dims, split, smallest, top_value):
    loudness, own = 1.0, jax.random.fold_in(own_key, 6)
    for position, blocks in split:
        draws = jnp.exp(jax.random.uniform(jax.random.fold_in(own, position), (blocks,), jnp.float32, smallest / len(split), top_value / len(split)))
        loudness = loudness * jnp.repeat(draws, dims[position] // blocks).reshape([-1 if axis == position else 1 for axis in range(len(dims))])
    return loudness


def deal_out(rng, own, number, rows, count, top, most, slope):
    sequence = jax.random.permutation(rng, count)
    heavy_load, common = load_shares(count, rows * top, most, slope, True), load_shares(count, rows * top, most, slope, False)
    places = jnp.arange(count)

    def named(lengths, offset_by):
        used = int((lengths > 0).sum())
        fixed = max(1, used // 4)
        shifted = fixed + (places - fixed + offset_by * (used - fixed)) % max(1, count - fixed)
        return jnp.zeros((count,), jnp.int32).at[sequence[jnp.where(places < fixed, places, shifted)]].set(jnp.asarray(lengths, jnp.int32))

    lengths = jnp.where(number % 4 == 0, named(heavy_load, number // 4), named(common, number - number // 4 - 1))
    mixed = jax.random.permutation(jax.random.fold_in(own, 3), count)
    giver, sink = mixed[0:count // 2 * 2:2], mixed[1:count // 2 * 2:2]
    slack = jnp.minimum(lengths[giver] - 1, most - lengths[sink]) // 2
    slack = jnp.where((giver == sequence[0]) | (sink == sequence[0]) | (lengths[sink] == 0), 0, jnp.maximum(slack, 0))
    shifted = jax.random.randint(jax.random.fold_in(own, 4), (count // 2,), 0, 1 << 20) % (slack + 1)
    lengths = lengths.at[giver].add(-shifted).at[sink].add(shifted)
    members = jnp.searchsorted(jnp.cumsum(lengths), jnp.arange(rows * top), side="right").astype(jnp.int32)
    grid = members.reshape(top, rows).T
    grid = grid[jax.random.permutation(jax.random.fold_in(own, 1), rows)]
    offset_by = jax.random.randint(jax.random.fold_in(own, 2), (rows, 1), 0, top)
    return jnp.take_along_axis(grid, (jnp.arange(top)[None, :] + offset_by) % top, axis=1)


def load_shares(number_of, total, limit, lean, full):
    portions = [(1 << 20) // math.isqrt(rank ** lean) + 1 for rank in range(1, number_of + 1)]
    largest = limit if full else min(limit, max(-(-total // number_of), total * portions[0] // sum(portions)))
    least = 1 if total - largest >= number_of - 1 else 0
    counts, surplus = [largest] + [least] * (number_of - 1), total - largest - least * (number_of - 1)
    while surplus > 0:
        candidates = [i for i in range(1, number_of) if counts[i] < largest] or [i for i in range(1, number_of) if counts[i] < limit]
        whole, budget = sum([portions[i] for i in candidates]), surplus
        for i in candidates:
            addition = min(limit - counts[i], max(1, budget * portions[i] // whole), surplus)
            counts[i] = counts[i] + addition
            surplus = surplus - addition
    return np.array(counts)


def bell_draw(key, dims, scale, limit, shards=(), kind=jnp.bfloat16):
    array = scale * jax.random.normal(key, dims, jnp.float32)
    if shards:
        array = array * levels(key, dims, shards, -0.22, 0.18)
    return jnp.clip(array, -limit, limit).astype(kind)


def heavy_noise(rng, extent, scale, bound, pieces, heavy, kind=jnp.bfloat16):
    values = scale * jax.random.normal(rng, extent, jnp.float32)
    if pieces:
        values = values * levels(rng, extent, pieces, -0.22, 0.18)
    return jnp.clip(strengthened(values, jax.random.fold_in(rng, 3), *heavy), -bound, bound).astype(kind)


def setup_inputs(seed: int = 0) -> dict:
    arg_keys = jax.random.split(jax.random.key(seed), 17)
    tokens = bell_draw(arg_keys[0], (TOKENS, D), 1.0, 6.0, ((0, 32),))
    ln1_gain = jnp.clip(1.0 + 0.1 * jax.random.normal(arg_keys[1], (D,), jnp.float32), 0.5, 1.5).astype(jnp.bfloat16)
    ln1_shift = bell_draw(arg_keys[2], (D,), 0.3, 3.0, ((0, 32),))
    qkv_weight = bell_draw(arg_keys[3], (D, 3 * D), D ** -0.5, 0.21875, ((0, 32),))
    qv_bias = bell_draw(arg_keys[4], (2, D), 0.3, 3.0, ((1, 32),))
    proj_weight = bell_draw(arg_keys[5], (D, D), (D * 8 // LEN) ** -0.5, 1.0, ((0, 32),))
    proj_bias = bell_draw(arg_keys[6], (D,), 0.3, 3.0, ((0, 32),))
    ln2_gain = jnp.clip(1.0 + 0.1 * jax.random.normal(arg_keys[7], (D,), jnp.float32), 0.5, 1.5).astype(jnp.bfloat16)
    ln2_shift = bell_draw(arg_keys[8], (D,), 0.3, 3.0, ((0, 32),))
    router_weight = bell_draw(arg_keys[9], (D, EXPERTS), (2 * D) ** -0.5, 0.15625, ((0, 32),))
    expert_in = bell_draw(arg_keys[10], (FF, EXPERTS, D), D ** -0.5, 0.21875, ((0, 32),))
    expert_in_bias = bell_draw(arg_keys[11], (FF, EXPERTS), 0.3, 3.0, ((0, 32),))
    expert_out = bell_draw(arg_keys[12], (FF, EXPERTS, D), (FF // 8) ** -0.5, 0.3125, ((0, 32),))
    expert_out_bias = bell_draw(arg_keys[13], (EXPERTS, D), 0.3, 3.0, ((1, 32),))
    routes_keys = jax.random.split(jax.random.fold_in(arg_keys[14], 1), TOKENS // TOK_DEV)
    routes_turns = jax.random.permutation(jax.random.fold_in(arg_keys[14], 3), TOKENS // TOK_DEV)
    routes = jax.vmap(lambda own, number: deal_out(jax.random.fold_in(arg_keys[14], 2), own, number, TOK_DEV, EXPERTS, TOP, CAP, 1))(routes_keys, routes_turns).reshape((TOKENS, TOP))
    out_grad = heavy_noise(arg_keys[15], (TOKENS, D), 1.0, 6.0, ((0, 32),), (0, 1, 32, 2.75))
    return {"tokens": tokens, "ln1_gain": ln1_gain, "ln1_shift": ln1_shift, "qkv_weight": qkv_weight, "qv_bias": qv_bias, "proj_weight": proj_weight, "proj_bias": proj_bias, "ln2_gain": ln2_gain, "ln2_shift": ln2_shift, "router_weight": router_weight, "expert_in": expert_in, "expert_in_bias": expert_in_bias, "expert_out": expert_out, "expert_out_bias": expert_out_bias, "routes": routes, "out_grad": out_grad}


@jax.custom_vjp
def low(v):
    return lax.optimization_barrier(v.astype(jnp.bfloat16)).astype(jnp.float32)

@jax.custom_vjp
def low_back(v):
    return v

def low_keep(v):
    return (low(v), None)

def low_pass(kept, grad):
    return (grad,)

def back_keep(v):
    return (v, None)

def back_low(kept, grad):
    return (low(grad),)
low.defvjp(low_keep, low_pass)
low_back.defvjp(back_keep, back_low)

def both_ways(values):
    return low(low_back(values))

def layer_norm(values, gain_vec, shift_vec):
    row_mean = lax.optimization_barrier(jnp.mean(values, axis=-1, keepdims=True))
    centred = values - row_mean
    spread = lax.optimization_barrier(jnp.mean(centred * centred, axis=-1, keepdims=True))
    return centred * lax.rsqrt(spread + 1e-06) * gain_vec + shift_vec

def route_index(routes):
    flat_routes = routes.reshape(-1)
    onehot = (flat_routes[:, None] == jnp.arange(EXPERTS, dtype=jnp.int32)[None, :]).astype(jnp.int32)
    before = jnp.cumsum(onehot, axis=0) - onehot
    slot_number = lax.optimization_barrier(jnp.sum(before * onehot, axis=1))
    return (flat_routes * CAP + slot_number).astype(jnp.int32)

def block_forward(inputs, routes, params):
    gain1, shift1, w_qkv, bias_qv, w_proj, bias_proj, gain2, shift2, w_router, w_in, bias_in, w_out, bias_out = params
    highest = lax.Precision.HIGHEST
    row_count = inputs.shape[0]
    shape_four = (SEQ_DEV, LEN, HEADS, HD)
    normed = low(layer_norm(inputs, gain1, shift1))
    projected = jnp.dot(normed, w_qkv, precision=highest)
    queries = both_ways((projected[:, :D] + bias_qv[0]) * HD ** (-0.5))
    key_rows = both_ways(projected[:, D:2 * D])
    values = both_ways(projected[:, 2 * D:] + bias_qv[1])
    scores = low_back(jnp.einsum('sqhd,skhd->shqk', queries.reshape(shape_four), key_rows.reshape(shape_four), precision=highest))
    probs_low = low(jax.nn.softmax(scores, axis=-1))
    attended = jnp.einsum('shqk,skhd->sqhd', probs_low, values.reshape(shape_four), precision=highest)
    attended = both_ways(attended.reshape(row_count, D))
    branch = low_back(jnp.dot(attended, w_proj, precision=highest) + bias_proj)
    middle = inputs + branch
    normed2 = low(layer_norm(middle, gain2, shift2))
    gate_probs = jax.nn.softmax(jnp.dot(normed2, w_router, precision=highest), axis=-1)
    slot_index = route_index(routes)
    onehot = (slot_index[:, None] == jnp.arange(EXPERTS * CAP, dtype=jnp.int32)[None, :]).astype(jnp.float32)
    onehot = onehot.reshape(row_count, TOP, EXPERTS * CAP)
    picks = (routes[:, :, None] == jnp.arange(EXPERTS, dtype=jnp.int32)[None, None, :]).astype(jnp.float32)
    chosen = lax.optimization_barrier(jnp.sum(gate_probs[:, None, :] * picks, axis=2))
    combine = low(lax.optimization_barrier(jnp.sum(onehot * chosen[:, :, None], axis=1)))
    dispatch = lax.optimization_barrier(jnp.sum(onehot, axis=1))
    slot_rows = low_back(jnp.dot(dispatch.T, normed2, precision=highest)).reshape(EXPERTS, CAP, D)
    pre_act = low_back(jnp.einsum('ecd,fed->ecf', slot_rows, w_in, precision=highest) + bias_in.T[:, None, :])
    hidden = low(jax.nn.gelu(pre_act, approximate=True))
    result = both_ways(jnp.einsum('ecf,fed->ecd', hidden, w_out, precision=highest) + bias_out[:, None, :])
    mixture = low_back(jnp.dot(combine, result.reshape(EXPERTS * CAP, D), precision=highest))
    return middle + mixture

def reference(tokens, ln1_gain, ln1_shift, qkv_weight, qv_bias, proj_weight, proj_bias, ln2_gain, ln2_shift, router_weight, expert_in, expert_in_bias, expert_out, expert_out_bias, routes, out_grad):
    weights = tuple((w.astype(jnp.float32) for w in (ln1_gain, ln1_shift, qkv_weight, qv_bias, proj_weight, proj_bias, ln2_gain, ln2_shift, router_weight, expert_in, expert_in_bias, expert_out, expert_out_bias)))
    route_blocks = routes.reshape(N_FSDP, TOK_DEV, TOP)

    def forward(inputs, *params):

        def one_block(carried, block_pair):
            return (carried, jax.checkpoint(block_forward)(block_pair[0], block_pair[1], params))
        _, outputs = lax.scan(one_block, jnp.zeros((), jnp.float32), (inputs.reshape(N_FSDP, TOK_DEV, D), route_blocks))
        return outputs.reshape(TOKENS, D)
    result, pull = jax.vjp(forward, tokens.astype(jnp.float32), *weights)
    grads = pull(out_grad.astype(jnp.float32))
    return (result.astype(jnp.bfloat16), grads[0], grads[1], grads[2], grads[3], grads[4], grads[5], grads[6], grads[7], grads[8], grads[9], grads[10], grads[11], grads[12], grads[13])
```

```python
import functools

import jax
import jax.numpy as jnp
from jax import lax
from jax.sharding import PartitionSpec as P

HEADS = 12
HD = 64
EXPERTS = 4
TOP = 2
LEN = 197
SEQ_DEV = 2
SLOTS = 256
PLANE = 2 * EXPERTS
LANES = 128


def layer_norm(values, gain_vec, shift_vec):
    row_mean = jnp.mean(values, axis=-1, keepdims=True)
    centred = values - row_mean
    spread = jnp.mean(centred * centred, axis=-1, keepdims=True)
    return centred * lax.rsqrt(spread + 1e-06) * gain_vec + shift_vec


def gelu_tanh(values):
    return jax.nn.gelu(values, approximate=True)


def take_columns(block, widths):
    pieces, at = [], 0
    for width in widths:
        pieces.append(block[:, at : at + width])
        at += width
    return pieces


def dot_f32(left, right, left_dim, right_dim):
    return lax.dot_general(
        left,
        right,
        (((left_dim,), (right_dim,)), ((), ())),
        preferred_element_type=jnp.float32,
    )


def to_chip(array, k, n_dev):
    return lax.ppermute(array, "fsdp", [(i, i ^ (2 * k)) for i in range(n_dev)])


def to_core(array, n_dev):
    return lax.ppermute(array, "fsdp", [(i, i ^ 1) for i in range(n_dev)])


def along_line(array, step, n_dev, first, last):
    pairs = [
        (i, i + step * PLANE) for i in range(n_dev) if first <= i // PLANE <= last
    ]
    return lax.ppermute(array, "fsdp", pairs)


def around_line(array, shift, n_dev):
    return lax.ppermute(array, "fsdp", [(i, (i + shift * PLANE) % n_dev) for i in range(n_dev)])


def gather_direct(array, n_dev):
    return [array] + [around_line(array, s, n_dev) for s in range(1, n_dev // PLANE)]


def gather_line(array, n_dev, plane):
    if n_dev // PLANE != 4:
        return gather_direct(array, n_dev)
    up1 = along_line(array, 1, n_dev, 0, 2)
    down1 = along_line(array, -1, n_dev, 1, 3)
    up2 = along_line(up1, 1, n_dev, 1, 2)
    down2 = along_line(down1, -1, n_dev, 1, 2)
    up3 = along_line(up2, 1, n_dev, 2, 2)
    down3 = along_line(down2, -1, n_dev, 1, 1)
    return [
        array,
        jnp.where(plane == 0, down3, up1),
        jnp.where(plane >= 2, up2, down2),
        jnp.where(plane == 3, up3, down1),
    ]


def scatter_direct(slots, n_dev):
    total = slots[0].astype(jnp.float32)
    for s in range(1, n_dev // PLANE):
        total = total + around_line(slots[s], -s, n_dev).astype(jnp.float32)
    return total


def scatter_line(slots, n_dev):
    if n_dev // PLANE != 4:
        return scatter_direct(slots, n_dev)
    f32, low = jnp.float32, jnp.bfloat16

    def plus(mine, got):
        return (mine.astype(f32) + got.astype(f32)).astype(low)

    up = along_line(slots[1], 1, n_dev, 0, 0)
    down = along_line(slots[3], -1, n_dev, 3, 3)
    up = along_line(plus(slots[2], up), 1, n_dev, 0, 1)
    down = along_line(plus(slots[2], down), -1, n_dev, 2, 3)
    up = along_line(plus(slots[3], up), 1, n_dev, 0, 2)
    down = along_line(plus(slots[1], down), -1, n_dev, 1, 3)
    return slots[0].astype(f32) + up.astype(f32) + down.astype(f32)


def on_device(
    n_dev,
    tokens,
    ln1_gain,
    ln1_shift,
    qkv_weight,
    qv_bias,
    proj_weight,
    proj_bias,
    ln2_gain,
    ln2_shift,
    router_weight,
    expert_in,
    expert_in_bias,
    expert_out,
    expert_out_bias,
    routes,
    out_grad,
):
    highest = lax.Precision.HIGHEST
    f32 = jnp.float32
    low = jnp.bfloat16
    row_count, model_width = tokens.shape
    shape_four = (SEQ_DEV, LEN, HEADS, HD)
    query_scale = HD ** (-0.5)
    own = qkv_weight.shape[0]
    units = expert_in.shape[0]
    planes = n_dev // PLANE
    each = range(EXPERTS)
    wide = 4 * model_width
    here = lax.axis_index("fsdp")
    core = here % 2
    chip = (here // 2) % EXPERTS
    plane = here // PLANE

    def owner_dense(j):
        s, k, c = j % planes, (j // planes) % EXPERTS, j // (planes * EXPERTS)
        return ((plane - s + planes) % planes) * PLANE + (chip ^ k) * 2 + (core ^ c)

    def owner_units(j):
        k, s, c = j % EXPERTS, (j // EXPERTS) % planes, j // (planes * EXPERTS)
        return ((plane - s + planes) % planes) * PLANE + (chip ^ k) * 2 + (core ^ c)

    devices = jnp.arange(n_dev, dtype=jnp.int32)
    sort_dense = (devices[:, None] == owner_dense(devices)[None, :]).astype(low)
    sort_units = (devices[:, None] == owner_units(devices)[None, :]).astype(low)
    features = jnp.arange(model_width, dtype=jnp.int32)
    home = owner_dense(features // own) * own + features % own
    sort_rows = (features[:, None] == home[None, :]).astype(low)

    def plane_gather(weight):
        flat = weight.reshape(units, EXPERTS * model_width)
        pieces = []
        for k in each:
            piece = lax.dynamic_slice_in_dim(flat, (chip ^ k) * model_width, model_width, axis=1)
            pieces.append(to_chip(piece, k, n_dev) if k else piece)
        return jnp.concatenate(pieces, axis=0)

    small_parts = [
        ln1_gain,
        ln1_shift,
        qv_bias.reshape(-1),
        proj_bias,
        ln2_gain,
        ln2_shift,
        router_weight.T.reshape(-1),
        expert_out_bias.reshape(-1),
        expert_in_bias.T.reshape(-1),
    ]
    small_widths = [p.shape[0] for p in small_parts]
    small_total = sum(small_widths)
    small_room = own * LANES
    small_mine = jnp.pad(jnp.concatenate(small_parts), (0, small_room - small_total))
    dense_mine = jnp.concatenate(
        [qkv_weight, proj_weight, small_mine.reshape(own, LANES)], axis=1
    )
    column = jnp.concatenate(gather_direct(dense_mine, n_dev), axis=0)
    in_plane = plane_gather(expert_in)
    out_plane = plane_gather(expert_out)
    blocks = [column] + [to_chip(column, k, n_dev) for k in range(1, EXPERTS)]
    blocks = blocks + [to_core(b, n_dev) for b in blocks]
    dense = jnp.concatenate(blocks, axis=0)

    def full_weight(piece):
        half = jnp.concatenate(gather_line(piece, n_dev, plane), axis=0)
        return half, to_core(half, n_dev)

    w_in = full_weight(in_plane)
    w_out = full_weight(out_plane)

    w_qkv = dense[:, : 3 * model_width]
    w_proj = dense[:, 3 * model_width : wide]
    small = dense[:, wide:].reshape(n_dev, small_room)
    small = dot_f32(sort_dense, small, 1, 0).astype(low)
    gain1, shift1, bias_qv, bias_proj, gain2, shift2, w_router, bias_out, bias_in = take_columns(
        small, small_widths
    )
    gain1 = gain1.reshape(-1).astype(f32)
    shift1 = shift1.reshape(-1).astype(f32)
    gain2 = gain2.reshape(-1).astype(f32)
    shift2 = shift2.reshape(-1).astype(f32)
    bias_proj = bias_proj.reshape(-1).astype(f32)
    bias_q = bias_qv[:, :own].reshape(-1).astype(f32)
    bias_v = bias_qv[:, own:].reshape(-1).astype(f32)
    w_router = jnp.stack([p.reshape(-1) for p in take_columns(w_router, [own] * EXPERTS)])
    bias_out = jnp.stack([p.reshape(-1) for p in take_columns(bias_out, [own] * EXPERTS)])
    mine = (jnp.arange(EXPERTS, dtype=jnp.int32) == chip).astype(f32)
    bias_out = jnp.sum(bias_out.astype(f32) * mine[:, None], axis=0)
    bias_in = jnp.stack(take_columns(bias_in, [units] * EXPERTS)).astype(f32)
    bias_in = jnp.sum(bias_in * mine[:, None, None], axis=0).astype(low)
    bias_in = dot_f32(sort_units, bias_in, 0, 0).reshape(2, n_dev * units // 2)

    experts = jnp.arange(EXPERTS, dtype=jnp.int32)[None, :]
    pick = [(routes[:, j : j + 1] == experts).astype(f32) for j in range(TOP)]
    picked = pick[0] + pick[1]
    tri = jnp.arange(row_count)[:, None] > jnp.arange(row_count)[None, :]
    before = dot_f32(tri.astype(low), picked.astype(low), 1, 0)
    slot_ids = jnp.arange(EXPERTS * SLOTS, dtype=jnp.int32)[None, :]
    hit = []
    for j in range(TOP):
        slot = jnp.sum(pick[j] * before, axis=1, keepdims=True).astype(jnp.int32)
        hit.append(slot_ids == (routes[:, j : j + 1] ^ chip) * SLOTS + slot)
    dispatch = (hit[0] | hit[1]).astype(low)

    inputs = tokens.astype(f32)
    normed_full, norm1_pull = jax.vjp(layer_norm, inputs, gain1, shift1)
    normed = dot_f32(normed_full.astype(low), sort_rows, 1, 0).astype(low)
    projected = jnp.dot(normed, w_qkv, preferred_element_type=f32)
    queries = ((projected[:, :model_width] + bias_q) * query_scale).astype(low).reshape(shape_four)
    key_rows = projected[:, model_width : 2 * model_width].astype(low).reshape(shape_four)
    values = (projected[:, 2 * model_width :] + bias_v).astype(low).reshape(shape_four)
    scores = jnp.einsum("sqhd,skhd->shqk", queries, key_rows, preferred_element_type=f32)
    exp_scores = jnp.exp(scores - jnp.max(scores, axis=-1, keepdims=True))
    probs_full = exp_scores / jnp.sum(exp_scores, axis=-1, keepdims=True)
    probs_low = probs_full.astype(low)
    attended = jnp.einsum("shqk,skhd->sqhd", probs_low, values, preferred_element_type=f32)
    attended = attended.reshape(row_count, model_width).astype(low)
    attended = dot_f32(attended, sort_rows, 1, 0).astype(low)
    middle = inputs + jnp.dot(attended, w_proj, preferred_element_type=f32) + bias_proj
    normed2_full, norm2_pull = jax.vjp(layer_norm, middle, gain2, shift2)
    normed2 = normed2_full.astype(low)
    gate_probs = jax.nn.softmax(dot_f32(normed2, w_router, 1, 1), axis=-1)
    chosen = [jnp.sum(gate_probs * pick[j], axis=1, keepdims=True) for j in range(TOP)]
    combine = (jnp.where(hit[0], chosen[0], 0.0) + jnp.where(hit[1], chosen[1], 0.0)).astype(low)

    def exchange(rows):
        pieces = [rows[k * SLOTS : (k + 1) * SLOTS] for k in each]
        pieces = [to_chip(p, k, n_dev) if k else p for k, p in enumerate(pieces)]
        return jnp.concatenate(pieces, axis=0)

    slot_rows = exchange(dot_f32(dispatch, normed2, 0, 0).astype(low))
    grad_result = exchange(dot_f32(combine, out_grad, 0, 0).astype(low))

    hidden, grad_pre, pulls = [], [], []
    for c in range(2):
        pre_act = dot_f32(slot_rows, w_in[c], 1, 1) + bias_in[c]
        out, pull = jax.vjp(gelu_tanh, pre_act)
        hidden.append(out.astype(low))
        pulls.append(pull)
    result = dot_f32(hidden[0], w_out[0], 1, 0) + dot_f32(hidden[1], w_out[1], 1, 0)
    result = exchange((result + bias_out).astype(low))
    for c in range(2):
        grad_pre.append(pulls[c](dot_f32(grad_result, w_out[c], 1, 1))[0].astype(low))
    grad_slots = dot_f32(grad_pre[0], w_in[0], 1, 0) + dot_f32(grad_pre[1], w_in[1], 1, 0)
    grad_slots = exchange(grad_slots.astype(low))

    def scatter_units(left, right):
        theirs = to_core(dot_f32(left[1], right, 0, 0).astype(low), n_dev)
        total = (dot_f32(left[0], right, 0, 0) + theirs.astype(f32)).astype(low)
        span = EXPERTS * units
        slots = [total[s * span : (s + 1) * span] for s in range(planes)]
        total = scatter_line(slots, n_dev).astype(low)
        pieces = [total[k * units : (k + 1) * units] for k in each]
        pieces = [to_chip(p, k, n_dev) if k else p for k, p in enumerate(pieces)]
        low_bit, high_bit = (chip & 1) == 1, (chip & 2) == 2
        pieces = [jnp.where(low_bit, pieces[k ^ 1], pieces[k]) for k in each]
        pieces = [jnp.where(high_bit, pieces[k ^ 2], pieces[k]) for k in each]
        return jnp.stack(pieces, axis=1).astype(f32)

    expert_out_mine = scatter_units(hidden, grad_result)
    expert_in_mine = scatter_units(grad_pre, slot_rows)
    grad_bias_in = jnp.concatenate([jnp.sum(g.astype(f32), axis=0) for g in grad_pre])
    grad_bias_in = jnp.dot(
        sort_units.astype(f32), grad_bias_in.reshape(n_dev, units), precision=highest
    )
    grad_bias_in = (mine[None, :, None] * grad_bias_in[:, None, :]).reshape(n_dev, EXPERTS * units)
    grad_bias_out = mine[:, None] * jnp.sum(grad_result.astype(f32), axis=0)[None, :]

    block_out = (middle + jnp.dot(combine, result, preferred_element_type=f32)).astype(low)

    grad_top = out_grad.astype(f32)
    slot_dots = dot_f32(out_grad, result, 1, 1)
    grad_gates = sum(
        pick[j] * jnp.sum(jnp.where(hit[j], slot_dots, 0.0), axis=1, keepdims=True)
        for j in range(TOP)
    )
    grad_logits = gate_probs * (
        grad_gates - jnp.sum(gate_probs * grad_gates, axis=-1, keepdims=True)
    )
    grad_router = jnp.dot(grad_logits.T, normed2.astype(f32), precision=highest)
    grad_normed2 = jnp.dot(grad_logits, w_router.astype(f32), precision=highest)
    grad_normed2 = grad_normed2 + jnp.dot(dispatch, grad_slots, preferred_element_type=f32)
    grad_mid_norm, grad_gain2, grad_shift2 = norm2_pull(grad_normed2)
    grad_middle = grad_top + grad_mid_norm

    grad_branch = grad_middle.astype(low)
    grad_bias_proj = jnp.sum(grad_branch.astype(f32), axis=0)
    grad_proj = dot_f32(attended, grad_branch, 0, 0)
    grad_attended = dot_f32(grad_branch, w_proj, 1, 1).astype(low)
    grad_attended = dot_f32(grad_attended, sort_rows, 1, 1).astype(low).reshape(shape_four)
    grad_probs = jnp.einsum("sqhd,skhd->shqk", grad_attended, values, preferred_element_type=f32)
    grad_values = jnp.einsum(
        "shqk,sqhd->skhd", probs_low, grad_attended, preferred_element_type=f32
    ).astype(low)
    grad_scores = (
        probs_full * (grad_probs - jnp.sum(probs_full * grad_probs, axis=-1, keepdims=True))
    ).astype(low)
    grad_queries = jnp.einsum(
        "shqk,skhd->sqhd", grad_scores, key_rows, preferred_element_type=f32
    ).astype(low)
    grad_keys = jnp.einsum(
        "shqk,sqhd->skhd", grad_scores, queries, preferred_element_type=f32
    ).astype(low)
    grad_query_pre = grad_queries.astype(f32).reshape(row_count, model_width) * query_scale
    grad_values = grad_values.reshape(row_count, model_width)
    grad_projected = jnp.concatenate(
        [grad_query_pre.astype(low), grad_keys.reshape(row_count, model_width), grad_values],
        axis=1,
    )
    grad_qkv = dot_f32(normed, grad_projected, 0, 0)
    grad_normed = dot_f32(grad_projected, w_qkv, 1, 1)
    upper = grad_normed.astype(low)
    lower = (grad_normed - upper.astype(f32)).astype(low)
    grad_normed = dot_f32(upper, sort_rows, 1, 1) + dot_f32(lower, sort_rows, 1, 1)
    grad_in_norm, grad_gain1, grad_shift1 = norm1_pull(grad_normed)
    tokens_grad = grad_middle + grad_in_norm

    def by_owner(rows):
        return rows.reshape(-1, n_dev, rows.shape[-1] // n_dev).transpose(1, 0, 2).reshape(n_dev, -1)

    small_grads = jnp.concatenate(
        [
            by_owner(
                jnp.concatenate(
                    [
                        jnp.stack(
                            [
                                grad_gain1,
                                grad_shift1,
                                jnp.sum(grad_query_pre, axis=0),
                                jnp.sum(grad_values.astype(f32), axis=0),
                                grad_bias_proj,
                                grad_gain2,
                                grad_shift2,
                            ]
                        ),
                        grad_router,
                        grad_bias_out,
                    ],
                    axis=0,
                )
            ),
            grad_bias_in,
        ],
        axis=1,
    ).astype(low)
    small_grads = jnp.pad(small_grads, ((0, 0), (0, small_room - small_total)))
    small_grads = dot_f32(sort_dense, small_grads, 0, 0).astype(low)
    dense_grads = jnp.concatenate(
        [
            grad_qkv.astype(low),
            grad_proj.astype(low),
            small_grads.reshape(n_dev * own, LANES),
        ],
        axis=1,
    )
    half = n_dev * own // 2
    theirs = to_core(dense_grads[half:], n_dev)
    total = (dense_grads[:half].astype(f32) + theirs.astype(f32)).astype(low)
    span = planes * own
    pieces = [total[k * span : (k + 1) * span] for k in each]
    pieces = [to_chip(p, k, n_dev) if k else p for k, p in enumerate(pieces)]
    total = sum(p.astype(f32) for p in pieces).astype(low)
    dense_out = scatter_direct([total[s * own : (s + 1) * own] for s in range(planes)], n_dev)
    small = dense_out[:, wide:].reshape(1, small_room)
    small = [p[0] for p in take_columns(small, small_widths)]
    return (
        block_out,
        tokens_grad,
        small[0],
        small[1],
        dense_out[:, : 3 * model_width],
        small[2].reshape(2, own),
        dense_out[:, 3 * model_width : wide],
        small[3],
        small[4],
        small[5],
        small[6].reshape(EXPERTS, own).T,
        expert_in_mine,
        small[8].reshape(EXPERTS, units).T,
        expert_out_mine,
        small[7].reshape(EXPERTS, own),
    )


def solution(mesh):
    row, flat, wide_row = P("fsdp", None), P("fsdp"), P(None, "fsdp")
    unit = P("fsdp", None, None)
    in_specs = (
        row, flat, flat, row, wide_row, row, flat, flat, flat, row,
        unit, row, unit, wide_row, row, row,
    )
    out_specs = (
        row, row, flat, flat, row, wide_row, row, flat, flat, flat, row,
        unit, row, unit, wide_row,
    )
    return jax.shard_map(
        functools.partial(on_device, mesh.shape["fsdp"]),
        mesh=mesh,
        in_specs=in_specs,
        out_specs=out_specs,
        check_vma=False,
    )
```

```python
import functools

import jax
import jax.numpy as jnp
from jax import lax
from jax.experimental import pallas as pl
from jax.experimental.pallas import tpu as pltpu
from jax.sharding import PartitionSpec as P

HEADS = 12
HD = 64
EXPERTS = 4
TOP = 2
LEN = 197
SEQ_DEV = 2
SLOTS = 256
PLANE = 2 * EXPERTS
LANES = 128


def layer_norm(values, gain_vec, shift_vec):
    row_mean = jnp.mean(values, axis=-1, keepdims=True)
    centred = values - row_mean
    spread = jnp.mean(centred * centred, axis=-1, keepdims=True)
    return centred * lax.rsqrt(spread + 1e-06) * gain_vec + shift_vec


def gelu_tanh(values):
    return jax.nn.gelu(values, approximate=True)


def take_columns(block, widths):
    pieces, at = [], 0
    for width in widths:
        pieces.append(block[:, at : at + width])
        at += width
    return pieces


def dot_f32(left, right, left_dim, right_dim):
    return lax.dot_general(
        left,
        right,
        (((left_dim,), (right_dim,)), ((), ())),
        preferred_element_type=jnp.float32,
    )


def to_chip(array, k, n_dev):
    return lax.ppermute(array, "fsdp", [(i, i ^ (2 * k)) for i in range(n_dev)])


def to_core(array, n_dev):
    return lax.ppermute(array, "fsdp", [(i, i ^ 1) for i in range(n_dev)])


def along_line(array, step, n_dev, first, last):
    pairs = [
        (i, i + step * PLANE) for i in range(n_dev) if first <= i // PLANE <= last
    ]
    return lax.ppermute(array, "fsdp", pairs)


def around_line(array, shift, n_dev):
    return lax.ppermute(array, "fsdp", [(i, (i + shift * PLANE) % n_dev) for i in range(n_dev)])


def after(value, *others):
    return lax.optimization_barrier((value,) + others)[0]


def place():
    here = lax.axis_index("fsdp")
    return here % 2, (here // 2) % EXPERTS, here // PLANE


def chip_apart(chip, k):
    x, y = chip % 2, chip // 2
    x = 1 - x if k % 2 else x
    y = 1 - y if k // 2 else y
    return 2 * y + x


def entry_barrier(planes, chips):
    core, chip, plane = place()
    barrier = pltpu.get_barrier_semaphore()
    mesh = pl.DeviceIdType.MESH

    def greet(device):
        pl.semaphore_signal(barrier, inc=1, device_id=(device,), device_id_type=mesh)

    greet(plane * PLANE + chip * 2 + 1 - core)
    for k in chips:
        greet(plane * PLANE + chip_apart(chip, k) * 2 + core)

    greet((plane + 1) % planes * PLANE + chip * 2 + core)
    greet((plane + planes - 1) % planes * PLANE + chip * 2 + core)
    pl.semaphore_wait(barrier, 3 + len(chips))


def remote(src, dst, send, recv, device):
    return pltpu.make_async_remote_copy(
        src_ref=src,
        dst_ref=dst,
        send_sem=send,
        recv_sem=recv,
        device_id=(device,),
        device_id_type=pl.DeviceIdType.MESH,
    )


def gather_kernel(
    planes, dense_in, weight_in, dense, weight,
    line_send, line_recv, hop_send, hop_recv, chip_send, chip_recv,
    part_send, part_recv, core_send, core_recv, local,
):
    core, chip, plane = place()
    last = planes - 1
    other = plane * PLANE + chip * 2 + 1 - core
    above = (plane + 1) * PLANE + chip * 2 + core
    below = (plane - 1) * PLANE + chip * 2 + core

    def peer(k):
        return plane * PLANE + chip_apart(chip, k) * 2 + core

    def line(slot, up):
        to = slot + 1 if up else (slot - 1) % planes
        return remote(
            dense.at[0, 0, slot], dense.at[0, 0, to],
            line_send.at[int(up), slot], line_recv.at[to], above if up else below,
        )

    def arrived(slot):
        return remote(
            dense.at[0, 0, slot], dense.at[0, 0, slot],
            line_send.at[0, slot], line_recv.at[slot], other,
        )

    def hop(up):
        to = 1 if up else last
        return remote(
            weight.at[:, 0], weight.at[:, to],
            hop_send.at[int(up)], hop_recv.at[to], above if up else below,
        )

    def hop_arrived(slot):
        return remote(
            weight.at[:, slot], weight.at[:, slot], hop_send.at[0], hop_recv.at[slot], other
        )

    parts = [
        remote(
            weight_in.at[:, chip_apart(chip, k)], weight.at[:, 0, k],
            part_send.at[k], part_recv.at[k], peer(k),
        )
        for k in range(1, EXPERTS)
    ]
    own_dense = pltpu.make_async_copy(dense_in, dense.at[0, 0, 0], local.at[0])
    own_part = pltpu.make_async_copy(weight_in.at[:, chip], weight.at[:, 0, 0], local.at[1])
    own_dense.start()
    own_part.start()
    entry_barrier(planes, (1, 2, 3))
    own_dense.wait()

    @pl.when(plane < last)
    def _():
        line(0, True).start()

    @pl.when(plane > 0)
    def _():
        line(0, False).start()

    for part in parts:
        part.start()

    def direct(slot, k):
        return remote(
            dense.at[0, 0, slot], dense.at[0, k, slot],
            chip_send.at[k, slot], chip_recv.at[k, slot], peer(k),
        )

    def first(slot):
        return 1 + slot % 2

    def onward(slot):
        k = first(slot)
        return remote(
            dense.at[0, k, slot], dense.at[0, 3, slot],
            chip_send.at[3, slot], chip_recv.at[3, slot], peer(3 - k),
        )

    def swap(slot, k):
        return remote(
            dense.at[0, k, slot], dense.at[1, k, slot],
            core_send.at[k, slot], core_recv.at[k, slot], other,
        )

    for d in range(1, planes):
        @pl.when(plane >= d)
        def _(d=d):
            arrived(d).wait_recv()

            @pl.when(plane < last)
            def _():
                line(d, True).start()

        @pl.when(plane <= last - d)
        def _(d=d):
            arrived(planes - d).wait_recv()

            @pl.when(plane > 0)
            def _():
                line(planes - d, False).start()

        if d == 1:
            for k in (1, 2):
                direct(0, k).start()
            swap(0, 0).start()

    for slot in range(1, planes):
        for k in (1, 2):
            direct(slot, k).start()
        swap(slot, 0).start()
    own_part.wait()
    for part in parts:
        part.wait()

    @pl.when(plane < last)
    def _():
        hop(True).start()

    @pl.when(plane > 0)
    def _():
        hop(False).start()

    for slot in range(planes):
        direct(slot, first(slot)).wait_recv()
        onward(slot).start()
        swap(slot, first(slot)).start()
    for slot in range(planes):
        direct(slot, 3 - first(slot)).wait_recv()
        swap(slot, 3 - first(slot)).start()
    for slot in range(planes):
        onward(slot).wait_recv()
        swap(slot, 3).start()
    for slot in range(planes):
        for k in (1, 2):
            direct(slot, k).wait_send()
        onward(slot).wait_send()
        for k in range(EXPERTS):
            swap(slot, k).wait()

    @pl.when(plane < last)
    def _():
        line(0, True).wait_send()
        hop(True).wait_send()
        hop_arrived(last).wait_recv()

    @pl.when(plane > 0)
    def _():
        line(0, False).wait_send()
        hop(False).wait_send()
        hop_arrived(1).wait_recv()

    for d in range(1, planes):
        @pl.when((plane >= d) & (plane < last))
        def _(d=d):
            line(d, True).wait_send()

        @pl.when((plane <= last - d) & (plane > 0))
        def _(d=d):
            line(planes - d, False).wait_send()


def gather_weights(dense_mine, weight_mine, n_dev):
    planes = n_dev // PLANE
    _, _, units, width = weight_mine.shape
    sem = pltpu.SemaphoreType.DMA
    any_spec = pl.BlockSpec(memory_space=pl.ANY)
    return pl.pallas_call(
        functools.partial(gather_kernel, planes),
        out_shape=(
            jax.ShapeDtypeStruct((2, EXPERTS, planes) + dense_mine.shape, dense_mine.dtype),
            jax.ShapeDtypeStruct((2, planes, EXPERTS, units, width), weight_mine.dtype),
        ),
        in_specs=[any_spec] * 2,
        out_specs=(any_spec,) * 2,
        scratch_shapes=[
            sem((2, planes)), sem((planes,)), sem((2,)), sem((planes,)),
            sem((EXPERTS, planes)), sem((EXPERTS, planes)),
            sem((EXPERTS,)), sem((EXPERTS,)),
            sem((EXPERTS, planes)), sem((EXPERTS, planes)), sem((2,)),
        ],
        compiler_params=pltpu.CompilerParams(collective_id=1, has_side_effects=True),
        cost_estimate=pl.CostEstimate(flops=0, bytes_accessed=100_000_000, transcendentals=0),
    )(dense_mine, weight_mine)


def exchange_kernel(
    planes, weight_in, rows, grads, weight, theirs, got_rows, got_grads,
    hop_send, hop_recv, core_send, core_recv, row_send, row_recv, local,
):
    core, chip, plane = place()
    last = planes - 1
    other = plane * PLANE + chip * 2 + 1 - core
    above = (plane + 1) * PLANE + chip * 2 + core
    below = (plane - 1) * PLANE + chip * 2 + core

    def hop(slot, up):
        to = slot + 1 if up else (slot - 1) % planes
        return remote(
            weight.at[:, slot], weight.at[:, to],
            hop_send.at[slot], hop_recv.at[to], above if up else below,
        )

    def hop_arrived(slot):
        return remote(
            weight.at[:, slot], weight.at[:, slot], hop_send.at[slot], hop_recv.at[slot], other
        )

    def swap(slot):
        return remote(
            weight.at[:, slot], theirs.at[:, slot],
            core_send.at[slot], core_recv.at[slot], other,
        )

    keep = [
        pltpu.make_async_copy(rows.at[0], got_rows.at[0], local.at[0]),
        pltpu.make_async_copy(grads.at[0], got_grads.at[0], local.at[1]),
    ]
    for copy in keep:
        copy.start()
    entry_barrier(planes, (1, 2, 3))

    def onward(d, wait):
        @pl.when(plane >= d)
        def _():
            if wait:
                hop_arrived(d).wait_recv()

            @pl.when(plane < last)
            def _():
                hop(d, True).start()

            swap(d).start()

        @pl.when(plane <= last - d)
        def _():
            if wait:
                hop_arrived(planes - d).wait_recv()

            @pl.when(plane > 0)
            def _():
                hop(planes - d, False).start()

            swap(planes - d).start()

    onward(1, False)
    trades = []
    for n, (src, dst) in enumerate(((rows, got_rows), (grads, got_grads))):
        for k in range(1, EXPERTS):
            trades.append(
                remote(
                    src.at[k], dst.at[k], row_send.at[n, k], row_recv.at[n, k],
                    plane * PLANE + chip_apart(chip, k) * 2 + core,
                )
            )
    for trade in trades:
        trade.start()
    swap(0).start()
    for d in range(2, planes):
        onward(d, True)
    for trade in trades:
        trade.wait()
    for copy in keep:
        copy.wait()
    for slot in range(planes):
        swap(slot).wait()
    for d in range(1, planes):
        @pl.when((plane >= d) & (plane < last))
        def _(d=d):
            hop(d, True).wait_send()

        @pl.when((plane <= last - d) & (plane > 0))
        def _(d=d):
            hop(planes - d, False).wait_send()


def exchange_rows(weight, rows, grads, n_dev):
    planes = n_dev // PLANE
    sem = pltpu.SemaphoreType.DMA
    any_spec = pl.BlockSpec(memory_space=pl.ANY)

    def like(array):
        return jax.ShapeDtypeStruct(array.shape, array.dtype)

    return pl.pallas_call(
        functools.partial(exchange_kernel, planes),
        out_shape=(like(weight), like(weight), like(rows), like(grads)),
        in_specs=[any_spec] * 3,
        out_specs=(any_spec,) * 4,
        input_output_aliases={0: 0},
        scratch_shapes=[
            sem((planes,)), sem((planes,)), sem((planes,)), sem((planes,)),
            sem((2, EXPERTS)), sem((2, EXPERTS)), sem((2,)),
        ],
        compiler_params=pltpu.CompilerParams(collective_id=2, has_side_effects=True),
        cost_estimate=pl.CostEstimate(flops=0, bytes_accessed=150_000_000, transcendentals=0),
    )(weight, rows, grads)


def scatter_direct(slots, n_dev):
    total = slots[0].astype(jnp.float32)
    for s in range(1, n_dev // PLANE):
        total = total + around_line(slots[s], -s, n_dev).astype(jnp.float32)
    return total


def sum_low(mine, got):
    return (mine.astype(jnp.float32) + got.astype(jnp.float32)).astype(jnp.bfloat16)


def scatter_start(slots, n_dev):
    if n_dev // PLANE != 4:
        return ()
    return along_line(slots[1], 1, n_dev, 0, 0), along_line(slots[3], -1, n_dev, 3, 3)


def scatter_middle(slots, hops, n_dev):
    if n_dev // PLANE != 4:
        return ()
    up = along_line(sum_low(slots[2], hops[0]), 1, n_dev, 0, 1)
    down = along_line(sum_low(slots[2], hops[1]), -1, n_dev, 2, 3)
    return up, down


def scatter_end(slots, hops, n_dev):
    if n_dev // PLANE != 4:
        return scatter_direct(slots, n_dev)
    up = along_line(sum_low(slots[3], hops[0]), 1, n_dev, 0, 2)
    down = along_line(sum_low(slots[1], hops[1]), -1, n_dev, 1, 3)
    return slots[0].astype(jnp.float32) + up.astype(jnp.float32) + down.astype(jnp.float32)


def on_device(
    n_dev,
    tokens,
    ln1_gain,
    ln1_shift,
    qkv_weight,
    qv_bias,
    proj_weight,
    proj_bias,
    ln2_gain,
    ln2_shift,
    router_weight,
    expert_in,
    expert_in_bias,
    expert_out,
    expert_out_bias,
    routes,
    out_grad,
):
    highest = lax.Precision.HIGHEST
    f32 = jnp.float32
    low = jnp.bfloat16
    row_count, model_width = tokens.shape
    shape_four = (SEQ_DEV, LEN, HEADS, HD)
    query_scale = HD ** (-0.5)
    own = qkv_weight.shape[0]
    units = expert_in.shape[0]
    planes = n_dev // PLANE
    each = range(EXPERTS)
    wide = 4 * model_width
    here = lax.axis_index("fsdp")
    core = here % 2
    chip = (here // 2) % EXPERTS
    plane = here // PLANE

    def owner_dense(j):
        s, k, c = j % planes, (j // planes) % EXPERTS, j // (planes * EXPERTS)
        return ((plane - s + planes) % planes) * PLANE + (chip ^ k) * 2 + (core ^ c)

    def owner_units(j):
        k, s, c = j % EXPERTS, (j // EXPERTS) % planes, j // (planes * EXPERTS)
        return ((plane - s + planes) % planes) * PLANE + (chip ^ k) * 2 + (core ^ c)

    devices = jnp.arange(n_dev, dtype=jnp.int32)
    sort_dense = (devices[:, None] == owner_dense(devices)[None, :]).astype(low)
    sort_units = (devices[:, None] == owner_units(devices)[None, :]).astype(low)
    features = jnp.arange(model_width, dtype=jnp.int32)
    home = owner_dense(features // own) * own + features % own
    sort_rows = (features[:, None] == home[None, :]).astype(low)

    small_parts = [
        ln1_gain,
        ln1_shift,
        qv_bias.reshape(-1),
        proj_bias,
        ln2_gain,
        ln2_shift,
        router_weight.T.reshape(-1),
        expert_out_bias.reshape(-1),
        expert_in_bias.T.reshape(-1),
    ]
    small_widths = [p.shape[0] for p in small_parts]
    small_total = sum(small_widths)
    small_room = own * LANES
    small_mine = jnp.pad(jnp.concatenate(small_parts), (0, small_room - small_total))
    dense_mine = jnp.concatenate(
        [qkv_weight, proj_weight, small_mine.reshape(own, LANES)], axis=1
    )
    weight_mine = jnp.stack([expert_in.transpose(1, 0, 2), expert_out.transpose(1, 0, 2)])
    dense, own_half = gather_weights(dense_mine, weight_mine, n_dev)
    dense = dense.reshape(model_width, wide + LANES)

    w_qkv = dense[:, : 3 * model_width]
    w_proj = dense[:, 3 * model_width : wide]
    small = dense[:, wide:].reshape(n_dev, small_room)
    small = dot_f32(sort_dense, small, 1, 0).astype(low)
    gain1, shift1, bias_qv, bias_proj, gain2, shift2, w_router, bias_out, bias_in = take_columns(
        small, small_widths
    )
    gain1 = gain1.reshape(-1).astype(f32)
    shift1 = shift1.reshape(-1).astype(f32)
    gain2 = gain2.reshape(-1).astype(f32)
    shift2 = shift2.reshape(-1).astype(f32)
    bias_proj = bias_proj.reshape(-1).astype(f32)
    bias_q = bias_qv[:, :own].reshape(-1).astype(f32)
    bias_v = bias_qv[:, own:].reshape(-1).astype(f32)
    w_router = jnp.stack([p.reshape(-1) for p in take_columns(w_router, [own] * EXPERTS)])
    bias_out = jnp.stack([p.reshape(-1) for p in take_columns(bias_out, [own] * EXPERTS)])
    mine = (jnp.arange(EXPERTS, dtype=jnp.int32) == chip).astype(f32)
    bias_out = jnp.sum(bias_out.astype(f32) * mine[:, None], axis=0)
    bias_in = jnp.stack(take_columns(bias_in, [units] * EXPERTS)).astype(f32)
    bias_in = jnp.sum(bias_in * mine[:, None, None], axis=0).astype(low)
    bias_in = dot_f32(sort_units, bias_in, 0, 0).reshape(2, n_dev * units // 2)

    experts = jnp.arange(EXPERTS, dtype=jnp.int32)[None, :]
    pick = [(routes[:, j : j + 1] == experts).astype(f32) for j in range(TOP)]
    picked = pick[0] + pick[1]
    tri = jnp.arange(row_count)[:, None] > jnp.arange(row_count)[None, :]
    before = dot_f32(tri.astype(low), picked.astype(low), 1, 0)
    slot_ids = jnp.arange(EXPERTS * SLOTS, dtype=jnp.int32)[None, :]
    hit = []
    for j in range(TOP):
        slot = jnp.sum(pick[j] * before, axis=1, keepdims=True).astype(jnp.int32)
        hit.append(slot_ids == (routes[:, j : j + 1] ^ chip) * SLOTS + slot)
    dispatch = (hit[0] | hit[1]).astype(low)

    inputs = tokens.astype(f32)
    normed_full, norm1_pull = jax.vjp(layer_norm, inputs, gain1, shift1)
    normed = dot_f32(normed_full.astype(low), sort_rows, 1, 0).astype(low)
    projected = jnp.dot(normed, w_qkv, preferred_element_type=f32)
    queries = ((projected[:, :model_width] + bias_q) * query_scale).astype(low).reshape(shape_four)
    key_rows = projected[:, model_width : 2 * model_width].astype(low).reshape(shape_four)
    values = (projected[:, 2 * model_width :] + bias_v).astype(low).reshape(shape_four)
    scores = jnp.einsum("sqhd,skhd->shqk", queries, key_rows, preferred_element_type=f32)
    exp_scores = jnp.exp(scores - jnp.max(scores, axis=-1, keepdims=True))
    probs_full = exp_scores / jnp.sum(exp_scores, axis=-1, keepdims=True)
    probs_low = probs_full.astype(low)
    attended = jnp.einsum("shqk,skhd->sqhd", probs_low, values, preferred_element_type=f32)
    attended = attended.reshape(row_count, model_width).astype(low)
    attended = dot_f32(attended, sort_rows, 1, 0).astype(low)

    middle = inputs + jnp.dot(attended, w_proj, preferred_element_type=f32) + bias_proj
    normed2_full, norm2_pull = jax.vjp(layer_norm, middle, gain2, shift2)
    normed2 = normed2_full.astype(low)
    gate_probs = jax.nn.softmax(dot_f32(normed2, w_router, 1, 1), axis=-1)
    chosen = [jnp.sum(gate_probs * pick[j], axis=1, keepdims=True) for j in range(TOP)]
    combine = (jnp.where(hit[0], chosen[0], 0.0) + jnp.where(hit[1], chosen[1], 0.0)).astype(low)

    def exchange(rows):
        pieces = [rows[k * SLOTS : (k + 1) * SLOTS] for k in each]
        pieces = [to_chip(p, k, n_dev) if k else p for k, p in enumerate(pieces)]
        return jnp.concatenate(pieces, axis=0)

    four = (EXPERTS, SLOTS, model_width)
    own_half, other_half, slot_rows, grad_result = exchange_rows(
        own_half,
        dot_f32(dispatch, normed2, 0, 0).astype(low).reshape(four),
        dot_f32(combine, out_grad, 0, 0).astype(low).reshape(four),
        n_dev,
    )
    slot_rows = slot_rows.reshape(EXPERTS * SLOTS, model_width)
    grad_result = grad_result.reshape(EXPERTS * SLOTS, model_width)
    halves = [h.reshape(2, n_dev * units // 2, model_width) for h in (own_half, other_half)]
    w_in = [half[0] for half in halves]
    w_out = [half[1] for half in halves]

    hidden, grad_pre, pulls = [], [], []
    for c in range(2):
        pre_act = dot_f32(slot_rows, w_in[c], 1, 1) + bias_in[c]
        out, pull = jax.vjp(gelu_tanh, pre_act)
        hidden.append(out.astype(low))
        pulls.append(pull)
    result = dot_f32(hidden[0], w_out[0], 1, 0) + dot_f32(hidden[1], w_out[1], 1, 0)
    result = exchange((result + bias_out).astype(low))
    for c in range(2):
        grad_pre.append(pulls[c](dot_f32(grad_result, w_out[c], 1, 1))[0].astype(low))
    grad_slots = dot_f32(grad_pre[0], w_in[0], 1, 0) + dot_f32(grad_pre[1], w_in[1], 1, 0)
    grad_slots = exchange(grad_slots.astype(low))

    theirs = jnp.stack(
        [
            dot_f32(grad_pre[1], slot_rows, 0, 0).astype(low),
            dot_f32(hidden[1], grad_result, 0, 0).astype(low),
        ]
    )
    theirs = to_core(theirs, n_dev)
    terms = jnp.stack(
        [dot_f32(grad_pre[0], slot_rows, 0, 0), dot_f32(hidden[0], grad_result, 0, 0)]
    )
    terms = (terms + theirs.astype(f32)).astype(low)
    grad_slots = after(grad_slots, terms)
    result = after(result, terms)
    span = EXPERTS * units
    terms = [terms[:, s * span : (s + 1) * span] for s in range(planes)]
    hops = scatter_start(terms, n_dev)

    grad_bias_in = jnp.concatenate([jnp.sum(g.astype(f32), axis=0) for g in grad_pre])
    grad_bias_in = jnp.dot(
        sort_units.astype(f32), grad_bias_in.reshape(n_dev, units), precision=highest
    )
    grad_bias_in = (mine[None, :, None] * grad_bias_in[:, None, :]).reshape(n_dev, EXPERTS * units)
    grad_bias_out = mine[:, None] * jnp.sum(grad_result.astype(f32), axis=0)[None, :]

    block_out = (middle + jnp.dot(combine, result, preferred_element_type=f32)).astype(low)

    grad_top = out_grad.astype(f32)
    slot_dots = dot_f32(out_grad, result, 1, 1)
    grad_gates = sum(
        pick[j] * jnp.sum(jnp.where(hit[j], slot_dots, 0.0), axis=1, keepdims=True)
        for j in range(TOP)
    )
    grad_logits = gate_probs * (
        grad_gates - jnp.sum(gate_probs * grad_gates, axis=-1, keepdims=True)
    )
    grad_router = jnp.dot(grad_logits.T, normed2.astype(f32), precision=highest)
    grad_normed2 = jnp.dot(grad_logits, w_router.astype(f32), precision=highest)
    grad_normed2 = grad_normed2 + jnp.dot(dispatch, grad_slots, preferred_element_type=f32)
    grad_mid_norm, grad_gain2, grad_shift2 = norm2_pull(grad_normed2)
    grad_middle = grad_top + grad_mid_norm

    grad_branch = grad_middle.astype(low)
    grad_bias_proj = jnp.sum(grad_branch.astype(f32), axis=0)
    grad_proj = dot_f32(attended, grad_branch, 0, 0)
    grad_attended = dot_f32(grad_branch, w_proj, 1, 1).astype(low)
    grad_attended = dot_f32(grad_attended, sort_rows, 1, 1).astype(low).reshape(shape_four)
    grad_probs = jnp.einsum("sqhd,skhd->shqk", grad_attended, values, preferred_element_type=f32)
    grad_values = jnp.einsum(
        "shqk,sqhd->skhd", probs_low, grad_attended, preferred_element_type=f32
    ).astype(low)
    grad_probs = after(grad_probs, *hops)
    hops = scatter_middle(terms, hops, n_dev)
    grad_scores = (
        probs_full * (grad_probs - jnp.sum(probs_full * grad_probs, axis=-1, keepdims=True))
    ).astype(low)
    grad_queries = jnp.einsum(
        "shqk,skhd->sqhd", grad_scores, key_rows, preferred_element_type=f32
    ).astype(low)
    grad_keys = jnp.einsum(
        "shqk,sqhd->skhd", grad_scores, queries, preferred_element_type=f32
    ).astype(low)
    grad_query_pre = grad_queries.astype(f32).reshape(row_count, model_width) * query_scale
    grad_values = grad_values.reshape(row_count, model_width)
    grad_projected = jnp.concatenate(
        [grad_query_pre.astype(low), grad_keys.reshape(row_count, model_width), grad_values],
        axis=1,
    )
    grad_projected = after(grad_projected, *hops)
    expert_mine = scatter_end(terms, hops, n_dev).astype(low)
    grad_qkv = dot_f32(normed, grad_projected, 0, 0)
    grad_normed = dot_f32(grad_projected, w_qkv, 1, 1)
    upper = grad_normed.astype(low)
    lower = (grad_normed - upper.astype(f32)).astype(low)
    grad_normed = dot_f32(upper, sort_rows, 1, 1) + dot_f32(lower, sort_rows, 1, 1)
    grad_in_norm, grad_gain1, grad_shift1 = norm1_pull(grad_normed)
    tokens_grad = grad_middle + grad_in_norm

    def by_owner(rows):
        return rows.reshape(-1, n_dev, rows.shape[-1] // n_dev).transpose(1, 0, 2).reshape(n_dev, -1)

    small_grads = jnp.concatenate(
        [
            by_owner(
                jnp.concatenate(
                    [
                        jnp.stack(
                            [
                                grad_gain1,
                                grad_shift1,
                                jnp.sum(grad_query_pre, axis=0),
                                jnp.sum(grad_values.astype(f32), axis=0),
                                grad_bias_proj,
                                grad_gain2,
                                grad_shift2,
                            ]
                        ),
                        grad_router,
                        grad_bias_out,
                    ],
                    axis=0,
                )
            ),
            grad_bias_in,
        ],
        axis=1,
    ).astype(low)
    small_grads = jnp.pad(small_grads, ((0, 0), (0, small_room - small_total)))
    small_grads = dot_f32(sort_dense, small_grads, 0, 0).astype(low)
    dense_grads = jnp.concatenate(
        [
            grad_qkv.astype(low),
            grad_proj.astype(low),
            small_grads.reshape(n_dev * own, LANES),
        ],
        axis=1,
    )
    half = n_dev * own // 2
    theirs = to_core(dense_grads[half:], n_dev)
    total = (dense_grads[:half].astype(f32) + theirs.astype(f32)).astype(low)
    span = planes * own
    pieces = [total[k * span : (k + 1) * span] for k in each]
    pieces = [to_chip(p, k, n_dev) if k else p for k, p in enumerate(pieces)]
    total = sum(p.astype(f32) for p in pieces).astype(low)
    dense_out = scatter_direct([total[s * own : (s + 1) * own] for s in range(planes)], n_dev)
    pieces = [expert_mine[:, k * units : (k + 1) * units] for k in each]
    pieces = [to_chip(p, k, n_dev) if k else p for k, p in enumerate(pieces)]
    low_bit, high_bit = (chip & 1) == 1, (chip & 2) == 2
    pieces = [jnp.where(low_bit, pieces[k ^ 1], pieces[k]) for k in each]
    pieces = [jnp.where(high_bit, pieces[k ^ 2], pieces[k]) for k in each]
    expert_in_mine, expert_out_mine = [
        jnp.stack([p[w] for p in pieces], axis=1).astype(f32) for w in range(2)
    ]
    small = dense_out[:, wide:].reshape(1, small_room)
    small = [p[0] for p in take_columns(small, small_widths)]
    return (
        block_out,
        tokens_grad,
        small[0],
        small[1],
        dense_out[:, : 3 * model_width],
        small[2].reshape(2, own),
        dense_out[:, 3 * model_width : wide],
        small[3],
        small[4],
        small[5],
        small[6].reshape(EXPERTS, own).T,
        expert_in_mine,
        small[8].reshape(EXPERTS, units).T,
        expert_out_mine,
        small[7].reshape(EXPERTS, own),
    )


def solution(mesh):
    row, flat, wide_row = P("fsdp", None), P("fsdp"), P(None, "fsdp")
    unit = P("fsdp", None, None)
    in_specs = (
        row, flat, flat, row, wide_row, row, flat, flat, flat, row,
        unit, row, unit, wide_row, row, row,
    )
    out_specs = (
        row, row, flat, flat, row, wide_row, row, flat, flat, flat, row,
        unit, row, unit, wide_row,
    )
    return jax.shard_map(
        functools.partial(on_device, mesh.shape["fsdp"]),
        mesh=mesh,
        in_specs=in_specs,
        out_specs=out_specs,
        check_vma=False,
    )
```

```python
import functools

import jax
import jax.numpy as jnp
from jax import lax
from jax.experimental import pallas as pl
from jax.experimental.pallas import tpu as pltpu
from jax.sharding import PartitionSpec as P

HD = 64
EXPERTS = 4
TOP = 2
LEN = 197
SEQ_DEV = 2
SLOTS = 256
PLANE = 2 * EXPERTS
LANES = 128


def gelu_tanh(values):
    return jax.nn.gelu(values, approximate=True)


def take_columns(block, widths):
    pieces, at = [], 0
    for width in widths:
        pieces.append(block[:, at : at + width])
        at += width
    return pieces


def dot_f32(left, right, left_dim, right_dim):
    return lax.dot_general(
        left,
        right,
        (((left_dim,), (right_dim,)), ((), ())),
        preferred_element_type=jnp.float32,
    )


def to_chip(array, k, n_dev):
    return lax.ppermute(array, "fsdp", [(i, i ^ (2 * k)) for i in range(n_dev)])


def to_core(array, n_dev):
    return lax.ppermute(array, "fsdp", [(i, i ^ 1) for i in range(n_dev)])


def along_line(array, step, n_dev, first, last):
    pairs = [
        (i, i + step * PLANE) for i in range(n_dev) if first <= i // PLANE <= last
    ]
    return lax.ppermute(array, "fsdp", pairs)


def around_line(array, shift, n_dev):
    return lax.ppermute(array, "fsdp", [(i, (i + shift * PLANE) % n_dev) for i in range(n_dev)])


def after(value, *others):
    return lax.optimization_barrier((value,) + others)[0]


def place():
    here = lax.axis_index("fsdp")
    return here % 2, (here // 2) % EXPERTS, here // PLANE


def chip_apart(chip, k):
    x, y = chip % 2, chip // 2
    x = 1 - x if k % 2 else x
    y = 1 - y if k // 2 else y
    return 2 * y + x


def entry_barrier(planes, chips):
    core, chip, plane = place()
    barrier = pltpu.get_barrier_semaphore()
    mesh = pl.DeviceIdType.MESH

    def greet(device):
        pl.semaphore_signal(barrier, inc=1, device_id=(device,), device_id_type=mesh)

    greet(plane * PLANE + chip * 2 + 1 - core)
    for k in chips:
        greet(plane * PLANE + chip_apart(chip, k) * 2 + core)

    greet((plane + 1) % planes * PLANE + chip * 2 + core)
    greet((plane + planes - 1) % planes * PLANE + chip * 2 + core)
    pl.semaphore_wait(barrier, 3 + len(chips))


def remote(src, dst, send, recv, device):
    return pltpu.make_async_remote_copy(
        src_ref=src,
        dst_ref=dst,
        send_sem=send,
        recv_sem=recv,
        device_id=(device,),
        device_id_type=pl.DeviceIdType.MESH,
    )


def gather_kernel(
    planes, dense_in, weight_in, dense, weight,
    line_send, line_recv, hop_send, hop_recv, chip_send, chip_recv,
    part_send, part_recv, core_send, core_recv, local,
):
    core, chip, plane = place()
    last = planes - 1
    other = plane * PLANE + chip * 2 + 1 - core
    above = (plane + 1) * PLANE + chip * 2 + core
    below = (plane - 1) * PLANE + chip * 2 + core

    def peer(k):
        return plane * PLANE + chip_apart(chip, k) * 2 + core

    def line(slot, up):
        to = slot + 1 if up else (slot - 1) % planes
        return remote(
            dense.at[0, 0, slot], dense.at[0, 0, to],
            line_send.at[int(up), slot], line_recv.at[to], above if up else below,
        )

    def arrived(slot):
        return remote(
            dense.at[0, 0, slot], dense.at[0, 0, slot],
            line_send.at[0, slot], line_recv.at[slot], other,
        )

    def hop(up):
        to = 1 if up else last
        return remote(
            weight.at[:, 0], weight.at[:, to],
            hop_send.at[int(up)], hop_recv.at[to], above if up else below,
        )

    def hop_arrived(slot):
        return remote(
            weight.at[:, slot], weight.at[:, slot], hop_send.at[0], hop_recv.at[slot], other
        )

    parts = [
        remote(
            weight_in.at[:, chip_apart(chip, k)], weight.at[:, 0, k],
            part_send.at[k], part_recv.at[k], peer(k),
        )
        for k in range(1, EXPERTS)
    ]
    own_dense = pltpu.make_async_copy(dense_in, dense.at[0, 0, 0], local.at[0])
    own_part = pltpu.make_async_copy(weight_in.at[:, chip], weight.at[:, 0, 0], local.at[1])
    own_dense.start()
    own_part.start()
    entry_barrier(planes, (1, 2, 3))
    own_dense.wait()

    @pl.when(plane < last)
    def _():
        line(0, True).start()

    @pl.when(plane > 0)
    def _():
        line(0, False).start()

    for part in parts:
        part.start()

    def direct(slot, k):
        return remote(
            dense.at[0, 0, slot], dense.at[0, k, slot],
            chip_send.at[k, slot], chip_recv.at[k, slot], peer(k),
        )

    def first(slot):
        return 1 + slot % 2

    def onward(slot):
        k = first(slot)
        return remote(
            dense.at[0, k, slot], dense.at[0, 3, slot],
            chip_send.at[3, slot], chip_recv.at[3, slot], peer(3 - k),
        )

    def swap(slot, k):
        return remote(
            dense.at[0, k, slot], dense.at[1, k, slot],
            core_send.at[k, slot], core_recv.at[k, slot], other,
        )

    for d in range(1, planes):
        @pl.when(plane >= d)
        def _(d=d):
            arrived(d).wait_recv()

            @pl.when(plane < last)
            def _():
                line(d, True).start()

        @pl.when(plane <= last - d)
        def _(d=d):
            arrived(planes - d).wait_recv()

            @pl.when(plane > 0)
            def _():
                line(planes - d, False).start()

        if d == 1:
            for k in (1, 2):
                direct(0, k).start()
            swap(0, 0).start()

    for slot in range(1, planes):
        for k in (1, 2):
            direct(slot, k).start()
        swap(slot, 0).start()
    own_part.wait()
    for part in parts:
        part.wait()

    @pl.when(plane < last)
    def _():
        hop(True).start()

    @pl.when(plane > 0)
    def _():
        hop(False).start()

    for slot in range(planes):
        direct(slot, first(slot)).wait_recv()
        onward(slot).start()
        swap(slot, first(slot)).start()
    for slot in range(planes):
        direct(slot, 3 - first(slot)).wait_recv()
        swap(slot, 3 - first(slot)).start()
    for slot in range(planes):
        onward(slot).wait_recv()
        swap(slot, 3).start()
    for slot in range(planes):
        for k in (1, 2):
            direct(slot, k).wait_send()
        onward(slot).wait_send()
        for k in range(EXPERTS):
            swap(slot, k).wait()

    @pl.when(plane < last)
    def _():
        line(0, True).wait_send()
        hop(True).wait_send()
        hop_arrived(last).wait_recv()

    @pl.when(plane > 0)
    def _():
        line(0, False).wait_send()
        hop(False).wait_send()
        hop_arrived(1).wait_recv()

    for d in range(1, planes):
        @pl.when((plane >= d) & (plane < last))
        def _(d=d):
            line(d, True).wait_send()

        @pl.when((plane <= last - d) & (plane > 0))
        def _(d=d):
            line(planes - d, False).wait_send()


def gather_weights(dense_mine, weight_mine, n_dev):
    planes = n_dev // PLANE
    _, _, units, width = weight_mine.shape
    sem = pltpu.SemaphoreType.DMA
    any_spec = pl.BlockSpec(memory_space=pl.ANY)
    return pl.pallas_call(
        functools.partial(gather_kernel, planes),
        out_shape=(
            jax.ShapeDtypeStruct((2, EXPERTS, planes) + dense_mine.shape, dense_mine.dtype),
            jax.ShapeDtypeStruct((2, planes, EXPERTS, units, width), weight_mine.dtype),
        ),
        in_specs=[any_spec] * 2,
        out_specs=(any_spec,) * 2,
        scratch_shapes=[
            sem((2, planes)), sem((planes,)), sem((2,)), sem((planes,)),
            sem((EXPERTS, planes)), sem((EXPERTS, planes)),
            sem((EXPERTS,)), sem((EXPERTS,)),
            sem((EXPERTS, planes)), sem((EXPERTS, planes)), sem((2,)),
        ],
        compiler_params=pltpu.CompilerParams(collective_id=1, has_side_effects=True),
        cost_estimate=pl.CostEstimate(flops=0, bytes_accessed=100_000_000, transcendentals=0),
    )(dense_mine, weight_mine)


def exchange_kernel(
    planes, weight_in, rows, grads, weight, theirs, got_rows, got_grads,
    hop_send, hop_recv, core_send, core_recv, row_send, row_recv, local,
):
    core, chip, plane = place()
    last = planes - 1
    other = plane * PLANE + chip * 2 + 1 - core
    above = (plane + 1) * PLANE + chip * 2 + core
    below = (plane - 1) * PLANE + chip * 2 + core

    def hop(slot, up):
        to = slot + 1 if up else (slot - 1) % planes
        return remote(
            weight.at[:, slot], weight.at[:, to],
            hop_send.at[slot], hop_recv.at[to], above if up else below,
        )

    def hop_arrived(slot):
        return remote(
            weight.at[:, slot], weight.at[:, slot], hop_send.at[slot], hop_recv.at[slot], other
        )

    def swap(slot):
        return remote(
            weight.at[:, slot], theirs.at[:, slot],
            core_send.at[slot], core_recv.at[slot], other,
        )

    keep = [
        pltpu.make_async_copy(rows.at[0], got_rows.at[0], local.at[0]),
        pltpu.make_async_copy(grads.at[0], got_grads.at[0], local.at[1]),
    ]
    for copy in keep:
        copy.start()
    entry_barrier(planes, (1, 2, 3))

    def onward(d, wait):
        @pl.when(plane >= d)
        def _():
            if wait:
                hop_arrived(d).wait_recv()

            @pl.when(plane < last)
            def _():
                hop(d, True).start()

            swap(d).start()

        @pl.when(plane <= last - d)
        def _():
            if wait:
                hop_arrived(planes - d).wait_recv()

            @pl.when(plane > 0)
            def _():
                hop(planes - d, False).start()

            swap(planes - d).start()

    onward(1, False)
    trades = []
    for n, (src, dst) in enumerate(((rows, got_rows), (grads, got_grads))):
        for k in range(1, EXPERTS):
            trades.append(
                remote(
                    src.at[k], dst.at[k], row_send.at[n, k], row_recv.at[n, k],
                    plane * PLANE + chip_apart(chip, k) * 2 + core,
                )
            )
    for trade in trades:
        trade.start()
    swap(0).start()
    for d in range(2, planes):
        onward(d, True)
    for trade in trades:
        trade.wait()
    for copy in keep:
        copy.wait()
    for slot in range(planes):
        swap(slot).wait()
    for d in range(1, planes):
        @pl.when((plane >= d) & (plane < last))
        def _(d=d):
            hop(d, True).wait_send()

        @pl.when((plane <= last - d) & (plane > 0))
        def _(d=d):
            hop(planes - d, False).wait_send()


def exchange_rows(weight, rows, grads, n_dev):
    planes = n_dev // PLANE
    sem = pltpu.SemaphoreType.DMA
    any_spec = pl.BlockSpec(memory_space=pl.ANY)

    def like(array):
        return jax.ShapeDtypeStruct(array.shape, array.dtype)

    return pl.pallas_call(
        functools.partial(exchange_kernel, planes),
        out_shape=(like(weight), like(weight), like(rows), like(grads)),
        in_specs=[any_spec] * 3,
        out_specs=(any_spec,) * 4,
        input_output_aliases={0: 0},
        scratch_shapes=[
            sem((planes,)), sem((planes,)), sem((planes,)), sem((planes,)),
            sem((2, EXPERTS)), sem((2, EXPERTS)), sem((2,)),
        ],
        compiler_params=pltpu.CompilerParams(collective_id=2, has_side_effects=True),
        cost_estimate=pl.CostEstimate(flops=0, bytes_accessed=150_000_000, transcendentals=0),
    )(weight, rows, grads)


def scatter_direct(slots, n_dev):
    total = slots[0].astype(jnp.float32)
    for s in range(1, n_dev // PLANE):
        total = total + around_line(slots[s], -s, n_dev).astype(jnp.float32)
    return total


def sum_low(mine, got):
    return (mine.astype(jnp.float32) + got.astype(jnp.float32)).astype(jnp.bfloat16)


def scatter_start(slots, n_dev):
    if n_dev // PLANE != 4:
        return ()
    return along_line(slots[1], 1, n_dev, 0, 0), along_line(slots[3], -1, n_dev, 3, 3)


def scatter_middle(slots, hops, n_dev):
    if n_dev // PLANE != 4:
        return ()
    up = along_line(sum_low(slots[2], hops[0]), 1, n_dev, 0, 1)
    down = along_line(sum_low(slots[2], hops[1]), -1, n_dev, 2, 3)
    return up, down


def scatter_end(slots, hops, n_dev):
    if n_dev // PLANE != 4:
        return scatter_direct(slots, n_dev)
    up = along_line(sum_low(slots[3], hops[0]), 1, n_dev, 0, 2)
    down = along_line(sum_low(slots[1], hops[1]), -1, n_dev, 1, 3)
    return slots[0].astype(jnp.float32) + up.astype(jnp.float32) + down.astype(jnp.float32)


def row_norm(values):
    centred = values - jnp.mean(values, axis=-1, keepdims=True)
    spread = jnp.mean(centred * centred, axis=-1, keepdims=True)
    return centred, lax.rsqrt(spread + 1e-06)


def norm_back(centred, scale, gain_vec, grad):
    inner = grad * gain_vec
    unit = centred * scale
    shared = jnp.mean(inner, axis=-1, keepdims=True)
    slope = jnp.mean(inner * unit, axis=-1, keepdims=True)
    return scale * (inner - shared - unit * slope), unit * grad


def head_lanes(h):
    lane = lax.broadcasted_iota(jnp.int32, (1, 2 * HD), 1)
    return (lane // HD == h).astype(jnp.float32)


def head_probs(queries, key_rows):
    scores = dot_f32(queries, key_rows, 1, 1)
    key = lax.broadcasted_iota(jnp.int32, scores.shape, 1)
    scores = jnp.where(key < LEN, scores, -1e30)
    scores = jnp.exp(scores - jnp.max(scores, axis=-1, keepdims=True))
    return scores * (1.0 / jnp.sum(scores, axis=-1, keepdims=True))


def forward_kernel(
    tokens, dense, vecs, sort, router, middle, normed2, logits, qkv, normed, attended, heads
):
    f32, low = jnp.float32, jnp.bfloat16
    width = tokens.shape[1]
    rows = tokens.shape[0] // SEQ_DEV
    inputs = tokens[...].astype(f32)
    centred, scale = row_norm(inputs)
    plain = (centred * scale * vecs[0:1] + vecs[1:2]).astype(low)
    normed[...] = dot_f32(plain, sort[...], 1, 0).astype(low)
    queries = dot_f32(normed[...], dense[:, :width], 1, 0)
    qkv[:, :width] = ((queries + vecs[2:3]) * HD ** (-0.5)).astype(low)
    key_rows = dot_f32(normed[...], dense[:, width : 2 * width], 1, 0)
    qkv[:, width : 2 * width] = key_rows.astype(low)
    values = dot_f32(normed[...], dense[:, 2 * width : 3 * width], 1, 0)
    qkv[:, 2 * width : 3 * width] = (values + vecs[3:4]).astype(low)

    @pl.loop(0, width // (2 * HD))
    def _(pair):
        q_at, k_at, v_at = [
            pl.ds(pl.multiple_of(pair * 2 * HD + n * width, 2 * HD), 2 * HD) for n in range(3)
        ]
        for seq in range(SEQ_DEV):
            at = pl.ds(seq * rows, rows)
            total = 0.0
            for h in range(2):
                lanes = head_lanes(h)
                probs = head_probs(qkv[at, q_at] * lanes.astype(low), qkv[at, k_at])
                total = total + dot_f32(probs.astype(low), qkv[at, v_at], 1, 0) * lanes
            heads[at, q_at] = total.astype(low)

    attended[...] = dot_f32(heads[...], sort[...], 1, 0).astype(low)
    branch = dot_f32(attended[...], dense[:, 3 * width : 4 * width], 1, 0)
    middle[...] = inputs + branch + vecs[4:5]
    centred, scale = row_norm(middle[...])
    normed2[...] = (centred * scale * vecs[5:6] + vecs[6:7]).astype(low)
    logits[...] = dot_f32(normed2[...], router[...], 1, 1)


def backward_kernel(
    tokens, dense, vecs, sort, middle, qkv, normed, attended, out_grad, grad_normed2,
    dense_grad, tokens_grad, sums, grad_mid, heads, grads,
):
    f32, low = jnp.float32, jnp.bfloat16
    width = tokens.shape[1]
    rows = tokens.shape[0] // SEQ_DEV

    def total(rows_of):
        return jnp.sum(rows_of, axis=0, keepdims=True)

    centred, scale = row_norm(middle[...])
    grad = grad_normed2[...]
    back, gain_terms = norm_back(centred, scale, vecs[5:6], grad)
    sums[5:6] = total(gain_terms)
    sums[6:7] = total(grad)
    sums[7:8] = jnp.zeros((1, width), f32)
    grad_mid[...] = out_grad[...].astype(f32) + back
    branch = grad_mid[...].astype(low)
    sums[4:5] = total(branch.astype(f32))
    dense_grad[:, 3 * width : 4 * width] = dot_f32(attended[...], branch, 0, 0).astype(low)
    grad_att = dot_f32(branch, dense[:, 3 * width : 4 * width], 1, 1).astype(low)
    heads[...] = dot_f32(grad_att, sort[...], 1, 1).astype(low)

    @pl.loop(0, width // (2 * HD))
    def _(pair):
        q_at, k_at, v_at = [
            pl.ds(pl.multiple_of(pair * 2 * HD + n * width, 2 * HD), 2 * HD) for n in range(3)
        ]
        for seq in range(SEQ_DEV):
            at = pl.ds(seq * rows, rows)
            queries, key_rows, values = qkv[at, q_at], qkv[at, k_at], qkv[at, v_at]
            grad_out = heads[at, q_at]
            grad_q, grad_k, grad_v = 0.0, 0.0, 0.0
            for h in range(2):
                lanes = head_lanes(h)
                probs = head_probs(queries * lanes.astype(low), key_rows)
                grad_probs = dot_f32(grad_out * lanes.astype(low), values, 1, 1)
                grad_v = grad_v + dot_f32(probs.astype(low), grad_out, 0, 0) * lanes
                shared = jnp.sum(probs * grad_probs, axis=-1, keepdims=True)
                scores = (probs * (grad_probs - shared)).astype(low)
                grad_q = grad_q + dot_f32(scores, key_rows, 1, 0) * lanes
                grad_k = grad_k + dot_f32(scores, queries, 0, 0) * lanes
            grads[at, q_at] = (grad_q.astype(low).astype(f32) * HD ** (-0.5)).astype(low)
            grads[at, k_at] = grad_k.astype(low)
            grads[at, v_at] = grad_v.astype(low)

    sums[2:3] = total(grads[:, :width].astype(f32))
    sums[3:4] = total(grads[:, 2 * width :].astype(f32))
    for n in range(3):
        at = pl.ds(n * width, width)
        dense_grad[:, at] = dot_f32(normed[...], grads[:, at], 0, 0).astype(low)
    grad = dot_f32(grads[...], dense[:, : 3 * width], 1, 1)
    upper = grad.astype(low)
    lower = (grad - upper.astype(f32)).astype(low)
    grad = dot_f32(upper, sort[...], 1, 1) + dot_f32(lower, sort[...], 1, 1)
    centred, scale = row_norm(tokens[...].astype(f32))
    back, gain_terms = norm_back(centred, scale, vecs[0:1], grad)
    sums[0:1] = total(gain_terms)
    sums[1:2] = total(grad)
    tokens_grad[...] = grad_mid[...] + back


def local_call(kernel, outs, scratch, flops, args):
    spec = pl.BlockSpec(memory_space=pltpu.VMEM)
    return pl.pallas_call(
        kernel,
        out_shape=tuple(jax.ShapeDtypeStruct(shape, kind) for shape, kind in outs),
        in_specs=[spec] * len(args),
        out_specs=(spec,) * len(outs),
        scratch_shapes=[pltpu.VMEM(shape, kind) for shape, kind in scratch],
        compiler_params=pltpu.CompilerParams(vmem_limit_bytes=48 * 1024 * 1024),
        cost_estimate=pl.CostEstimate(
            flops=flops, bytes_accessed=20_000_000, transcendentals=1_000_000
        ),
    )(*args)


def on_device(
    n_dev,
    tokens,
    ln1_gain,
    ln1_shift,
    qkv_weight,
    qv_bias,
    proj_weight,
    proj_bias,
    ln2_gain,
    ln2_shift,
    router_weight,
    expert_in,
    expert_in_bias,
    expert_out,
    expert_out_bias,
    routes,
    out_grad,
):
    highest = lax.Precision.HIGHEST
    f32 = jnp.float32
    low = jnp.bfloat16
    model_width = tokens.shape[1]
    spare = -LEN % 16
    row_count = SEQ_DEV * (LEN + spare)

    def spread_rows(array, fill=0):
        array = array.reshape(SEQ_DEV, LEN, -1)
        array = jnp.pad(array, ((0, 0), (0, spare), (0, 0)), constant_values=fill)
        return array.reshape(row_count, -1)

    def close_rows(array):
        return array.reshape(SEQ_DEV, LEN + spare, -1)[:, :LEN].reshape(SEQ_DEV * LEN, -1)

    tokens = spread_rows(tokens)
    out_grad = spread_rows(out_grad)
    routes = spread_rows(routes, -1)
    own = qkv_weight.shape[0]
    units = expert_in.shape[0]
    planes = n_dev // PLANE
    each = range(EXPERTS)
    wide = 4 * model_width
    here = lax.axis_index("fsdp")
    core = here % 2
    chip = (here // 2) % EXPERTS
    plane = here // PLANE

    def owner_dense(j):
        s, k, c = j % planes, (j // planes) % EXPERTS, j // (planes * EXPERTS)
        return ((plane - s + planes) % planes) * PLANE + (chip ^ k) * 2 + (core ^ c)

    def owner_units(j):
        k, s, c = j % EXPERTS, (j // EXPERTS) % planes, j // (planes * EXPERTS)
        return ((plane - s + planes) % planes) * PLANE + (chip ^ k) * 2 + (core ^ c)

    devices = jnp.arange(n_dev, dtype=jnp.int32)
    sort_dense = (devices[:, None] == owner_dense(devices)[None, :]).astype(low)
    sort_units = (devices[:, None] == owner_units(devices)[None, :]).astype(low)
    features = jnp.arange(model_width, dtype=jnp.int32)
    home = owner_dense(features // own) * own + features % own
    sort_rows = (features[:, None] == home[None, :]).astype(low)

    small_parts = [
        ln1_gain,
        ln1_shift,
        qv_bias.reshape(-1),
        proj_bias,
        ln2_gain,
        ln2_shift,
        router_weight.T.reshape(-1),
        expert_out_bias.reshape(-1),
        expert_in_bias.T.reshape(-1),
    ]
    small_widths = [p.shape[0] for p in small_parts]
    small_total = sum(small_widths)
    small_room = own * LANES
    small_mine = jnp.pad(jnp.concatenate(small_parts), (0, small_room - small_total))
    dense_mine = jnp.concatenate(
        [qkv_weight, proj_weight, small_mine.reshape(own, LANES)], axis=1
    )
    weight_mine = jnp.stack([expert_in.transpose(1, 0, 2), expert_out.transpose(1, 0, 2)])
    dense, own_half = gather_weights(dense_mine, weight_mine, n_dev)
    dense = dense.reshape(model_width, wide + LANES)

    small = dense[:, wide:].reshape(n_dev, small_room)
    small = dot_f32(sort_dense, small, 1, 0).astype(low)
    gain1, shift1, bias_qv, bias_proj, gain2, shift2, w_router, bias_out, bias_in = take_columns(
        small, small_widths
    )
    vecs = [gain1, shift1, bias_qv[:, :own], bias_qv[:, own:], bias_proj, gain2, shift2, shift2]
    vecs = jnp.stack([v.reshape(-1) for v in vecs]).astype(f32)
    w_router = jnp.stack([p.reshape(-1) for p in take_columns(w_router, [own] * EXPERTS)])
    bias_out = jnp.stack([p.reshape(-1) for p in take_columns(bias_out, [own] * EXPERTS)])
    mine = (jnp.arange(EXPERTS, dtype=jnp.int32) == chip).astype(f32)
    bias_out = jnp.sum(bias_out.astype(f32) * mine[:, None], axis=0)
    bias_in = jnp.stack(take_columns(bias_in, [units] * EXPERTS)).astype(f32)
    bias_in = jnp.sum(bias_in * mine[:, None, None], axis=0).astype(low)
    bias_in = dot_f32(sort_units, bias_in, 0, 0).reshape(2, n_dev * units // 2)

    experts = jnp.arange(EXPERTS, dtype=jnp.int32)[None, :]
    pick = [(routes[:, j : j + 1] == experts).astype(f32) for j in range(TOP)]
    picked = pick[0] + pick[1]
    tri = jnp.arange(row_count)[:, None] > jnp.arange(row_count)[None, :]
    before = dot_f32(tri.astype(low), picked.astype(low), 1, 0)
    slot_ids = jnp.arange(EXPERTS * SLOTS, dtype=jnp.int32)[None, :]
    hit = []
    for j in range(TOP):
        slot = jnp.sum(pick[j] * before, axis=1, keepdims=True).astype(jnp.int32)
        hit.append(slot_ids == (routes[:, j : j + 1] ^ chip) * SLOTS + slot)
    dispatch = (hit[0] | hit[1]).astype(low)

    square = (row_count, model_width)
    router = jnp.pad(w_router, ((0, LANES - EXPERTS), (0, 0)))
    middle, normed2, logits, qkv, normed, attended = local_call(
        forward_kernel,
        [
            (square, f32),
            (square, low),
            ((row_count, LANES), f32),
            ((row_count, 3 * model_width), low),
            (square, low),
            (square, low),
        ],
        [(square, low)],
        20_000_000_000,
        (tokens, dense, vecs, sort_rows, router),
    )
    gate_probs = jax.nn.softmax(logits[:, :EXPERTS], axis=-1)
    chosen = [jnp.sum(gate_probs * pick[j], axis=1, keepdims=True) for j in range(TOP)]
    combine = (jnp.where(hit[0], chosen[0], 0.0) + jnp.where(hit[1], chosen[1], 0.0)).astype(low)

    def exchange(rows):
        pieces = [rows[k * SLOTS : (k + 1) * SLOTS] for k in each]
        pieces = [to_chip(p, k, n_dev) if k else p for k, p in enumerate(pieces)]
        return jnp.concatenate(pieces, axis=0)

    four = (EXPERTS, SLOTS, model_width)
    own_half, other_half, slot_rows, grad_result = exchange_rows(
        own_half,
        dot_f32(dispatch, normed2, 0, 0).astype(low).reshape(four),
        dot_f32(combine, out_grad, 0, 0).astype(low).reshape(four),
        n_dev,
    )
    slot_rows = slot_rows.reshape(EXPERTS * SLOTS, model_width)
    grad_result = grad_result.reshape(EXPERTS * SLOTS, model_width)
    halves = [h.reshape(2, n_dev * units // 2, model_width) for h in (own_half, other_half)]
    w_in = [half[0] for half in halves]
    w_out = [half[1] for half in halves]

    hidden, grad_pre, pulls = [], [], []
    for c in range(2):
        pre_act = dot_f32(slot_rows, w_in[c], 1, 1) + bias_in[c]
        out, pull = jax.vjp(gelu_tanh, pre_act)
        hidden.append(out.astype(low))
        pulls.append(pull)
    result = dot_f32(hidden[0], w_out[0], 1, 0) + dot_f32(hidden[1], w_out[1], 1, 0)
    result = exchange((result + bias_out).astype(low))
    for c in range(2):
        grad_pre.append(pulls[c](dot_f32(grad_result, w_out[c], 1, 1))[0].astype(low))
    grad_slots = dot_f32(grad_pre[0], w_in[0], 1, 0) + dot_f32(grad_pre[1], w_in[1], 1, 0)
    grad_slots = exchange(grad_slots.astype(low))

    theirs = jnp.stack(
        [
            dot_f32(grad_pre[1], slot_rows, 0, 0).astype(low),
            dot_f32(hidden[1], grad_result, 0, 0).astype(low),
        ]
    )
    theirs = to_core(theirs, n_dev)
    terms = jnp.stack(
        [dot_f32(grad_pre[0], slot_rows, 0, 0), dot_f32(hidden[0], grad_result, 0, 0)]
    )
    terms = (terms + theirs.astype(f32)).astype(low)
    grad_slots = after(grad_slots, terms)
    result = after(result, terms)
    span = EXPERTS * units
    terms = [terms[:, s * span : (s + 1) * span] for s in range(planes)]
    hops = scatter_start(terms, n_dev)

    grad_bias_in = jnp.concatenate([jnp.sum(g.astype(f32), axis=0) for g in grad_pre])
    grad_bias_in = jnp.dot(
        sort_units.astype(f32), grad_bias_in.reshape(n_dev, units), precision=highest
    )
    grad_bias_in = (mine[None, :, None] * grad_bias_in[:, None, :]).reshape(n_dev, EXPERTS * units)
    grad_bias_out = mine[:, None] * jnp.sum(grad_result.astype(f32), axis=0)[None, :]

    block_out = (middle + jnp.dot(combine, result, preferred_element_type=f32)).astype(low)

    slot_dots = dot_f32(out_grad, result, 1, 1)
    grad_gates = sum(
        pick[j] * jnp.sum(jnp.where(hit[j], slot_dots, 0.0), axis=1, keepdims=True)
        for j in range(TOP)
    )
    grad_logits = gate_probs * (
        grad_gates - jnp.sum(gate_probs * grad_gates, axis=-1, keepdims=True)
    )
    grad_router = jnp.dot(grad_logits.T, normed2.astype(f32), precision=highest)
    grad_normed2 = jnp.dot(grad_logits, w_router.astype(f32), precision=highest)
    grad_normed2 = grad_normed2 + jnp.dot(dispatch, grad_slots, preferred_element_type=f32)
    dense_grad, tokens_grad, sums = local_call(
        backward_kernel,
        [((model_width, wide), low), (square, f32), ((8, model_width), f32)],
        [(square, f32), (square, low), ((row_count, 3 * model_width), low)],
        20_000_000_000,
        (
            tokens, dense, vecs, sort_rows, middle, qkv, normed, attended, out_grad,
            grad_normed2,
        ),
    )
    expert_mine = scatter_end(terms, scatter_middle(terms, hops, n_dev), n_dev).astype(low)

    def by_owner(rows):
        return rows.reshape(-1, n_dev, rows.shape[-1] // n_dev).transpose(1, 0, 2).reshape(n_dev, -1)

    small_grads = jnp.concatenate(
        [
            by_owner(
                jnp.concatenate(
                    [
                        sums[:7],
                        grad_router,
                        grad_bias_out,
                    ],
                    axis=0,
                )
            ),
            grad_bias_in,
        ],
        axis=1,
    ).astype(low)
    small_grads = jnp.pad(small_grads, ((0, 0), (0, small_room - small_total)))
    small_grads = dot_f32(sort_dense, small_grads, 0, 0).astype(low)
    dense_grads = jnp.concatenate(
        [
            dense_grad,
            small_grads.reshape(n_dev * own, LANES),
        ],
        axis=1,
    )
    half = n_dev * own // 2
    theirs = to_core(dense_grads[half:], n_dev)
    total = (dense_grads[:half].astype(f32) + theirs.astype(f32)).astype(low)
    span = planes * own
    pieces = [total[k * span : (k + 1) * span] for k in each]
    pieces = [to_chip(p, k, n_dev) if k else p for k, p in enumerate(pieces)]
    total = sum(p.astype(f32) for p in pieces).astype(low)
    dense_out = scatter_direct([total[s * own : (s + 1) * own] for s in range(planes)], n_dev)
    pieces = [expert_mine[:, k * units : (k + 1) * units] for k in each]
    pieces = [to_chip(p, k, n_dev) if k else p for k, p in enumerate(pieces)]
    low_bit, high_bit = (chip & 1) == 1, (chip & 2) == 2
    pieces = [jnp.where(low_bit, pieces[k ^ 1], pieces[k]) for k in each]
    pieces = [jnp.where(high_bit, pieces[k ^ 2], pieces[k]) for k in each]
    expert_in_mine, expert_out_mine = [
        jnp.stack([p[w] for p in pieces], axis=1).astype(f32) for w in range(2)
    ]
    small = dense_out[:, wide:].reshape(1, small_room)
    small = [p[0] for p in take_columns(small, small_widths)]
    return (
        close_rows(block_out),
        close_rows(tokens_grad),
        small[0],
        small[1],
        dense_out[:, : 3 * model_width],
        small[2].reshape(2, own),
        dense_out[:, 3 * model_width : wide],
        small[3],
        small[4],
        small[5],
        small[6].reshape(EXPERTS, own).T,
        expert_in_mine,
        small[8].reshape(EXPERTS, units).T,
        expert_out_mine,
        small[7].reshape(EXPERTS, own),
    )


def solution(mesh):
    row, flat, wide_row = P("fsdp", None), P("fsdp"), P(None, "fsdp")
    unit = P("fsdp", None, None)
    in_specs = (
        row, flat, flat, row, wide_row, row, flat, flat, flat, row,
        unit, row, unit, wide_row, row, row,
    )
    out_specs = (
        row, row, flat, flat, row, wide_row, row, flat, flat, flat, row,
        unit, row, unit, wide_row,
    )
    return jax.shard_map(
        functools.partial(on_device, mesh.shape["fsdp"]),
        mesh=mesh,
        in_specs=in_specs,
        out_specs=out_specs,
        check_vma=False,
    )
```

```python
import functools

import jax
import jax.numpy as jnp
from jax import lax
from jax.experimental import pallas as pl
from jax.experimental.pallas import tpu as pltpu
from jax.sharding import PartitionSpec as P

HD = 64
EXPERTS = 4
TOP = 2
LEN = 197
SEQ_DEV = 2
SLOTS = 256
PLANE = 2 * EXPERTS
LANES = 128


def gelu_tanh(values):
    return jax.nn.gelu(values, approximate=True)


def take_columns(block, widths):
    pieces, at = [], 0
    for width in widths:
        pieces.append(block[:, at : at + width])
        at += width
    return pieces


def dot_f32(left, right, left_dim, right_dim):
    return lax.dot_general(
        left,
        right,
        (((left_dim,), (right_dim,)), ((), ())),
        preferred_element_type=jnp.float32,
    )


def to_chip(array, k, n_dev):
    return lax.ppermute(array, "fsdp", [(i, i ^ (2 * k)) for i in range(n_dev)])


def to_core(array, n_dev):
    return lax.ppermute(array, "fsdp", [(i, i ^ 1) for i in range(n_dev)])


def after(value, *others):
    return lax.optimization_barrier((value,) + others)[0]


def place():
    here = lax.axis_index("fsdp")
    return here % 2, (here // 2) % EXPERTS, here // PLANE


def chip_apart(chip, k):
    x, y = chip % 2, chip // 2
    x = 1 - x if k % 2 else x
    y = 1 - y if k // 2 else y
    return 2 * y + x


def entry_barrier(planes, shifts):
    core, chip, plane = place()
    barrier = pltpu.get_barrier_semaphore()
    greeted = [plane * PLANE + chip * 2 + 1 - core]
    greeted += [plane * PLANE + chip_apart(chip, k) * 2 + core for k in range(1, EXPERTS)]
    greeted += [(plane + s) % planes * PLANE + chip * 2 + core for s in shifts]
    for device in greeted:
        pl.semaphore_signal(
            barrier, inc=1, device_id=(device,), device_id_type=pl.DeviceIdType.MESH
        )
    pl.semaphore_wait(barrier, len(greeted))


def remote(src, dst, send, recv, device):
    return pltpu.make_async_remote_copy(
        src_ref=src,
        dst_ref=dst,
        send_sem=send,
        recv_sem=recv,
        device_id=(device,),
        device_id_type=pl.DeviceIdType.MESH,
    )


def gather_kernel(
    planes, dense_in, weight_in, dense, weight,
    line_send, line_recv, hop_send, hop_recv, chip_send, chip_recv,
    part_send, part_recv, core_send, core_recv, local,
):
    core, chip, plane = place()
    last = planes - 1
    other = plane * PLANE + chip * 2 + 1 - core
    above = (plane + 1) * PLANE + chip * 2 + core
    below = (plane - 1) * PLANE + chip * 2 + core

    def peer(k):
        return plane * PLANE + chip_apart(chip, k) * 2 + core

    def line(slot, up):
        to = slot + 1 if up else (slot - 1) % planes
        return remote(
            dense.at[0, 0, slot], dense.at[0, 0, to],
            line_send.at[int(up), slot], line_recv.at[to], above if up else below,
        )

    def arrived(slot):
        return remote(
            dense.at[0, 0, slot], dense.at[0, 0, slot],
            line_send.at[0, slot], line_recv.at[slot], other,
        )

    def hop(up):
        to = 1 if up else last
        return remote(
            weight.at[:, 0], weight.at[:, to],
            hop_send.at[int(up)], hop_recv.at[to], above if up else below,
        )

    def hop_arrived(slot):
        return remote(
            weight.at[:, slot], weight.at[:, slot], hop_send.at[0], hop_recv.at[slot], other
        )

    parts = [
        remote(
            weight_in.at[:, chip_apart(chip, k)], weight.at[:, 0, k],
            part_send.at[k], part_recv.at[k], peer(k),
        )
        for k in range(1, EXPERTS)
    ]
    own_dense = pltpu.make_async_copy(dense_in, dense.at[0, 0, 0], local.at[0])
    own_part = pltpu.make_async_copy(weight_in.at[:, chip], weight.at[:, 0, 0], local.at[1])
    own_dense.start()
    own_part.start()
    entry_barrier(planes, (1, planes - 1))
    own_dense.wait()

    @pl.when(plane < last)
    def _():
        line(0, True).start()

    @pl.when(plane > 0)
    def _():
        line(0, False).start()

    for part in parts:
        part.start()

    def direct(slot, k):
        return remote(
            dense.at[0, 0, slot], dense.at[0, k, slot],
            chip_send.at[k, slot], chip_recv.at[k, slot], peer(k),
        )

    def first(slot):
        return 1 + slot % 2

    def onward(slot):
        k = first(slot)
        return remote(
            dense.at[0, k, slot], dense.at[0, 3, slot],
            chip_send.at[3, slot], chip_recv.at[3, slot], peer(3 - k),
        )

    def swap(slot, k):
        return remote(
            dense.at[0, k, slot], dense.at[1, k, slot],
            core_send.at[k, slot], core_recv.at[k, slot], other,
        )

    for d in range(1, planes):
        @pl.when(plane >= d)
        def _(d=d):
            arrived(d).wait_recv()

            @pl.when(plane < last)
            def _():
                line(d, True).start()

        @pl.when(plane <= last - d)
        def _(d=d):
            arrived(planes - d).wait_recv()

            @pl.when(plane > 0)
            def _():
                line(planes - d, False).start()

        if d == 1:
            for k in (1, 2):
                direct(0, k).start()
            swap(0, 0).start()

    for slot in range(1, planes):
        for k in (1, 2):
            direct(slot, k).start()
        swap(slot, 0).start()
    own_part.wait()
    for part in parts:
        part.wait()

    @pl.when(plane < last)
    def _():
        hop(True).start()

    @pl.when(plane > 0)
    def _():
        hop(False).start()

    for slot in range(planes):
        direct(slot, first(slot)).wait_recv()
        onward(slot).start()
        swap(slot, first(slot)).start()
    for slot in range(planes):
        direct(slot, 3 - first(slot)).wait_recv()
        swap(slot, 3 - first(slot)).start()
    for slot in range(planes):
        onward(slot).wait_recv()
        swap(slot, 3).start()
    for slot in range(planes):
        for k in (1, 2):
            direct(slot, k).wait_send()
        onward(slot).wait_send()
        for k in range(EXPERTS):
            swap(slot, k).wait()

    @pl.when(plane < last)
    def _():
        line(0, True).wait_send()
        hop(True).wait_send()
        hop_arrived(last).wait_recv()

    @pl.when(plane > 0)
    def _():
        line(0, False).wait_send()
        hop(False).wait_send()
        hop_arrived(1).wait_recv()

    for d in range(1, planes):
        @pl.when((plane >= d) & (plane < last))
        def _(d=d):
            line(d, True).wait_send()

        @pl.when((plane <= last - d) & (plane > 0))
        def _(d=d):
            line(planes - d, False).wait_send()


def gather_weights(dense_mine, weight_mine, n_dev):
    planes = n_dev // PLANE
    _, _, units, width = weight_mine.shape
    sem = pltpu.SemaphoreType.DMA
    any_spec = pl.BlockSpec(memory_space=pl.ANY)
    return pl.pallas_call(
        functools.partial(gather_kernel, planes),
        out_shape=(
            jax.ShapeDtypeStruct((2, EXPERTS, planes) + dense_mine.shape, dense_mine.dtype),
            jax.ShapeDtypeStruct((2, planes, EXPERTS, units, width), weight_mine.dtype),
        ),
        in_specs=[any_spec] * 2,
        out_specs=(any_spec,) * 2,
        scratch_shapes=[
            sem((2, planes)), sem((planes,)), sem((2,)), sem((planes,)),
            sem((EXPERTS, planes)), sem((EXPERTS, planes)),
            sem((EXPERTS,)), sem((EXPERTS,)),
            sem((EXPERTS, planes)), sem((EXPERTS, planes)), sem((2,)),
        ],
        compiler_params=pltpu.CompilerParams(collective_id=1, has_side_effects=True),
        cost_estimate=pl.CostEstimate(flops=0, bytes_accessed=100_000_000, transcendentals=0),
    )(dense_mine, weight_mine)


def exchange_kernel(
    planes, weight_in, rows, grads, weight, theirs, got_rows, got_grads,
    hop_send, hop_recv, core_send, core_recv, row_send, row_recv, local,
):
    core, chip, plane = place()
    last = planes - 1
    other = plane * PLANE + chip * 2 + 1 - core
    above = (plane + 1) * PLANE + chip * 2 + core
    below = (plane - 1) * PLANE + chip * 2 + core

    def hop(slot, up):
        to = slot + 1 if up else (slot - 1) % planes
        return remote(
            weight.at[:, slot], weight.at[:, to],
            hop_send.at[slot], hop_recv.at[to], above if up else below,
        )

    def hop_arrived(slot):
        return remote(
            weight.at[:, slot], weight.at[:, slot], hop_send.at[slot], hop_recv.at[slot], other
        )

    def swap(slot):
        return remote(
            weight.at[:, slot], theirs.at[:, slot],
            core_send.at[slot], core_recv.at[slot], other,
        )

    keep = [
        pltpu.make_async_copy(rows.at[0], got_rows.at[0], local.at[0]),
        pltpu.make_async_copy(grads.at[0], got_grads.at[0], local.at[1]),
    ]
    for copy in keep:
        copy.start()
    entry_barrier(planes, (1, planes - 1))

    def onward(d, wait):
        @pl.when(plane >= d)
        def _():
            if wait:
                hop_arrived(d).wait_recv()

            @pl.when(plane < last)
            def _():
                hop(d, True).start()

            swap(d).start()

        @pl.when(plane <= last - d)
        def _():
            if wait:
                hop_arrived(planes - d).wait_recv()

            @pl.when(plane > 0)
            def _():
                hop(planes - d, False).start()

            swap(planes - d).start()

    onward(1, False)
    trades = []
    for n, (src, dst) in enumerate(((rows, got_rows), (grads, got_grads))):
        for k in range(1, EXPERTS):
            trades.append(
                remote(
                    src.at[k], dst.at[k], row_send.at[n, k], row_recv.at[n, k],
                    plane * PLANE + chip_apart(chip, k) * 2 + core,
                )
            )
    for trade in trades:
        trade.start()
    swap(0).start()
    for d in range(2, planes):
        onward(d, True)
    for trade in trades:
        trade.wait()
    for copy in keep:
        copy.wait()
    for slot in range(planes):
        swap(slot).wait()
    for d in range(1, planes):
        @pl.when((plane >= d) & (plane < last))
        def _(d=d):
            hop(d, True).wait_send()

        @pl.when((plane <= last - d) & (plane > 0))
        def _(d=d):
            hop(planes - d, False).wait_send()


def exchange_rows(weight, rows, grads, n_dev):
    planes = n_dev // PLANE
    sem = pltpu.SemaphoreType.DMA
    any_spec = pl.BlockSpec(memory_space=pl.ANY)

    def like(array):
        return jax.ShapeDtypeStruct(array.shape, array.dtype)

    return pl.pallas_call(
        functools.partial(exchange_kernel, planes),
        out_shape=(like(weight), like(weight), like(rows), like(grads)),
        in_specs=[any_spec] * 3,
        out_specs=(any_spec,) * 4,
        input_output_aliases={0: 0},
        scratch_shapes=[
            sem((planes,)), sem((planes,)), sem((planes,)), sem((planes,)),
            sem((2, EXPERTS)), sem((2, EXPERTS)), sem((2,)),
        ],
        compiler_params=pltpu.CompilerParams(collective_id=2, has_side_effects=True),
        cost_estimate=pl.CostEstimate(flops=0, bytes_accessed=150_000_000, transcendentals=0),
    )(weight, rows, grads)


def row_norm(values):
    centred = values - jnp.mean(values, axis=-1, keepdims=True)
    spread = jnp.mean(centred * centred, axis=-1, keepdims=True)
    return centred, lax.rsqrt(spread + 1e-06)


def norm_back(centred, scale, gain_vec, grad):
    inner = grad * gain_vec
    unit = centred * scale
    shared = jnp.mean(inner, axis=-1, keepdims=True)
    slope = jnp.mean(inner * unit, axis=-1, keepdims=True)
    return scale * (inner - shared - unit * slope), unit * grad


def head_lanes(h):
    lane = lax.broadcasted_iota(jnp.int32, (1, 2 * HD), 1)
    return (lane // HD == h).astype(jnp.float32)


def head_probs(queries, key_rows):
    scores = dot_f32(queries, key_rows, 1, 1)
    key = lax.broadcasted_iota(jnp.int32, scores.shape, 1)
    scores = jnp.where(key < LEN, scores, -1e30)
    scores = jnp.exp(scores - jnp.max(scores, axis=-1, keepdims=True))
    return scores * (1.0 / jnp.sum(scores, axis=-1, keepdims=True))


def forward_kernel(
    tokens, dense, vecs, sort, router, middle, normed2, logits, qkv, normed, attended, heads
):
    f32, low = jnp.float32, jnp.bfloat16
    width = tokens.shape[1]
    rows = tokens.shape[0] // SEQ_DEV
    inputs = tokens[...].astype(f32)
    centred, scale = row_norm(inputs)
    plain = (centred * scale * vecs[0:1] + vecs[1:2]).astype(low)
    normed[...] = dot_f32(plain, sort[...], 1, 0).astype(low)
    queries = dot_f32(normed[...], dense[:, :width], 1, 0)
    qkv[:, :width] = ((queries + vecs[2:3]) * HD ** (-0.5)).astype(low)
    key_rows = dot_f32(normed[...], dense[:, width : 2 * width], 1, 0)
    qkv[:, width : 2 * width] = key_rows.astype(low)
    values = dot_f32(normed[...], dense[:, 2 * width : 3 * width], 1, 0)
    qkv[:, 2 * width : 3 * width] = (values + vecs[3:4]).astype(low)

    @pl.loop(0, width // (2 * HD))
    def _(pair):
        q_at, k_at, v_at = [
            pl.ds(pl.multiple_of(pair * 2 * HD + n * width, 2 * HD), 2 * HD) for n in range(3)
        ]
        for seq in range(SEQ_DEV):
            at = pl.ds(seq * rows, rows)
            total = 0.0
            for h in range(2):
                lanes = head_lanes(h)
                probs = head_probs(qkv[at, q_at] * lanes.astype(low), qkv[at, k_at])
                total = total + dot_f32(probs.astype(low), qkv[at, v_at], 1, 0) * lanes
            heads[at, q_at] = total.astype(low)

    attended[...] = dot_f32(heads[...], sort[...], 1, 0).astype(low)
    branch = dot_f32(attended[...], dense[:, 3 * width : 4 * width], 1, 0)
    middle[...] = inputs + branch + vecs[4:5]
    centred, scale = row_norm(middle[...])
    normed2[...] = (centred * scale * vecs[5:6] + vecs[6:7]).astype(low)
    logits[...] = dot_f32(normed2[...], router[...], 1, 1)


def backward_kernel(
    planes, tokens, dense, vecs, sort, middle, qkv, normed, attended, out_grad, grad_normed2,
    terms, small_in, tokens_grad, dense_out, small_out, expert,
    grad_mid, heads, grads, dense_grad, dense_core, dense_chip, dense_send, dense_line,
    up, down, mine, small, small_got, send, recv, local,
):
    f32, low = jnp.float32, jnp.bfloat16
    width = tokens.shape[1]
    rows = tokens.shape[0] // SEQ_DEV
    own = dense_out.shape[0]
    half, span = planes * EXPERTS * own, planes * own
    core, chip, plane = place()
    last = planes - 1
    other = plane * PLANE + chip * 2 + 1 - core
    above = (plane + 1) * PLANE + chip * 2 + core
    below = (plane - 1) * PLANE + chip * 2 + core
    used = [0]
    sums = small.at[0]

    def copy(src, dst, device):
        used[0] += 1
        return remote(src, dst, send.at[used[0] - 1], recv.at[used[0] - 1], device)

    def peer(k):
        return plane * PLANE + chip_apart(chip, k) * 2 + core

    def away(s):
        return (plane + planes - s) % planes * PLANE + chip * 2 + core

    def total(rows_of):
        return jnp.sum(rows_of, axis=0, keepdims=True)

    first_up, next_up, first_down, next_down = {}, {}, {}, {}
    for t in range(1, planes):
        first_up[t] = copy(terms.at[:, t], up.at[t], above)
        first_down[t] = copy(terms.at[:, planes - t], down.at[t], below)
        n = used[0]
        if t > 1:
            next_up[t] = remote(up.at[t - 1], up.at[t], send.at[n - 2], recv.at[n - 2], above)
            next_down[t] = remote(
                down.at[t - 1], down.at[t], send.at[n - 1], recv.at[n - 1], below
            )

    def add_terms(buffer, slot):
        @pl.loop(0, 2 * EXPERTS)
        def _(i):
            w, k = i // EXPERTS, i % EXPERTS
            got = buffer[w, k].astype(f32) + terms[w, slot, k].astype(f32)
            buffer[w, k] = got.astype(low)

    def hop(t):
        @pl.when(plane == 0)
        def _():
            first_up[t].start()

        @pl.when(plane == last)
        def _():
            first_down[t].start()

        if t > 1:
            @pl.when((plane >= 1) & (plane <= t - 1))
            def _():
                first_up[t - 1].wait_recv()
                add_terms(up.at[t - 1], t)
                next_up[t].start()

            @pl.when((plane <= last - 1) & (plane >= planes - t))
            def _():
                first_down[t - 1].wait_recv()
                add_terms(down.at[t - 1], planes - t)
                next_down[t].start()

    entry_barrier(planes, range(1, planes))
    hop(1)
    centred, scale = row_norm(middle[...])
    grad = grad_normed2[...]
    back, gain_terms = norm_back(centred, scale, vecs[5:6], grad)
    sums[5:6] = total(gain_terms)
    sums[6:7] = total(grad)
    sums[7:8] = jnp.zeros((1, width), f32)
    sums[8:] = small_in[8:]
    grad_mid[...] = out_grad[...].astype(f32) + back
    branch = grad_mid[...].astype(low)
    sums[4:5] = total(branch.astype(f32))
    dense_grad[:, 3 * width : 4 * width] = dot_f32(attended[...], branch, 0, 0).astype(low)
    grad_att = dot_f32(branch, dense[:, 3 * width : 4 * width], 1, 1).astype(low)
    heads[...] = dot_f32(grad_att, sort[...], 1, 1).astype(low)

    @pl.loop(0, width // (2 * HD))
    def _(pair):
        q_at, k_at, v_at = [
            pl.ds(pl.multiple_of(pair * 2 * HD + n * width, 2 * HD), 2 * HD) for n in range(3)
        ]
        for seq in range(SEQ_DEV):
            at = pl.ds(seq * rows, rows)
            queries, key_rows, values = qkv[at, q_at], qkv[at, k_at], qkv[at, v_at]
            grad_out = heads[at, q_at]
            grad_q, grad_k, grad_v = 0.0, 0.0, 0.0
            for h in range(2):
                lanes = head_lanes(h)
                probs = head_probs(queries * lanes.astype(low), key_rows)
                grad_probs = dot_f32(grad_out * lanes.astype(low), values, 1, 1)
                grad_v = grad_v + dot_f32(probs.astype(low), grad_out, 0, 0) * lanes
                shared = jnp.sum(probs * grad_probs, axis=-1, keepdims=True)
                scores = (probs * (grad_probs - shared)).astype(low)
                grad_q = grad_q + dot_f32(scores, key_rows, 1, 0) * lanes
                grad_k = grad_k + dot_f32(scores, queries, 0, 0) * lanes
            grads[at, q_at] = (grad_q.astype(low).astype(f32) * HD ** (-0.5)).astype(low)
            grads[at, k_at] = grad_k.astype(low)
            grads[at, v_at] = grad_v.astype(low)

    sums[2:3] = total(grads[:, :width].astype(f32))
    sums[3:4] = total(grads[:, 2 * width :].astype(f32))
    for n in range(3):
        at = pl.ds(n * width, width)
        dense_grad[:, at] = dot_f32(normed[...], grads[:, at], 0, 0).astype(low)
    core_copies = [
        copy(
            dense_grad.at[pl.ds(half + k * span, span)],
            dense_core.at[pl.ds(k * span, span)],
            other,
        )
        for k in (1, 2, 3, 0)
    ]
    for sent in core_copies:
        sent.start()
    grad = dot_f32(grads[...], dense[:, : 3 * width], 1, 1)
    upper = grad.astype(low)
    lower = (grad - upper.astype(f32)).astype(low)
    grad = dot_f32(upper, sort[...], 1, 1) + dot_f32(lower, sort[...], 1, 1)
    centred, scale = row_norm(tokens[...].astype(f32))
    back, gain_terms = norm_back(centred, scale, vecs[0:1], grad)
    sums[0:1] = total(gain_terms)
    sums[1:2] = total(grad)
    tokens_grad[...] = grad_mid[...] + back

    small_copies = [copy(small.at[0], small_got.at[0], other)]
    small_copies += [copy(small.at[k], small_got.at[k], peer(k)) for k in (1, 2)]
    small_copies += [
        copy(small.at[3], small_got.at[2 + s], away(s)) for s in range(1, planes)
    ]

    def small_step(n):
        small_copies[n].wait_recv()
        small[n + 1] = small[n] + small_got[n]

    small_copies[0].start()
    chip_copies = []
    for n, k in enumerate((1, 2, 3, 0)):
        core_copies[n].wait_recv()
        at = pl.ds(k * span, span)
        both = dense_grad[at].astype(f32) + dense_core[at].astype(f32)
        dense_grad[at] = both.astype(low)
        if k:
            chip_copies.append(copy(dense_grad.at[at], dense_chip.at[k - 1], peer(k)))
            chip_copies[-1].start()
    small_step(0)
    small_copies[1].start()
    for t in range(2, planes - 1):
        hop(t)
    small_step(1)
    small_copies[2].start()
    small_step(2)
    for sent in small_copies[3:]:
        sent.start()
    for sent in chip_copies:
        sent.wait_recv()
    line_copies = []
    for n in range(4):
        at = pl.ds(n * width, width)
        both = dense_grad[:span, at].astype(f32)
        for k in range(1, EXPERTS):
            both = both + dense_chip[k - 1, :, at].astype(f32)
        dense_out[:, at] = both[:own]
        for s in range(1, planes):
            dense_send[s, :, at] = both[s * own : (s + 1) * own].astype(low)
    for s in range(1, planes):
        line_copies.append(copy(dense_send.at[s], dense_line.at[s], away(s)))
        line_copies[-1].start()
    if planes > 2:
        hop(last)

    @pl.when(plane >= 1)
    def _():
        first_up[last].wait_recv()

    @pl.when(plane <= last - 1)
    def _():
        first_down[last].wait_recv()

    def finish(buffers):
        @pl.loop(0, 2 * EXPERTS)
        def _(i):
            w, k = i // EXPERTS, i % EXPERTS
            got = terms[w, 0, k].astype(f32)
            for buffer in buffers:
                got = got + buffer[last, w, k].astype(f32)
            mine[k, w] = got.astype(low)

    @pl.when(plane == 0)
    def _():
        finish([down])

    @pl.when(plane == last)
    def _():
        finish([up])

    @pl.when((plane > 0) & (plane < last))
    def _():
        finish([up, down])

    unit_copies = [copy(mine.at[k], expert.at[chip], peer(k)) for k in range(1, EXPERTS)]
    for sent in unit_copies:
        sent.start()
    kept = pltpu.make_async_copy(mine.at[0], expert.at[chip], local.at[0])
    kept.start()
    for sent in line_copies:
        sent.wait_recv()
    for s in range(1, planes):
        dense_out[...] = dense_out[...] + dense_line[s].astype(f32)
    for sent in small_copies[3:]:
        sent.wait_recv()
    every = small[3]
    for s in range(1, planes):
        every = every + small_got[2 + s]
    small_out[...] = every
    for sent in core_copies + small_copies + chip_copies + line_copies:
        sent.wait_send()
    for t in range(1, planes):
        @pl.when(plane <= t - 1)
        def _(t=t):
            first_up[t].wait_send()

        @pl.when(plane >= planes - t)
        def _(t=t):
            first_down[t].wait_send()

    kept.wait()
    for sent in unit_copies:
        sent.wait()


def backward(planes, own, args):
    f32, low = jnp.float32, jnp.bfloat16
    square, width = args[0].shape, args[0].shape[1]
    terms, small_in = args[-2:]
    units = terms.shape[3]
    block = (2, EXPERTS, units, width)
    half, span, wide = planes * EXPERTS * own, planes * own, 4 * width
    spec = pl.BlockSpec(memory_space=pltpu.VMEM)
    shape = jax.ShapeDtypeStruct
    copies = 20 + 5 * planes
    return pl.pallas_call(
        functools.partial(backward_kernel, planes),
        out_shape=(
            shape(square, f32),
            shape((own, wide), f32),
            shape(small_in.shape, f32),
            shape((EXPERTS, 2, units, width), low),
        ),
        in_specs=[spec] * len(args),
        out_specs=(spec,) * 4,
        scratch_shapes=[
            pltpu.VMEM(square, f32),
            pltpu.VMEM(square, low),
            pltpu.VMEM((square[0], 3 * width), low),
            pltpu.VMEM((2 * half, wide), low),
            pltpu.VMEM((half, wide), low),
            pltpu.VMEM((EXPERTS - 1, span, wide), low),
            pltpu.VMEM((planes, own, wide), low),
            pltpu.VMEM((planes, own, wide), low),
            pltpu.VMEM((planes,) + block, low),
            pltpu.VMEM((planes,) + block, low),
            pltpu.VMEM((EXPERTS, 2, units, width), low),
            pltpu.VMEM((4,) + small_in.shape, f32),
            pltpu.VMEM((2 + planes,) + small_in.shape, f32),
            pltpu.SemaphoreType.DMA((copies,)),
            pltpu.SemaphoreType.DMA((copies,)),
            pltpu.SemaphoreType.DMA((1,)),
        ],
        compiler_params=pltpu.CompilerParams(
            collective_id=3, has_side_effects=True, vmem_limit_bytes=60 * 1024 * 1024
        ),
        cost_estimate=pl.CostEstimate(
            flops=20_000_000_000, bytes_accessed=50_000_000, transcendentals=1_000_000
        ),
    )(*args)


def local_call(kernel, outs, scratch, flops, args):
    spec = pl.BlockSpec(memory_space=pltpu.VMEM)
    return pl.pallas_call(
        kernel,
        out_shape=tuple(jax.ShapeDtypeStruct(shape, kind) for shape, kind in outs),
        in_specs=[spec] * len(args),
        out_specs=(spec,) * len(outs),
        scratch_shapes=[pltpu.VMEM(shape, kind) for shape, kind in scratch],
        compiler_params=pltpu.CompilerParams(vmem_limit_bytes=48 * 1024 * 1024),
        cost_estimate=pl.CostEstimate(
            flops=flops, bytes_accessed=20_000_000, transcendentals=1_000_000
        ),
    )(*args)


def on_device(
    n_dev,
    tokens,
    ln1_gain,
    ln1_shift,
    qkv_weight,
    qv_bias,
    proj_weight,
    proj_bias,
    ln2_gain,
    ln2_shift,
    router_weight,
    expert_in,
    expert_in_bias,
    expert_out,
    expert_out_bias,
    routes,
    out_grad,
):
    highest = lax.Precision.HIGHEST
    f32 = jnp.float32
    low = jnp.bfloat16
    model_width = tokens.shape[1]
    spare = -LEN % 16
    row_count = SEQ_DEV * (LEN + spare)

    def spread_rows(array, fill=0):
        array = array.reshape(SEQ_DEV, LEN, -1)
        array = jnp.pad(array, ((0, 0), (0, spare), (0, 0)), constant_values=fill)
        return array.reshape(row_count, -1)

    def close_rows(array):
        return array.reshape(SEQ_DEV, LEN + spare, -1)[:, :LEN].reshape(SEQ_DEV * LEN, -1)

    tokens = spread_rows(tokens)
    out_grad = spread_rows(out_grad)
    routes = spread_rows(routes, -1)
    own = qkv_weight.shape[0]
    units = expert_in.shape[0]
    planes = n_dev // PLANE
    each = range(EXPERTS)
    wide = 4 * model_width
    here = lax.axis_index("fsdp")
    core = here % 2
    chip = (here // 2) % EXPERTS
    plane = here // PLANE

    def owner_dense(j):
        s, k, c = j % planes, (j // planes) % EXPERTS, j // (planes * EXPERTS)
        return ((plane - s + planes) % planes) * PLANE + (chip ^ k) * 2 + (core ^ c)

    def owner_units(j):
        k, s, c = j % EXPERTS, (j // EXPERTS) % planes, j // (planes * EXPERTS)
        return ((plane - s + planes) % planes) * PLANE + (chip ^ k) * 2 + (core ^ c)

    devices = jnp.arange(n_dev, dtype=jnp.int32)
    sort_dense = (devices[:, None] == owner_dense(devices)[None, :]).astype(low)
    sort_units = (devices[:, None] == owner_units(devices)[None, :]).astype(low)
    features = jnp.arange(model_width, dtype=jnp.int32)
    home = owner_dense(features // own) * own + features % own
    sort_rows = (features[:, None] == home[None, :]).astype(low)

    small_parts = [
        ln1_gain,
        ln1_shift,
        qv_bias.reshape(-1),
        proj_bias,
        ln2_gain,
        ln2_shift,
        router_weight.T.reshape(-1),
        expert_out_bias.reshape(-1),
        expert_in_bias.T.reshape(-1),
    ]
    small_widths = [p.shape[0] for p in small_parts]
    small_total = sum(small_widths)
    small_room = own * LANES
    small_mine = jnp.pad(jnp.concatenate(small_parts), (0, small_room - small_total))
    dense_mine = jnp.concatenate(
        [qkv_weight, proj_weight, small_mine.reshape(own, LANES)], axis=1
    )
    weight_mine = jnp.stack([expert_in.transpose(1, 0, 2), expert_out.transpose(1, 0, 2)])
    dense, own_half = gather_weights(dense_mine, weight_mine, n_dev)
    dense = dense.reshape(model_width, wide + LANES)

    small = dense[:, wide:].reshape(n_dev, small_room)
    small = dot_f32(sort_dense, small, 1, 0).astype(low)
    gain1, shift1, bias_qv, bias_proj, gain2, shift2, w_router, bias_out, bias_in = take_columns(
        small, small_widths
    )
    vecs = [gain1, shift1, bias_qv[:, :own], bias_qv[:, own:], bias_proj, gain2, shift2, shift2]
    vecs = jnp.stack([v.reshape(-1) for v in vecs]).astype(f32)
    w_router = jnp.stack([p.reshape(-1) for p in take_columns(w_router, [own] * EXPERTS)])
    bias_out = jnp.stack([p.reshape(-1) for p in take_columns(bias_out, [own] * EXPERTS)])
    mine = (jnp.arange(EXPERTS, dtype=jnp.int32) == chip).astype(f32)
    bias_out = jnp.sum(bias_out.astype(f32) * mine[:, None], axis=0)
    bias_in = jnp.stack(take_columns(bias_in, [units] * EXPERTS)).astype(f32)
    bias_in = jnp.sum(bias_in * mine[:, None, None], axis=0).astype(low)
    bias_in = dot_f32(sort_units, bias_in, 0, 0).reshape(2, n_dev * units // 2)

    experts = jnp.arange(EXPERTS, dtype=jnp.int32)[None, :]
    pick = [(routes[:, j : j + 1] == experts).astype(f32) for j in range(TOP)]
    picked = pick[0] + pick[1]
    tri = jnp.arange(row_count)[:, None] > jnp.arange(row_count)[None, :]
    before = dot_f32(tri.astype(low), picked.astype(low), 1, 0)
    slot_ids = jnp.arange(EXPERTS * SLOTS, dtype=jnp.int32)[None, :]
    hit = []
    for j in range(TOP):
        slot = jnp.sum(pick[j] * before, axis=1, keepdims=True).astype(jnp.int32)
        hit.append(slot_ids == (routes[:, j : j + 1] ^ chip) * SLOTS + slot)
    dispatch = (hit[0] | hit[1]).astype(low)

    square = (row_count, model_width)
    router = jnp.pad(w_router, ((0, LANES - EXPERTS), (0, 0)))
    middle, normed2, logits, qkv, normed, attended = local_call(
        forward_kernel,
        [
            (square, f32),
            (square, low),
            ((row_count, LANES), f32),
            ((row_count, 3 * model_width), low),
            (square, low),
            (square, low),
        ],
        [(square, low)],
        20_000_000_000,
        (tokens, dense, vecs, sort_rows, router),
    )
    gate_probs = jax.nn.softmax(logits[:, :EXPERTS], axis=-1)
    chosen = [jnp.sum(gate_probs * pick[j], axis=1, keepdims=True) for j in range(TOP)]
    combine = (jnp.where(hit[0], chosen[0], 0.0) + jnp.where(hit[1], chosen[1], 0.0)).astype(low)

    def exchange(rows):
        pieces = [rows[k * SLOTS : (k + 1) * SLOTS] for k in each]
        pieces = [to_chip(p, k, n_dev) if k else p for k, p in enumerate(pieces)]
        return jnp.concatenate(pieces, axis=0)

    four = (EXPERTS, SLOTS, model_width)
    own_half, other_half, slot_rows, grad_result = exchange_rows(
        own_half,
        dot_f32(dispatch, normed2, 0, 0).astype(low).reshape(four),
        dot_f32(combine, out_grad, 0, 0).astype(low).reshape(four),
        n_dev,
    )
    slot_rows = slot_rows.reshape(EXPERTS * SLOTS, model_width)
    grad_result = grad_result.reshape(EXPERTS * SLOTS, model_width)
    halves = [h.reshape(2, n_dev * units // 2, model_width) for h in (own_half, other_half)]
    w_in = [half[0] for half in halves]
    w_out = [half[1] for half in halves]

    hidden, grad_pre, pulls = [], [], []
    for c in range(2):
        pre_act = dot_f32(slot_rows, w_in[c], 1, 1) + bias_in[c]
        out, pull = jax.vjp(gelu_tanh, pre_act)
        hidden.append(out.astype(low))
        pulls.append(pull)
    result = dot_f32(hidden[0], w_out[0], 1, 0) + dot_f32(hidden[1], w_out[1], 1, 0)
    result = exchange((result + bias_out).astype(low))
    for c in range(2):
        grad_pre.append(pulls[c](dot_f32(grad_result, w_out[c], 1, 1))[0].astype(low))
    grad_slots = dot_f32(grad_pre[0], w_in[0], 1, 0) + dot_f32(grad_pre[1], w_in[1], 1, 0)
    grad_slots = exchange(grad_slots.astype(low))

    theirs = jnp.stack(
        [
            dot_f32(grad_pre[1], slot_rows, 0, 0).astype(low),
            dot_f32(hidden[1], grad_result, 0, 0).astype(low),
        ]
    )
    theirs = to_core(theirs, n_dev)
    terms = jnp.stack(
        [dot_f32(grad_pre[0], slot_rows, 0, 0), dot_f32(hidden[0], grad_result, 0, 0)]
    )
    terms = (terms + theirs.astype(f32)).astype(low)
    grad_slots = after(grad_slots, terms)
    result = after(result, terms)
    terms = terms.reshape(2, planes, EXPERTS, units, model_width)

    grad_bias_in = jnp.concatenate([jnp.sum(g.astype(f32), axis=0) for g in grad_pre])
    grad_bias_in = jnp.dot(
        sort_units.astype(f32), grad_bias_in.reshape(n_dev, units), precision=highest
    )
    grad_bias_in = mine[:, None] * grad_bias_in.reshape(1, n_dev * units)
    grad_bias_out = mine[:, None] * jnp.sum(grad_result.astype(f32), axis=0)[None, :]

    block_out = (middle + jnp.dot(combine, result, preferred_element_type=f32)).astype(low)

    slot_dots = dot_f32(out_grad, result, 1, 1)
    grad_gates = sum(
        pick[j] * jnp.sum(jnp.where(hit[j], slot_dots, 0.0), axis=1, keepdims=True)
        for j in range(TOP)
    )
    grad_logits = gate_probs * (
        grad_gates - jnp.sum(gate_probs * grad_gates, axis=-1, keepdims=True)
    )
    grad_router = jnp.dot(grad_logits.T, normed2.astype(f32), precision=highest)
    grad_normed2 = jnp.dot(grad_logits, w_router.astype(f32), precision=highest)
    grad_normed2 = grad_normed2 + jnp.dot(dispatch, grad_slots, preferred_element_type=f32)
    small_in = jnp.concatenate(
        [
            jnp.zeros((8, model_width), f32),
            grad_router,
            grad_bias_out,
            grad_bias_in.reshape(-1, model_width),
        ]
    )
    tokens_grad, dense_out, small_out, expert_out_terms = backward(
        planes,
        own,
        (
            tokens, dense, vecs, sort_rows, middle, qkv, normed, attended, out_grad,
            grad_normed2, terms, small_in,
        ),
    )
    small = lax.dynamic_slice_in_dim(small_out[:16], here * own, own, axis=1)
    bias_in_mine = lax.dynamic_slice_in_dim(
        small_out[16:].reshape(EXPERTS, n_dev * units), here * units, units, axis=1
    )
    expert_in_mine, expert_out_mine = [
        expert_out_terms[:, w].transpose(1, 0, 2).astype(f32) for w in range(2)
    ]
    return (
        close_rows(block_out),
        close_rows(tokens_grad),
        small[0],
        small[1],
        dense_out[:, : 3 * model_width],
        small[2:4],
        dense_out[:, 3 * model_width :],
        small[4],
        small[5],
        small[6],
        small[8:12].T,
        expert_in_mine,
        bias_in_mine.T,
        expert_out_mine,
        small[12:16],
    )


def solution(mesh):
    row, flat, wide_row = P("fsdp", None), P("fsdp"), P(None, "fsdp")
    unit = P("fsdp", None, None)
    in_specs = (
        row, flat, flat, row, wide_row, row, flat, flat, flat, row,
        unit, row, unit, wide_row, row, row,
    )
    out_specs = (
        row, row, flat, flat, row, wide_row, row, flat, flat, flat, row,
        unit, row, unit, wide_row,
    )
    return jax.shard_map(
        functools.partial(on_device, mesh.shape["fsdp"]),
        mesh=mesh,
        in_specs=in_specs,
        out_specs=out_specs,
        check_vma=False,
    )
```

```python
import functools

import jax
import jax.numpy as jnp
from jax import lax
from jax.experimental import pallas as pl
from jax.experimental.pallas import tpu as pltpu
from jax.sharding import PartitionSpec as P

HD = 64
EXPERTS = 4
TOP = 2
LEN = 197
SEQ_DEV = 2
SLOTS = 256
PLANE = 2 * EXPERTS
LANES = 128


def gelu_tanh(values):
    return jax.nn.gelu(values, approximate=True)


def take_columns(block, widths):
    pieces, at = [], 0
    for width in widths:
        pieces.append(block[:, at : at + width])
        at += width
    return pieces


def dot_f32(left, right, left_dim, right_dim):
    return lax.dot_general(
        left,
        right,
        (((left_dim,), (right_dim,)), ((), ())),
        preferred_element_type=jnp.float32,
    )


def to_chip(array, k, n_dev):
    return lax.ppermute(array, "fsdp", [(i, i ^ (2 * k)) for i in range(n_dev)])


def to_core(array, n_dev):
    return lax.ppermute(array, "fsdp", [(i, i ^ 1) for i in range(n_dev)])


def after(value, *others):
    return lax.optimization_barrier((value,) + others)[0]


def place():
    here = lax.axis_index("fsdp")
    return here % 2, (here // 2) % EXPERTS, here // PLANE


def chip_apart(chip, k):
    x, y = chip % 2, chip // 2
    x = 1 - x if k % 2 else x
    y = 1 - y if k // 2 else y
    return 2 * y + x


def entry_barrier(planes, shifts):
    core, chip, plane = place()
    barrier = pltpu.get_barrier_semaphore()
    greeted = [plane * PLANE + chip * 2 + 1 - core]
    greeted += [plane * PLANE + chip_apart(chip, k) * 2 + core for k in range(1, EXPERTS)]
    greeted += [(plane + s) % planes * PLANE + chip * 2 + core for s in shifts]
    for device in greeted:
        pl.semaphore_signal(
            barrier, inc=1, device_id=(device,), device_id_type=pl.DeviceIdType.MESH
        )
    pl.semaphore_wait(barrier, len(greeted))


def remote(src, dst, send, recv, device):
    return pltpu.make_async_remote_copy(
        src_ref=src,
        dst_ref=dst,
        send_sem=send,
        recv_sem=recv,
        device_id=(device,),
        device_id_type=pl.DeviceIdType.MESH,
    )


def gather_kernel(
    planes, dense_in, weight_in, dense, weight,
    line_send, line_recv, hop_send, hop_recv, chip_send, chip_recv,
    part_send, part_recv, core_send, core_recv, local,
):
    core, chip, plane = place()
    last = planes - 1
    other = plane * PLANE + chip * 2 + 1 - core
    above = (plane + 1) * PLANE + chip * 2 + core
    below = (plane - 1) * PLANE + chip * 2 + core

    def peer(k):
        return plane * PLANE + chip_apart(chip, k) * 2 + core

    def line(slot, up):
        to = slot + 1 if up else (slot - 1) % planes
        return remote(
            dense.at[0, 0, slot], dense.at[0, 0, to],
            line_send.at[int(up), slot], line_recv.at[to], above if up else below,
        )

    def arrived(slot):
        return remote(
            dense.at[0, 0, slot], dense.at[0, 0, slot],
            line_send.at[0, slot], line_recv.at[slot], other,
        )

    def hop(up):
        to = 1 if up else last
        return remote(
            weight.at[:, 0], weight.at[:, to],
            hop_send.at[int(up)], hop_recv.at[to], above if up else below,
        )

    def hop_arrived(slot):
        return remote(
            weight.at[:, slot], weight.at[:, slot], hop_send.at[0], hop_recv.at[slot], other
        )

    parts = [
        remote(
            weight_in.at[:, chip_apart(chip, k)], weight.at[:, 0, k],
            part_send.at[k], part_recv.at[k], peer(k),
        )
        for k in range(1, EXPERTS)
    ]
    own_dense = pltpu.make_async_copy(dense_in, dense.at[0, 0, 0], local.at[0])
    own_part = pltpu.make_async_copy(weight_in.at[:, chip], weight.at[:, 0, 0], local.at[1])
    own_dense.start()
    own_part.start()
    entry_barrier(planes, (1, planes - 1))
    own_dense.wait()

    @pl.when(plane < last)
    def _():
        line(0, True).start()

    @pl.when(plane > 0)
    def _():
        line(0, False).start()

    for part in parts:
        part.start()

    def direct(slot, k):
        return remote(
            dense.at[0, 0, slot], dense.at[0, k, slot],
            chip_send.at[k, slot], chip_recv.at[k, slot], peer(k),
        )

    def first(slot):
        return 1 + slot % 2

    def onward(slot):
        k = first(slot)
        return remote(
            dense.at[0, k, slot], dense.at[0, 3, slot],
            chip_send.at[3, slot], chip_recv.at[3, slot], peer(3 - k),
        )

    def swap(slot, k):
        return remote(
            dense.at[0, k, slot], dense.at[1, k, slot],
            core_send.at[k, slot], core_recv.at[k, slot], other,
        )

    for d in range(1, planes):
        @pl.when(plane >= d)
        def _(d=d):
            arrived(d).wait_recv()

            @pl.when(plane < last)
            def _():
                line(d, True).start()

        @pl.when(plane <= last - d)
        def _(d=d):
            arrived(planes - d).wait_recv()

            @pl.when(plane > 0)
            def _():
                line(planes - d, False).start()

        if d == 1:
            for k in (1, 2):
                direct(0, k).start()
            swap(0, 0).start()

    for slot in range(1, planes):
        for k in (1, 2):
            direct(slot, k).start()
        swap(slot, 0).start()
    own_part.wait()
    for part in parts:
        part.wait()

    @pl.when(plane < last)
    def _():
        hop(True).start()

    @pl.when(plane > 0)
    def _():
        hop(False).start()

    for slot in range(planes):
        direct(slot, first(slot)).wait_recv()
        onward(slot).start()
        swap(slot, first(slot)).start()
    for slot in range(planes):
        direct(slot, 3 - first(slot)).wait_recv()
        swap(slot, 3 - first(slot)).start()
    for slot in range(planes):
        onward(slot).wait_recv()
        swap(slot, 3).start()
    for slot in range(planes):
        for k in (1, 2):
            direct(slot, k).wait_send()
        onward(slot).wait_send()
        for k in range(EXPERTS):
            swap(slot, k).wait()

    @pl.when(plane < last)
    def _():
        line(0, True).wait_send()
        hop(True).wait_send()
        hop_arrived(last).wait_recv()

    @pl.when(plane > 0)
    def _():
        line(0, False).wait_send()
        hop(False).wait_send()
        hop_arrived(1).wait_recv()

    for d in range(1, planes):
        @pl.when((plane >= d) & (plane < last))
        def _(d=d):
            line(d, True).wait_send()

        @pl.when((plane <= last - d) & (plane > 0))
        def _(d=d):
            line(planes - d, False).wait_send()


def gather_weights(dense_mine, weight_mine, n_dev):
    planes = n_dev // PLANE
    _, _, units, width = weight_mine.shape
    sem = pltpu.SemaphoreType.DMA
    any_spec = pl.BlockSpec(memory_space=pl.ANY)
    return pl.pallas_call(
        functools.partial(gather_kernel, planes),
        out_shape=(
            jax.ShapeDtypeStruct((2, EXPERTS, planes) + dense_mine.shape, dense_mine.dtype),
            jax.ShapeDtypeStruct((2, planes, EXPERTS, units, width), weight_mine.dtype),
        ),
        in_specs=[any_spec] * 2,
        out_specs=(any_spec,) * 2,
        scratch_shapes=[
            sem((2, planes)), sem((planes,)), sem((2,)), sem((planes,)),
            sem((EXPERTS, planes)), sem((EXPERTS, planes)),
            sem((EXPERTS,)), sem((EXPERTS,)),
            sem((EXPERTS, planes)), sem((EXPERTS, planes)), sem((2,)),
        ],
        compiler_params=pltpu.CompilerParams(collective_id=1, has_side_effects=True),
        cost_estimate=pl.CostEstimate(flops=0, bytes_accessed=100_000_000, transcendentals=0),
    )(dense_mine, weight_mine)


def forward_exchange_kernel(
    planes, weight_in, tokens, dense, vecs, sort, router, out_grad, routes, columns,
    weight, theirs, got_rows, got_grads, dispatch, combine, gates,
    middle, normed2, qkv, normed, attended,
    heads, rows, grads, hop_send, hop_recv, core_send, core_recv, row_send, row_recv, local,
):
    f32, low = jnp.float32, jnp.bfloat16
    core, chip, plane = place()
    last = planes - 1
    other = plane * PLANE + chip * 2 + 1 - core
    above = (plane + 1) * PLANE + chip * 2 + core
    below = (plane - 1) * PLANE + chip * 2 + core

    def hop(slot, up):
        to = slot + 1 if up else (slot - 1) % planes
        return remote(
            weight.at[:, slot], weight.at[:, to],
            hop_send.at[slot], hop_recv.at[to], above if up else below,
        )

    def hop_arrived(slot):
        return remote(
            weight.at[:, slot], weight.at[:, slot], hop_send.at[slot], hop_recv.at[slot], other
        )

    def swap(slot):
        return remote(
            weight.at[:, slot], theirs.at[:, slot],
            core_send.at[slot], core_recv.at[slot], other,
        )

    keep = [
        pltpu.make_async_copy(rows.at[0], got_rows.at[0], local.at[0]),
        pltpu.make_async_copy(grads.at[0], got_grads.at[0], local.at[1]),
    ]
    entry_barrier(planes, (1, planes - 1))

    def onward(d, wait):
        @pl.when(plane >= d)
        def _():
            if wait:
                hop_arrived(d).wait_recv()

            @pl.when(plane < last)
            def _():
                hop(d, True).start()

            swap(d).start()

        @pl.when(plane <= last - d)
        def _():
            if wait:
                hop_arrived(planes - d).wait_recv()

            @pl.when(plane > 0)
            def _():
                hop(planes - d, False).start()

            swap(planes - d).start()

    onward(1, False)
    trades = []
    for n, (src, dst) in enumerate(((rows, got_rows), (grads, got_grads))):
        for k in range(1, EXPERTS):
            trades.append(
                remote(
                    src.at[k], dst.at[k], row_send.at[n, k], row_recv.at[n, k],
                    plane * PLANE + chip_apart(chip, k) * 2 + core,
                )
            )
    swap(0).start()
    forward_part(
        tokens, dense, vecs, sort, router, middle, normed2, gates, qkv, normed, attended, heads
    )

    lane = lax.broadcasted_iota(jnp.int32, gates.shape, 1)
    logits = jnp.where(lane < EXPERTS, gates[...], -1e30)
    chance = jnp.exp(logits - jnp.max(logits, axis=-1, keepdims=True))
    chance = chance / jnp.sum(chance, axis=-1, keepdims=True)
    gates[...] = chance
    slot = lax.broadcasted_iota(jnp.int32, dispatch.shape, 1)
    marks, shares = 0.0, 0.0
    for j in range(TOP):
        pick = jnp.where(lane == routes[:, j : j + 1], chance, 0.0)
        chosen = jnp.sum(pick, axis=1, keepdims=True)
        hit = slot == columns[:, j : j + 1]
        marks = marks + jnp.where(hit, 1.0, 0.0)
        shares = shares + jnp.where(hit, chosen, 0.0)
    dispatch[...] = marks.astype(low)
    combine[...] = shares.astype(low)
    for n, (sent, table, source) in enumerate(
        ((rows, dispatch, normed2), (grads, combine, out_grad))
    ):
        for k in (3, 1, 2, 0):
            at = pl.ds(k * SLOTS, SLOTS)
            sent[k] = dot_f32(table[:, at], source[...], 0, 0).astype(low)
            if k:
                trades[n * (EXPERTS - 1) + k - 1].start()
        keep[n].start()
    for d in range(2, planes):
        onward(d, True)
    for trade in trades:
        trade.wait()
    for copy in keep:
        copy.wait()
    for slot in range(planes):
        swap(slot).wait()
    for d in range(1, planes):
        @pl.when((plane >= d) & (plane < last))
        def _(d=d):
            hop(d, True).wait_send()

        @pl.when((plane <= last - d) & (plane > 0))
        def _(d=d):
            hop(planes - d, False).wait_send()


def forward_exchange(n_dev, args):
    planes = n_dev // PLANE
    f32, low = jnp.float32, jnp.bfloat16
    weight, tokens = args[:2]
    count, width = tokens.shape
    sem = pltpu.SemaphoreType.DMA
    anywhere = pl.BlockSpec(memory_space=pl.ANY)
    vmem = pl.BlockSpec(memory_space=pltpu.VMEM)
    shape = jax.ShapeDtypeStruct
    slots = (EXPERTS, SLOTS, width)
    table = shape((count, EXPERTS * SLOTS), low)
    return pl.pallas_call(
        functools.partial(forward_exchange_kernel, planes),
        out_shape=(
            shape(weight.shape, low),
            shape(weight.shape, low),
            shape(slots, low),
            shape(slots, low),
            table,
            table,
            shape((count, LANES), f32),
            shape((count, width), f32),
            shape((count, width), low),
            shape((count, 3 * width), low),
            shape((count, width), low),
            shape((count, width), low),
        ),
        in_specs=[anywhere] + [vmem] * (len(args) - 1),
        out_specs=(anywhere,) * 4 + (vmem,) * 8,
        input_output_aliases={0: 0},
        scratch_shapes=[
            pltpu.VMEM((count, width), low),
            pltpu.VMEM(slots, low),
            pltpu.VMEM(slots, low),
            sem((planes,)), sem((planes,)), sem((planes,)), sem((planes,)),
            sem((2, EXPERTS)), sem((2, EXPERTS)), sem((2,)),
        ],
        compiler_params=pltpu.CompilerParams(
            collective_id=2, has_side_effects=True, vmem_limit_bytes=48 * 1024 * 1024
        ),
        cost_estimate=pl.CostEstimate(
            flops=20_000_000_000, bytes_accessed=100_000_000, transcendentals=1_000_000
        ),
    )(*args)


def row_norm(values):
    centred = values - jnp.mean(values, axis=-1, keepdims=True)
    spread = jnp.mean(centred * centred, axis=-1, keepdims=True)
    return centred, lax.rsqrt(spread + 1e-06)


def norm_back(centred, scale, gain_vec, grad):
    inner = grad * gain_vec
    unit = centred * scale
    shared = jnp.mean(inner, axis=-1, keepdims=True)
    slope = jnp.mean(inner * unit, axis=-1, keepdims=True)
    return scale * (inner - shared - unit * slope), unit * grad


def head_lanes(h):
    lane = lax.broadcasted_iota(jnp.int32, (1, 2 * HD), 1)
    return (lane // HD == h).astype(jnp.float32)


def head_probs(queries, key_rows):
    scores = dot_f32(queries, key_rows, 1, 1)
    key = lax.broadcasted_iota(jnp.int32, scores.shape, 1)
    scores = jnp.where(key < LEN, scores, -1e30)
    scores = jnp.exp(scores - jnp.max(scores, axis=-1, keepdims=True))
    return scores * (1.0 / jnp.sum(scores, axis=-1, keepdims=True))


def forward_part(
    tokens, dense, vecs, sort, router, middle, normed2, logits, qkv, normed, attended, heads
):
    f32, low = jnp.float32, jnp.bfloat16
    width = tokens.shape[1]
    rows = tokens.shape[0] // SEQ_DEV
    inputs = tokens[...].astype(f32)
    centred, scale = row_norm(inputs)
    plain = (centred * scale * vecs[0:1] + vecs[1:2]).astype(low)
    normed[...] = dot_f32(plain, sort[...], 1, 0).astype(low)
    queries = dot_f32(normed[...], dense[:, :width], 1, 0)
    qkv[:, :width] = ((queries + vecs[2:3]) * HD ** (-0.5)).astype(low)
    key_rows = dot_f32(normed[...], dense[:, width : 2 * width], 1, 0)
    qkv[:, width : 2 * width] = key_rows.astype(low)
    values = dot_f32(normed[...], dense[:, 2 * width : 3 * width], 1, 0)
    qkv[:, 2 * width : 3 * width] = (values + vecs[3:4]).astype(low)

    @pl.loop(0, width // (2 * HD))
    def _(pair):
        q_at, k_at, v_at = [
            pl.ds(pl.multiple_of(pair * 2 * HD + n * width, 2 * HD), 2 * HD) for n in range(3)
        ]
        for seq in range(SEQ_DEV):
            at = pl.ds(seq * rows, rows)
            total = 0.0
            for h in range(2):
                lanes = head_lanes(h)
                probs = head_probs(qkv[at, q_at] * lanes.astype(low), qkv[at, k_at])
                total = total + dot_f32(probs.astype(low), qkv[at, v_at], 1, 0) * lanes
            heads[at, q_at] = total.astype(low)

    attended[...] = dot_f32(heads[...], sort[...], 1, 0).astype(low)
    branch = dot_f32(attended[...], dense[:, 3 * width : 4 * width], 1, 0)
    middle[...] = inputs + branch + vecs[4:5]
    centred, scale = row_norm(middle[...])
    normed2[...] = (centred * scale * vecs[5:6] + vecs[6:7]).astype(low)
    logits[...] = dot_f32(normed2[...], router[...], 1, 1)


def backward_kernel(
    planes, tokens, dense, vecs, sort, middle, qkv, normed, attended, out_grad, grad_normed2,
    terms, small_in, tokens_grad, dense_out, small_out, expert,
    grad_mid, heads, grads, dense_grad, dense_core, dense_chip, dense_send, dense_line,
    up, down, mine, small, small_got, send, recv, local,
):
    f32, low = jnp.float32, jnp.bfloat16
    width = tokens.shape[1]
    rows = tokens.shape[0] // SEQ_DEV
    own = dense_out.shape[0]
    half, span = planes * EXPERTS * own, planes * own
    core, chip, plane = place()
    last = planes - 1
    other = plane * PLANE + chip * 2 + 1 - core
    above = (plane + 1) * PLANE + chip * 2 + core
    below = (plane - 1) * PLANE + chip * 2 + core
    used = [0]
    sums = small.at[0]

    def copy(src, dst, device):
        used[0] += 1
        return remote(src, dst, send.at[used[0] - 1], recv.at[used[0] - 1], device)

    def peer(k):
        return plane * PLANE + chip_apart(chip, k) * 2 + core

    def away(s):
        return (plane + planes - s) % planes * PLANE + chip * 2 + core

    def total(rows_of):
        return jnp.sum(rows_of, axis=0, keepdims=True)

    first_up, next_up, first_down, next_down = {}, {}, {}, {}
    for t in range(1, planes):
        for w in range(2):
            first_up[t, w] = copy(terms.at[w, t], up.at[t - 1, w], above)
            first_down[t, w] = copy(terms.at[w, planes - t], down.at[t - 1, w], below)
            n = used[0]
            if t > 1:
                next_up[t, w] = remote(
                    up.at[t - 2, w], up.at[t - 1, w], send.at[n - 2], recv.at[n - 2], above
                )
                next_down[t, w] = remote(
                    down.at[t - 2, w], down.at[t - 1, w], send.at[n - 1], recv.at[n - 1], below
                )

    def add_terms(buffer, w, slot):
        @pl.loop(0, EXPERTS)
        def _(k):
            got = buffer[w, k].astype(f32) + terms[w, slot, k].astype(f32)
            buffer[w, k] = got.astype(low)

    def hop(t):
        for w in range(2):
            @pl.when(plane == 0)
            def _(w=w):
                first_up[t, w].start()

            @pl.when(plane == last)
            def _(w=w):
                first_down[t, w].start()

            if t == 1:
                continue

            @pl.when((plane >= 1) & (plane <= t - 1))
            def _(w=w):
                first_up[t - 1, w].wait_recv()
                add_terms(up.at[t - 2], w, t)
                next_up[t, w].start()

            @pl.when((plane <= last - 1) & (plane >= planes - t))
            def _(w=w):
                first_down[t - 1, w].wait_recv()
                add_terms(down.at[t - 2], w, planes - t)
                next_down[t, w].start()

    entry_barrier(planes, range(1, planes))
    hop(1)
    centred, scale = row_norm(middle[...])
    grad = grad_normed2[...]
    back, gain_terms = norm_back(centred, scale, vecs[5:6], grad)
    sums[5:6] = total(gain_terms)
    sums[6:7] = total(grad)
    sums[7:8] = jnp.zeros((1, width), f32)
    sums[8:] = small_in[8:]
    grad_mid[...] = out_grad[...].astype(f32) + back
    branch = grad_mid[...].astype(low)
    sums[4:5] = total(branch.astype(f32))
    dense_grad[:, 3 * width : 4 * width] = dot_f32(attended[...], branch, 0, 0).astype(low)
    grad_att = dot_f32(branch, dense[:, 3 * width : 4 * width], 1, 1).astype(low)
    heads[...] = dot_f32(grad_att, sort[...], 1, 1).astype(low)

    @pl.loop(0, width // (2 * HD))
    def _(pair):
        q_at, k_at, v_at = [
            pl.ds(pl.multiple_of(pair * 2 * HD + n * width, 2 * HD), 2 * HD) for n in range(3)
        ]
        for seq in range(SEQ_DEV):
            at = pl.ds(seq * rows, rows)
            queries, key_rows, values = qkv[at, q_at], qkv[at, k_at], qkv[at, v_at]
            grad_out = heads[at, q_at]
            grad_q, grad_k, grad_v = 0.0, 0.0, 0.0
            for h in range(2):
                lanes = head_lanes(h)
                probs = head_probs(queries * lanes.astype(low), key_rows)
                grad_probs = dot_f32(grad_out * lanes.astype(low), values, 1, 1)
                grad_v = grad_v + dot_f32(probs.astype(low), grad_out, 0, 0) * lanes
                shared = jnp.sum(probs * grad_probs, axis=-1, keepdims=True)
                scores = (probs * (grad_probs - shared)).astype(low)
                grad_q = grad_q + dot_f32(scores, key_rows, 1, 0) * lanes
                grad_k = grad_k + dot_f32(scores, queries, 0, 0) * lanes
            grads[at, q_at] = (grad_q.astype(low).astype(f32) * HD ** (-0.5)).astype(low)
            grads[at, k_at] = grad_k.astype(low)
            grads[at, v_at] = grad_v.astype(low)

    sums[2:3] = total(grads[:, :width].astype(f32))
    sums[3:4] = total(grads[:, 2 * width :].astype(f32))
    for n in range(3):
        at = pl.ds(n * width, width)
        dense_grad[:, at] = dot_f32(normed[...], grads[:, at], 0, 0).astype(low)
    core_copies = [
        copy(
            dense_grad.at[pl.ds(half + k * span, span)],
            dense_core.at[pl.ds(k * span, span)],
            other,
        )
        for k in (1, 2, 3, 0)
    ]
    for sent in core_copies:
        sent.start()
    grad = dot_f32(grads[...], dense[:, : 3 * width], 1, 1)
    upper = grad.astype(low)
    lower = (grad - upper.astype(f32)).astype(low)
    grad = dot_f32(upper, sort[...], 1, 1) + dot_f32(lower, sort[...], 1, 1)
    centred, scale = row_norm(tokens[...].astype(f32))
    back, gain_terms = norm_back(centred, scale, vecs[0:1], grad)
    sums[0:1] = total(gain_terms)
    sums[1:2] = total(grad)
    tokens_grad[...] = grad_mid[...] + back

    small_copies = [copy(small.at[0], small_got.at[0], other)]
    small_copies += [copy(small.at[k], small_got.at[k], peer(k)) for k in (1, 2)]
    small_copies += [
        copy(small.at[3], small_got.at[2 + s], away(s)) for s in range(1, planes)
    ]

    def small_step(n):
        small_copies[n].wait_recv()
        small[n + 1] = small[n] + small_got[n]

    small_copies[0].start()
    chip_copies = []
    for n, k in enumerate((1, 2, 3, 0)):
        core_copies[n].wait_recv()
        at = pl.ds(k * span, span)
        both = dense_grad[at].astype(f32) + dense_core[at].astype(f32)
        dense_grad[at] = both.astype(low)
        if k:
            chip_copies.append(copy(dense_grad.at[at], dense_chip.at[k - 1], peer(k)))
            chip_copies[-1].start()
    for t in range(2, planes - 1):
        hop(t)
    small_step(0)
    small_copies[1].start()
    small_step(1)
    small_copies[2].start()
    small_step(2)
    for sent in small_copies[3:]:
        sent.start()
    if planes > 2:
        hop(last)
    for sent in chip_copies:
        sent.wait_recv()
    line_copies = []
    for n in range(4):
        at = pl.ds(n * width, width)
        both = dense_grad[:span, at].astype(f32)
        for k in range(1, EXPERTS):
            both = both + dense_chip[k - 1, :, at].astype(f32)
        dense_out[:, at] = both[:own]
        for s in range(1, planes):
            dense_send[s, :, at] = both[s * own : (s + 1) * own].astype(low)
    for s in range(1, planes):
        line_copies.append(copy(dense_send.at[s], dense_line.at[s], away(s)))
        line_copies[-1].start()

    def finish(w, buffers):
        @pl.loop(0, EXPERTS)
        def _(k):
            got = terms[w, 0, k].astype(f32)
            for buffer in buffers:
                got = got + buffer[last - 1, w, k].astype(f32)
            mine[w, k] = got.astype(low)

    unit_copies = []
    for w in range(2):
        @pl.when(plane >= 1)
        def _(w=w):
            first_up[last, w].wait_recv()

        @pl.when(plane <= last - 1)
        def _(w=w):
            first_down[last, w].wait_recv()

        @pl.when(plane == 0)
        def _(w=w):
            finish(w, [down])

        @pl.when(plane == last)
        def _(w=w):
            finish(w, [up])

        @pl.when((plane > 0) & (plane < last))
        def _(w=w):
            finish(w, [up, down])

        for k in range(1, EXPERTS):
            unit_copies.append(copy(mine.at[w, k], expert.at[w, chip], peer(k)))
            unit_copies[-1].start()
    kept = pltpu.make_async_copy(mine.at[:, 0], expert.at[:, chip], local.at[0])
    kept.start()
    for sent in line_copies:
        sent.wait_recv()
    for s in range(1, planes):
        dense_out[...] = dense_out[...] + dense_line[s].astype(f32)
    for sent in small_copies[3:]:
        sent.wait_recv()
    every = small[3]
    for s in range(1, planes):
        every = every + small_got[2 + s]
    small_out[...] = every
    for sent in core_copies + small_copies + chip_copies + line_copies:
        sent.wait_send()
    for t in range(1, planes):
        for w in range(2):
            @pl.when(plane <= t - 1)
            def _(t=t, w=w):
                first_up[t, w].wait_send()

            @pl.when(plane >= planes - t)
            def _(t=t, w=w):
                first_down[t, w].wait_send()

    kept.wait()
    for sent in unit_copies:
        sent.wait()


def backward(planes, own, args):
    f32, low = jnp.float32, jnp.bfloat16
    square, width = args[0].shape, args[0].shape[1]
    terms, small_in = args[-2:]
    units = terms.shape[3]
    block = (2, EXPERTS, units, width)
    half, span, wide = planes * EXPERTS * own, planes * own, 4 * width
    spec = pl.BlockSpec(memory_space=pltpu.VMEM)
    shape = jax.ShapeDtypeStruct
    copies = 20 + 8 * planes
    return pl.pallas_call(
        functools.partial(backward_kernel, planes),
        out_shape=(
            shape(square, f32),
            shape((own, wide), f32),
            shape(small_in.shape, f32),
            shape(block, low),
        ),
        in_specs=[spec] * len(args),
        out_specs=(spec,) * 4,
        scratch_shapes=[
            pltpu.VMEM(square, f32),
            pltpu.VMEM(square, low),
            pltpu.VMEM((square[0], 3 * width), low),
            pltpu.VMEM((2 * half, wide), low),
            pltpu.VMEM((half, wide), low),
            pltpu.VMEM((EXPERTS - 1, span, wide), low),
            pltpu.VMEM((planes, own, wide), low),
            pltpu.VMEM((planes, own, wide), low),
            pltpu.VMEM((planes - 1,) + block, low),
            pltpu.VMEM((planes - 1,) + block, low),
            pltpu.VMEM(block, low),
            pltpu.VMEM((4,) + small_in.shape, f32),
            pltpu.VMEM((2 + planes,) + small_in.shape, f32),
            pltpu.SemaphoreType.DMA((copies,)),
            pltpu.SemaphoreType.DMA((copies,)),
            pltpu.SemaphoreType.DMA((1,)),
        ],
        compiler_params=pltpu.CompilerParams(
            collective_id=3, has_side_effects=True, vmem_limit_bytes=60 * 1024 * 1024
        ),
        cost_estimate=pl.CostEstimate(
            flops=20_000_000_000, bytes_accessed=50_000_000, transcendentals=1_000_000
        ),
    )(*args)


def on_device(
    n_dev,
    tokens,
    ln1_gain,
    ln1_shift,
    qkv_weight,
    qv_bias,
    proj_weight,
    proj_bias,
    ln2_gain,
    ln2_shift,
    router_weight,
    expert_in,
    expert_in_bias,
    expert_out,
    expert_out_bias,
    routes,
    out_grad,
):
    highest = lax.Precision.HIGHEST
    f32 = jnp.float32
    low = jnp.bfloat16
    model_width = tokens.shape[1]
    spare = -LEN % 16
    row_count = SEQ_DEV * (LEN + spare)

    def spread_rows(array, fill=0):
        array = array.reshape(SEQ_DEV, LEN, -1)
        array = jnp.pad(array, ((0, 0), (0, spare), (0, 0)), constant_values=fill)
        return array.reshape(row_count, -1)

    def close_rows(array):
        return array.reshape(SEQ_DEV, LEN + spare, -1)[:, :LEN].reshape(SEQ_DEV * LEN, -1)

    tokens = spread_rows(tokens)
    out_grad = spread_rows(out_grad)
    routes = spread_rows(routes, -1)
    own = qkv_weight.shape[0]
    units = expert_in.shape[0]
    planes = n_dev // PLANE
    each = range(EXPERTS)
    wide = 4 * model_width
    here = lax.axis_index("fsdp")
    core = here % 2
    chip = (here // 2) % EXPERTS
    plane = here // PLANE

    def owner_dense(j):
        s, k, c = j % planes, (j // planes) % EXPERTS, j // (planes * EXPERTS)
        return ((plane - s + planes) % planes) * PLANE + (chip ^ k) * 2 + (core ^ c)

    def owner_units(j):
        k, s, c = j % EXPERTS, (j // EXPERTS) % planes, j // (planes * EXPERTS)
        return ((plane - s + planes) % planes) * PLANE + (chip ^ k) * 2 + (core ^ c)

    devices = jnp.arange(n_dev, dtype=jnp.int32)
    sort_dense = (devices[:, None] == owner_dense(devices)[None, :]).astype(low)
    sort_units = (devices[:, None] == owner_units(devices)[None, :]).astype(low)
    features = jnp.arange(model_width, dtype=jnp.int32)
    home = owner_dense(features // own) * own + features % own
    sort_rows = (features[:, None] == home[None, :]).astype(low)

    small_parts = [
        ln1_gain,
        ln1_shift,
        qv_bias.reshape(-1),
        proj_bias,
        ln2_gain,
        ln2_shift,
        router_weight.T.reshape(-1),
        expert_out_bias.reshape(-1),
        expert_in_bias.T.reshape(-1),
    ]
    small_widths = [p.shape[0] for p in small_parts]
    small_total = sum(small_widths)
    small_room = own * LANES
    small_mine = jnp.pad(jnp.concatenate(small_parts), (0, small_room - small_total))
    dense_mine = jnp.concatenate(
        [qkv_weight, proj_weight, small_mine.reshape(own, LANES)], axis=1
    )
    weight_mine = jnp.stack([expert_in.transpose(1, 0, 2), expert_out.transpose(1, 0, 2)])
    dense, own_half = gather_weights(dense_mine, weight_mine, n_dev)
    dense = dense.reshape(model_width, wide + LANES)

    small = dense[:, wide:].reshape(n_dev, small_room)
    small = dot_f32(sort_dense, small, 1, 0).astype(low)
    gain1, shift1, bias_qv, bias_proj, gain2, shift2, w_router, bias_out, bias_in = take_columns(
        small, small_widths
    )
    vecs = [gain1, shift1, bias_qv[:, :own], bias_qv[:, own:], bias_proj, gain2, shift2, shift2]
    vecs = jnp.stack([v.reshape(-1) for v in vecs]).astype(f32)
    w_router = jnp.stack([p.reshape(-1) for p in take_columns(w_router, [own] * EXPERTS)])
    bias_out = jnp.stack([p.reshape(-1) for p in take_columns(bias_out, [own] * EXPERTS)])
    mine = (jnp.arange(EXPERTS, dtype=jnp.int32) == chip).astype(f32)
    bias_out = jnp.sum(bias_out.astype(f32) * mine[:, None], axis=0)
    bias_in = jnp.stack(take_columns(bias_in, [units] * EXPERTS)).astype(f32)
    bias_in = jnp.sum(bias_in * mine[:, None, None], axis=0).astype(low)
    bias_in = dot_f32(sort_units, bias_in, 0, 0).reshape(2, n_dev * units // 2)

    experts = jnp.arange(EXPERTS, dtype=jnp.int32)[None, :]
    pick = [(routes[:, j : j + 1] == experts).astype(f32) for j in range(TOP)]
    picked = pick[0] + pick[1]
    tri = jnp.arange(row_count)[:, None] > jnp.arange(row_count)[None, :]
    before = dot_f32(tri.astype(low), picked.astype(low), 1, 0)
    slot_ids = jnp.arange(EXPERTS * SLOTS, dtype=jnp.int32)[None, :]
    columns = []
    for j in range(TOP):
        slot = jnp.sum(pick[j] * before, axis=1, keepdims=True).astype(jnp.int32)
        columns.append((routes[:, j : j + 1] ^ chip) * SLOTS + slot)
    columns = jnp.concatenate(columns, axis=1)
    hit = [slot_ids == columns[:, j : j + 1] for j in range(TOP)]

    router = jnp.pad(w_router, ((0, LANES - EXPERTS), (0, 0)))
    (
        own_half, other_half, slot_rows, grad_result, dispatch, combine, gates,
        middle, normed2, qkv, normed, attended,
    ) = forward_exchange(
        n_dev,
        (own_half, tokens, dense, vecs, sort_rows, router, out_grad, routes, columns),
    )
    gate_probs = gates[:, :EXPERTS]

    def exchange(rows):
        pieces = [rows[k * SLOTS : (k + 1) * SLOTS] for k in each]
        pieces = [to_chip(p, k, n_dev) if k else p for k, p in enumerate(pieces)]
        return jnp.concatenate(pieces, axis=0)

    slot_rows = slot_rows.reshape(EXPERTS * SLOTS, model_width)
    grad_result = grad_result.reshape(EXPERTS * SLOTS, model_width)
    halves = [h.reshape(2, n_dev * units // 2, model_width) for h in (own_half, other_half)]
    w_in = [half[0] for half in halves]
    w_out = [half[1] for half in halves]

    hidden, grad_pre, pulls = [], [], []
    for c in range(2):
        pre_act = dot_f32(slot_rows, w_in[c], 1, 1) + bias_in[c]
        out, pull = jax.vjp(gelu_tanh, pre_act)
        hidden.append(out.astype(low))
        pulls.append(pull)
    result = dot_f32(hidden[0], w_out[0], 1, 0) + dot_f32(hidden[1], w_out[1], 1, 0)
    result = exchange((result + bias_out).astype(low))
    for c in range(2):
        grad_pre.append(pulls[c](dot_f32(grad_result, w_out[c], 1, 1))[0].astype(low))
    grad_slots = dot_f32(grad_pre[0], w_in[0], 1, 0) + dot_f32(grad_pre[1], w_in[1], 1, 0)
    grad_slots = exchange(grad_slots.astype(low))

    theirs = jnp.stack(
        [
            dot_f32(grad_pre[1], slot_rows, 0, 0).astype(low),
            dot_f32(hidden[1], grad_result, 0, 0).astype(low),
        ]
    )
    theirs = to_core(theirs, n_dev)
    terms = jnp.stack(
        [dot_f32(grad_pre[0], slot_rows, 0, 0), dot_f32(hidden[0], grad_result, 0, 0)]
    )
    terms = (terms + theirs.astype(f32)).astype(low)
    grad_slots = after(grad_slots, terms)
    result = after(result, terms)
    terms = terms.reshape(2, planes, EXPERTS, units, model_width)

    grad_bias_in = jnp.concatenate([jnp.sum(g.astype(f32), axis=0) for g in grad_pre])
    grad_bias_in = jnp.dot(
        sort_units.astype(f32), grad_bias_in.reshape(n_dev, units), precision=highest
    )
    grad_bias_in = mine[:, None] * grad_bias_in.reshape(1, n_dev * units)
    grad_bias_out = mine[:, None] * jnp.sum(grad_result.astype(f32), axis=0)[None, :]

    block_out = (middle + jnp.dot(combine, result, preferred_element_type=f32)).astype(low)

    slot_dots = dot_f32(out_grad, result, 1, 1)
    grad_gates = sum(
        pick[j] * jnp.sum(jnp.where(hit[j], slot_dots, 0.0), axis=1, keepdims=True)
        for j in range(TOP)
    )
    grad_logits = gate_probs * (
        grad_gates - jnp.sum(gate_probs * grad_gates, axis=-1, keepdims=True)
    )
    grad_router = jnp.dot(grad_logits.T, normed2.astype(f32), precision=highest)
    grad_normed2 = jnp.dot(grad_logits, w_router.astype(f32), precision=highest)
    grad_normed2 = grad_normed2 + jnp.dot(dispatch, grad_slots, preferred_element_type=f32)
    small_in = jnp.concatenate(
        [
            jnp.zeros((8, model_width), f32),
            grad_router,
            grad_bias_out,
            grad_bias_in.reshape(-1, model_width),
        ]
    )
    tokens_grad, dense_out, small_out, expert_out_terms = backward(
        planes,
        own,
        (
            tokens, dense, vecs, sort_rows, middle, qkv, normed, attended, out_grad,
            grad_normed2, terms, small_in,
        ),
    )
    small = lax.dynamic_slice_in_dim(small_out[:16], here * own, own, axis=1)
    bias_in_mine = lax.dynamic_slice_in_dim(
        small_out[16:].reshape(EXPERTS, n_dev * units), here * units, units, axis=1
    )
    expert_in_mine, expert_out_mine = [
        expert_out_terms[w].transpose(1, 0, 2).astype(f32) for w in range(2)
    ]
    return (
        close_rows(block_out),
        close_rows(tokens_grad),
        small[0],
        small[1],
        dense_out[:, : 3 * model_width],
        small[2:4],
        dense_out[:, 3 * model_width :],
        small[4],
        small[5],
        small[6],
        small[8:12].T,
        expert_in_mine,
        bias_in_mine.T,
        expert_out_mine,
        small[12:16],
    )


def solution(mesh):
    row, flat, wide_row = P("fsdp", None), P("fsdp"), P(None, "fsdp")
    unit = P("fsdp", None, None)
    in_specs = (
        row, flat, flat, row, wide_row, row, flat, flat, flat, row,
        unit, row, unit, wide_row, row, row,
    )
    out_specs = (
        row, row, flat, flat, row, wide_row, row, flat, flat, flat, row,
        unit, row, unit, wide_row,
    )
    return jax.shard_map(
        functools.partial(on_device, mesh.shape["fsdp"]),
        mesh=mesh,
        in_specs=in_specs,
        out_specs=out_specs,
        check_vma=False,
    )
```

```python
import functools

import jax
import jax.numpy as jnp
from jax import lax
from jax.experimental import pallas as pl
from jax.experimental.pallas import tpu as pltpu
from jax.sharding import PartitionSpec as P

HD = 64
EXPERTS = 4
TOP = 2
LEN = 197
SEQ_DEV = 2
SLOTS = 256
PLANE = 2 * EXPERTS
LANES = 128


def take_columns(block, widths):
    pieces, at = [], 0
    for width in widths:
        pieces.append(block[:, at : at + width])
        at += width
    return pieces


def dot_f32(left, right, left_dim, right_dim):
    return lax.dot_general(
        left,
        right,
        (((left_dim,), (right_dim,)), ((), ())),
        preferred_element_type=jnp.float32,
    )


def place():
    here = lax.axis_index("fsdp")
    return here % 2, (here // 2) % EXPERTS, here // PLANE


def chip_apart(chip, k):
    x, y = chip % 2, chip // 2
    x = 1 - x if k % 2 else x
    y = 1 - y if k // 2 else y
    return 2 * y + x


def entry_barrier(planes, shifts):
    core, chip, plane = place()
    barrier = pltpu.get_barrier_semaphore()
    greeted = [plane * PLANE + chip * 2 + 1 - core]
    greeted += [plane * PLANE + chip_apart(chip, k) * 2 + core for k in range(1, EXPERTS)]
    greeted += [(plane + s) % planes * PLANE + chip * 2 + core for s in shifts]
    for device in greeted:
        pl.semaphore_signal(
            barrier, inc=1, device_id=(device,), device_id_type=pl.DeviceIdType.MESH
        )
    pl.semaphore_wait(barrier, len(greeted))


def remote(src, dst, send, recv, device):
    return pltpu.make_async_remote_copy(
        src_ref=src,
        dst_ref=dst,
        send_sem=send,
        recv_sem=recv,
        device_id=(device,),
        device_id_type=pl.DeviceIdType.MESH,
    )


def gather_kernel(
    planes, dense_in, weight_in, dense, weight,
    line_send, line_recv, hop_send, hop_recv, chip_send, chip_recv,
    part_send, part_recv, core_send, core_recv, local,
):
    core, chip, plane = place()
    last = planes - 1
    other = plane * PLANE + chip * 2 + 1 - core
    above = (plane + 1) * PLANE + chip * 2 + core
    below = (plane - 1) * PLANE + chip * 2 + core

    def peer(k):
        return plane * PLANE + chip_apart(chip, k) * 2 + core

    def line(slot, up):
        to = slot + 1 if up else (slot - 1) % planes
        return remote(
            dense.at[0, 0, slot], dense.at[0, 0, to],
            line_send.at[int(up), slot], line_recv.at[to], above if up else below,
        )

    def arrived(slot):
        return remote(
            dense.at[0, 0, slot], dense.at[0, 0, slot],
            line_send.at[0, slot], line_recv.at[slot], other,
        )

    def hop(up):
        to = 1 if up else last
        return remote(
            weight.at[:, 0], weight.at[:, to],
            hop_send.at[int(up)], hop_recv.at[to], above if up else below,
        )

    def hop_arrived(slot):
        return remote(
            weight.at[:, slot], weight.at[:, slot], hop_send.at[0], hop_recv.at[slot], other
        )

    parts = [
        remote(
            weight_in.at[:, chip_apart(chip, k)], weight.at[:, 0, k],
            part_send.at[k], part_recv.at[k], peer(k),
        )
        for k in range(1, EXPERTS)
    ]
    own_dense = pltpu.make_async_copy(dense_in, dense.at[0, 0, 0], local.at[0])
    own_part = pltpu.make_async_copy(weight_in.at[:, chip], weight.at[:, 0, 0], local.at[1])
    own_dense.start()
    own_part.start()
    entry_barrier(planes, (1, planes - 1))
    own_dense.wait()

    @pl.when(plane < last)
    def _():
        line(0, True).start()

    @pl.when(plane > 0)
    def _():
        line(0, False).start()

    for part in parts:
        part.start()

    def direct(slot, k):
        return remote(
            dense.at[0, 0, slot], dense.at[0, k, slot],
            chip_send.at[k, slot], chip_recv.at[k, slot], peer(k),
        )

    def first(slot):
        return 1 + slot % 2

    def onward(slot):
        k = first(slot)
        return remote(
            dense.at[0, k, slot], dense.at[0, 3, slot],
            chip_send.at[3, slot], chip_recv.at[3, slot], peer(3 - k),
        )

    def swap(slot, k):
        return remote(
            dense.at[0, k, slot], dense.at[1, k, slot],
            core_send.at[k, slot], core_recv.at[k, slot], other,
        )

    for d in range(1, planes):
        @pl.when(plane >= d)
        def _(d=d):
            arrived(d).wait_recv()

            @pl.when(plane < last)
            def _():
                line(d, True).start()

        @pl.when(plane <= last - d)
        def _(d=d):
            arrived(planes - d).wait_recv()

            @pl.when(plane > 0)
            def _():
                line(planes - d, False).start()

        if d == 1:
            for k in (1, 2):
                direct(0, k).start()
            swap(0, 0).start()

    for slot in range(1, planes):
        for k in (1, 2):
            direct(slot, k).start()
        swap(slot, 0).start()
    own_part.wait()
    for part in parts:
        part.wait()

    @pl.when(plane < last)
    def _():
        hop(True).start()

    @pl.when(plane > 0)
    def _():
        hop(False).start()

    for slot in range(planes):
        direct(slot, first(slot)).wait_recv()
        onward(slot).start()
        swap(slot, first(slot)).start()
    for slot in range(planes):
        direct(slot, 3 - first(slot)).wait_recv()
        swap(slot, 3 - first(slot)).start()
    for slot in range(planes):
        onward(slot).wait_recv()
        swap(slot, 3).start()
    for slot in range(planes):
        for k in (1, 2):
            direct(slot, k).wait_send()
        onward(slot).wait_send()
        for k in range(EXPERTS):
            swap(slot, k).wait()

    @pl.when(plane < last)
    def _():
        line(0, True).wait_send()
        hop(True).wait_send()
        hop_arrived(last).wait_recv()

    @pl.when(plane > 0)
    def _():
        line(0, False).wait_send()
        hop(False).wait_send()
        hop_arrived(1).wait_recv()

    for d in range(1, planes):
        @pl.when((plane >= d) & (plane < last))
        def _(d=d):
            line(d, True).wait_send()

        @pl.when((plane <= last - d) & (plane > 0))
        def _(d=d):
            line(planes - d, False).wait_send()


def gather_weights(dense_mine, weight_mine, n_dev):
    planes = n_dev // PLANE
    _, _, units, width = weight_mine.shape
    sem = pltpu.SemaphoreType.DMA
    any_spec = pl.BlockSpec(memory_space=pl.ANY)
    return pl.pallas_call(
        functools.partial(gather_kernel, planes),
        out_shape=(
            jax.ShapeDtypeStruct((2, EXPERTS, planes) + dense_mine.shape, dense_mine.dtype),
            jax.ShapeDtypeStruct((2, planes, EXPERTS, units, width), weight_mine.dtype),
        ),
        in_specs=[any_spec] * 2,
        out_specs=(any_spec,) * 2,
        scratch_shapes=[
            sem((2, planes)), sem((planes,)), sem((2,)), sem((planes,)),
            sem((EXPERTS, planes)), sem((EXPERTS, planes)),
            sem((EXPERTS,)), sem((EXPERTS,)),
            sem((EXPERTS, planes)), sem((EXPERTS, planes)), sem((2,)),
        ],
        compiler_params=pltpu.CompilerParams(collective_id=1, has_side_effects=True),
        cost_estimate=pl.CostEstimate(flops=0, bytes_accessed=100_000_000, transcendentals=0),
    )(dense_mine, weight_mine)


def forward_exchange_kernel(
    planes, weight_in, tokens, dense, vecs, sort, router, out_grad, routes, columns,
    weight, theirs, got_rows, got_grads, dispatch, combine, gates,
    middle, normed2, qkv, normed, attended,
    heads, rows, grads, hop_send, hop_recv, core_send, core_recv, row_send, row_recv, local,
):
    f32, low = jnp.float32, jnp.bfloat16
    core, chip, plane = place()
    last = planes - 1
    other = plane * PLANE + chip * 2 + 1 - core
    above = (plane + 1) * PLANE + chip * 2 + core
    below = (plane - 1) * PLANE + chip * 2 + core

    def hop(slot, up):
        to = slot + 1 if up else (slot - 1) % planes
        return remote(
            weight.at[:, slot], weight.at[:, to],
            hop_send.at[slot], hop_recv.at[to], above if up else below,
        )

    def hop_arrived(slot):
        return remote(
            weight.at[:, slot], weight.at[:, slot], hop_send.at[slot], hop_recv.at[slot], other
        )

    def swap(slot):
        return remote(
            weight.at[:, slot], theirs.at[:, slot],
            core_send.at[slot], core_recv.at[slot], other,
        )

    keep = [
        pltpu.make_async_copy(rows.at[0], got_rows.at[0], local.at[0]),
        pltpu.make_async_copy(grads.at[0], got_grads.at[0], local.at[1]),
    ]
    entry_barrier(planes, (1, planes - 1))

    def onward(d, wait):
        @pl.when(plane >= d)
        def _():
            if wait:
                hop_arrived(d).wait_recv()

            @pl.when(plane < last)
            def _():
                hop(d, True).start()

            swap(d).start()

        @pl.when(plane <= last - d)
        def _():
            if wait:
                hop_arrived(planes - d).wait_recv()

            @pl.when(plane > 0)
            def _():
                hop(planes - d, False).start()

            swap(planes - d).start()

    onward(1, False)
    trades = []
    for n, (src, dst) in enumerate(((rows, got_rows), (grads, got_grads))):
        for k in range(1, EXPERTS):
            trades.append(
                remote(
                    src.at[k], dst.at[k], row_send.at[n, k], row_recv.at[n, k],
                    plane * PLANE + chip_apart(chip, k) * 2 + core,
                )
            )
    swap(0).start()
    forward_part(
        tokens, dense, vecs, sort, router, middle, normed2, gates, qkv, normed, attended, heads
    )

    lane = lax.broadcasted_iota(jnp.int32, gates.shape, 1)
    logits = jnp.where(lane < EXPERTS, gates[...], -1e30)
    chance = jnp.exp(logits - jnp.max(logits, axis=-1, keepdims=True))
    chance = chance / jnp.sum(chance, axis=-1, keepdims=True)
    gates[...] = chance
    slot = lax.broadcasted_iota(jnp.int32, dispatch.shape, 1)
    marks, shares = 0.0, 0.0
    for j in range(TOP):
        pick = jnp.where(lane == routes[:, j : j + 1], chance, 0.0)
        chosen = jnp.sum(pick, axis=1, keepdims=True)
        hit = slot == columns[:, j : j + 1]
        marks = marks + jnp.where(hit, 1.0, 0.0)
        shares = shares + jnp.where(hit, chosen, 0.0)
    dispatch[...] = marks.astype(low)
    combine[...] = shares.astype(low)
    for n, (sent, table, source) in enumerate(
        ((rows, dispatch, normed2), (grads, combine, out_grad))
    ):
        for k in (3, 1, 2, 0):
            at = pl.ds(k * SLOTS, SLOTS)
            sent[k] = dot_f32(table[:, at], source[...], 0, 0).astype(low)
            if k:
                trades[n * (EXPERTS - 1) + k - 1].start()
        keep[n].start()
    for d in range(2, planes):
        onward(d, True)
    for trade in trades:
        trade.wait()
    for copy in keep:
        copy.wait()
    for slot in range(planes):
        swap(slot).wait()
    for d in range(1, planes):
        @pl.when((plane >= d) & (plane < last))
        def _(d=d):
            hop(d, True).wait_send()

        @pl.when((plane <= last - d) & (plane > 0))
        def _(d=d):
            hop(planes - d, False).wait_send()


def forward_exchange(n_dev, args):
    planes = n_dev // PLANE
    f32, low = jnp.float32, jnp.bfloat16
    weight, tokens = args[:2]
    count, width = tokens.shape
    sem = pltpu.SemaphoreType.DMA
    anywhere = pl.BlockSpec(memory_space=pl.ANY)
    vmem = pl.BlockSpec(memory_space=pltpu.VMEM)
    shape = jax.ShapeDtypeStruct
    slots = (EXPERTS, SLOTS, width)
    table = shape((count, EXPERTS * SLOTS), low)
    return pl.pallas_call(
        functools.partial(forward_exchange_kernel, planes),
        out_shape=(
            shape(weight.shape, low),
            shape(weight.shape, low),
            shape(slots, low),
            shape(slots, low),
            table,
            table,
            shape((count, LANES), f32),
            shape((count, width), f32),
            shape((count, width), low),
            shape((count, 3 * width), low),
            shape((count, width), low),
            shape((count, width), low),
        ),
        in_specs=[anywhere] + [vmem] * (len(args) - 1),
        out_specs=(anywhere,) * 4 + (vmem,) * 8,
        input_output_aliases={0: 0},
        scratch_shapes=[
            pltpu.VMEM((count, width), low),
            pltpu.VMEM(slots, low),
            pltpu.VMEM(slots, low),
            sem((planes,)), sem((planes,)), sem((planes,)), sem((planes,)),
            sem((2, EXPERTS)), sem((2, EXPERTS)), sem((2,)),
        ],
        compiler_params=pltpu.CompilerParams(
            collective_id=2, has_side_effects=True, vmem_limit_bytes=48 * 1024 * 1024
        ),
        cost_estimate=pl.CostEstimate(
            flops=20_000_000_000, bytes_accessed=100_000_000, transcendentals=1_000_000
        ),
    )(*args)


def row_norm(values):
    centred = values - jnp.mean(values, axis=-1, keepdims=True)
    spread = jnp.mean(centred * centred, axis=-1, keepdims=True)
    return centred, lax.rsqrt(spread + 1e-06)


def norm_back(centred, scale, gain_vec, grad):
    inner = grad * gain_vec
    unit = centred * scale
    shared = jnp.mean(inner, axis=-1, keepdims=True)
    slope = jnp.mean(inner * unit, axis=-1, keepdims=True)
    return scale * (inner - shared - unit * slope), unit * grad


def head_lanes(h):
    lane = lax.broadcasted_iota(jnp.int32, (1, 2 * HD), 1)
    return (lane // HD == h).astype(jnp.float32)


def head_probs(queries, key_rows):
    scores = dot_f32(queries, key_rows, 1, 1)
    key = lax.broadcasted_iota(jnp.int32, scores.shape, 1)
    scores = jnp.where(key < LEN, scores, -1e30)
    scores = jnp.exp(scores - jnp.max(scores, axis=-1, keepdims=True))
    return scores * (1.0 / jnp.sum(scores, axis=-1, keepdims=True))


def forward_part(
    tokens, dense, vecs, sort, router, middle, normed2, logits, qkv, normed, attended, heads
):
    f32, low = jnp.float32, jnp.bfloat16
    width = tokens.shape[1]
    rows = tokens.shape[0] // SEQ_DEV
    inputs = tokens[...].astype(f32)
    centred, scale = row_norm(inputs)
    plain = (centred * scale * vecs[0:1] + vecs[1:2]).astype(low)
    normed[...] = dot_f32(plain, sort[...], 1, 0).astype(low)
    queries = dot_f32(normed[...], dense[:, :width], 1, 0)
    qkv[:, :width] = ((queries + vecs[2:3]) * HD ** (-0.5)).astype(low)
    key_rows = dot_f32(normed[...], dense[:, width : 2 * width], 1, 0)
    qkv[:, width : 2 * width] = key_rows.astype(low)
    values = dot_f32(normed[...], dense[:, 2 * width : 3 * width], 1, 0)
    qkv[:, 2 * width : 3 * width] = (values + vecs[3:4]).astype(low)

    @pl.loop(0, width // (2 * HD))
    def _(pair):
        q_at, k_at, v_at = [
            pl.ds(pl.multiple_of(pair * 2 * HD + n * width, 2 * HD), 2 * HD) for n in range(3)
        ]
        for seq in range(SEQ_DEV):
            at = pl.ds(seq * rows, rows)
            total = 0.0
            for h in range(2):
                lanes = head_lanes(h)
                probs = head_probs(qkv[at, q_at] * lanes.astype(low), qkv[at, k_at])
                total = total + dot_f32(probs.astype(low), qkv[at, v_at], 1, 0) * lanes
            heads[at, q_at] = total.astype(low)

    attended[...] = dot_f32(heads[...], sort[...], 1, 0).astype(low)
    branch = dot_f32(attended[...], dense[:, 3 * width : 4 * width], 1, 0)
    middle[...] = inputs + branch + vecs[4:5]
    centred, scale = row_norm(middle[...])
    normed2[...] = (centred * scale * vecs[5:6] + vecs[6:7]).astype(low)
    logits[...] = dot_f32(normed2[...], router[...], 1, 1)


def backward_kernel(
    planes, tokens, dense, vecs, sort, middle, qkv, normed, attended, out_grad,
    normed2, router, combine, dispatch, gates, routes, columns, result, slot_grads,
    terms, small_in, tokens_grad, block_out, dense_out, small_out, expert,
    got_result, got_slots, grad_mid, heads, grads, dense_grad, dense_core, dense_chip, dense_send, dense_line,
    up, down, mine, small, small_got, send, recv, local,
):
    f32, low = jnp.float32, jnp.bfloat16
    width = tokens.shape[1]
    rows = tokens.shape[0] // SEQ_DEV
    own = dense_out.shape[0]
    half, span = planes * EXPERTS * own, planes * own
    core, chip, plane = place()
    last = planes - 1
    other = plane * PLANE + chip * 2 + 1 - core
    above = (plane + 1) * PLANE + chip * 2 + core
    below = (plane - 1) * PLANE + chip * 2 + core
    used = [0]
    sums = small.at[0]

    def copy(src, dst, device):
        used[0] += 1
        return remote(src, dst, send.at[used[0] - 1], recv.at[used[0] - 1], device)

    def peer(k):
        return plane * PLANE + chip_apart(chip, k) * 2 + core

    def away(s):
        return (plane + planes - s) % planes * PLANE + chip * 2 + core

    def total(rows_of):
        return jnp.sum(rows_of, axis=0, keepdims=True)

    first_up, next_up, first_down, next_down = {}, {}, {}, {}
    for t in range(1, planes):
        for w in range(2):
            first_up[t, w] = copy(terms.at[w, t], up.at[t - 1, w], above)
            first_down[t, w] = copy(terms.at[w, planes - t], down.at[t - 1, w], below)
            n = used[0]
            if t > 1:
                next_up[t, w] = remote(
                    up.at[t - 2, w], up.at[t - 1, w], send.at[n - 2], recv.at[n - 2], above
                )
                next_down[t, w] = remote(
                    down.at[t - 2, w], down.at[t - 1, w], send.at[n - 1], recv.at[n - 1], below
                )

    def add_terms(buffer, w, slot):
        @pl.loop(0, EXPERTS)
        def _(k):
            got = buffer[w, k].astype(f32) + terms[w, slot, k].astype(f32)
            buffer[w, k] = got.astype(low)

    def hop(t):
        for w in range(2):
            @pl.when(plane == 0)
            def _(w=w):
                first_up[t, w].start()

            @pl.when(plane == last)
            def _(w=w):
                first_down[t, w].start()

            if t == 1:
                continue

            @pl.when((plane >= 1) & (plane <= t - 1))
            def _(w=w):
                first_up[t - 1, w].wait_recv()
                add_terms(up.at[t - 2], w, t)
                next_up[t, w].start()

            @pl.when((plane <= last - 1) & (plane >= planes - t))
            def _(w=w):
                first_down[t - 1, w].wait_recv()
                add_terms(down.at[t - 2], w, planes - t)
                next_down[t, w].start()

    entry_barrier(planes, range(1, planes))
    hop(1)

    trades, keep = [], []
    for n, (mine_of, got) in enumerate(((result, got_result), (slot_grads, got_slots))):
        for k in range(1, EXPERTS):
            trades.append(copy(mine_of.at[k], got.at[pl.ds(k * SLOTS, SLOTS)], peer(k)))
            trades[-1].start()
        keep.append(
            pltpu.make_async_copy(mine_of.at[0], got.at[pl.ds(0, SLOTS)], local.at[1 + n])
        )
        keep[-1].start()

    def trade_done(n):
        keep[n].wait()
        for k in range(EXPERTS - 1):
            trades[n * (EXPERTS - 1) + k].wait_recv()

    trade_done(0)
    mixed = dot_f32(combine[...], got_result[...], 1, 0)
    block_out[...] = (middle[...] + mixed).astype(low)
    slot_dots = dot_f32(out_grad[...], got_result[...], 1, 1)
    lane = lax.broadcasted_iota(jnp.int32, gates.shape, 1)
    slot = lax.broadcasted_iota(jnp.int32, slot_dots.shape, 1)
    grad_gates = 0.0
    for j in range(TOP):
        picked = jnp.where(slot == columns[:, j : j + 1], slot_dots, 0.0)
        picked = jnp.sum(picked, axis=1, keepdims=True)
        grad_gates = grad_gates + jnp.where(lane == routes[:, j : j + 1], picked, 0.0)
    chance = gates[...]
    shared = jnp.sum(chance * grad_gates, axis=1, keepdims=True)
    grad_logits = chance * (grad_gates - shared)
    upper = grad_logits.astype(low)
    lower = (grad_logits - upper.astype(f32)).astype(low)
    grad_router = dot_f32(upper, normed2[...], 0, 0) + dot_f32(lower, normed2[...], 0, 0)
    grad = dot_f32(upper, router[...], 1, 0) + dot_f32(lower, router[...], 1, 0)
    trade_done(1)
    grad = grad + dot_f32(dispatch[...], got_slots[...], 1, 0)
    for t in range(2, planes - 1):
        hop(t)
    centred, scale = row_norm(middle[...])
    back, gain_terms = norm_back(centred, scale, vecs[5:6], grad)
    sums[5:6] = total(gain_terms)
    sums[6:7] = total(grad)
    sums[7:8] = jnp.zeros((1, width), f32)
    sums[8:12] = grad_router[:EXPERTS]
    sums[12:] = small_in[12:]
    grad_mid[...] = out_grad[...].astype(f32) + back
    branch = grad_mid[...].astype(low)
    sums[4:5] = total(branch.astype(f32))
    dense_grad[:, 3 * width : 4 * width] = dot_f32(attended[...], branch, 0, 0).astype(low)
    grad_att = dot_f32(branch, dense[:, 3 * width : 4 * width], 1, 1).astype(low)
    heads[...] = dot_f32(grad_att, sort[...], 1, 1).astype(low)

    @pl.loop(0, width // (2 * HD))
    def _(pair):
        q_at, k_at, v_at = [
            pl.ds(pl.multiple_of(pair * 2 * HD + n * width, 2 * HD), 2 * HD) for n in range(3)
        ]
        for seq in range(SEQ_DEV):
            at = pl.ds(seq * rows, rows)
            queries, key_rows, values = qkv[at, q_at], qkv[at, k_at], qkv[at, v_at]
            grad_out = heads[at, q_at]
            grad_q, grad_k, grad_v = 0.0, 0.0, 0.0
            for h in range(2):
                lanes = head_lanes(h)
                probs = head_probs(queries * lanes.astype(low), key_rows)
                grad_probs = dot_f32(grad_out * lanes.astype(low), values, 1, 1)
                grad_v = grad_v + dot_f32(probs.astype(low), grad_out, 0, 0) * lanes
                shared = jnp.sum(probs * grad_probs, axis=-1, keepdims=True)
                scores = (probs * (grad_probs - shared)).astype(low)
                grad_q = grad_q + dot_f32(scores, key_rows, 1, 0) * lanes
                grad_k = grad_k + dot_f32(scores, queries, 0, 0) * lanes
            grads[at, q_at] = (grad_q.astype(low).astype(f32) * HD ** (-0.5)).astype(low)
            grads[at, k_at] = grad_k.astype(low)
            grads[at, v_at] = grad_v.astype(low)

    sums[2:3] = total(grads[:, :width].astype(f32))
    sums[3:4] = total(grads[:, 2 * width :].astype(f32))
    for n in range(3):
        at = pl.ds(n * width, width)
        dense_grad[:, at] = dot_f32(normed[...], grads[:, at], 0, 0).astype(low)
    core_copies = [
        copy(
            dense_grad.at[pl.ds(half + k * span, span)],
            dense_core.at[pl.ds(k * span, span)],
            other,
        )
        for k in (1, 2, 3, 0)
    ]
    for sent in core_copies:
        sent.start()
    if planes > 2:
        hop(last)
    grad = dot_f32(grads[...], dense[:, : 3 * width], 1, 1)
    upper = grad.astype(low)
    lower = (grad - upper.astype(f32)).astype(low)
    grad = dot_f32(upper, sort[...], 1, 1) + dot_f32(lower, sort[...], 1, 1)
    centred, scale = row_norm(tokens[...].astype(f32))
    back, gain_terms = norm_back(centred, scale, vecs[0:1], grad)
    sums[0:1] = total(gain_terms)
    sums[1:2] = total(grad)
    tokens_grad[...] = grad_mid[...] + back

    small_copies = [copy(small.at[0], small_got.at[0], other)]
    small_copies += [copy(small.at[k], small_got.at[k], peer(k)) for k in (1, 2)]
    small_copies += [
        copy(small.at[3], small_got.at[2 + s], away(s)) for s in range(1, planes)
    ]

    def small_step(n):
        small_copies[n].wait_recv()
        small[n + 1] = small[n] + small_got[n]

    small_copies[0].start()
    chip_copies = []
    for n, k in enumerate((1, 2, 3, 0)):
        core_copies[n].wait_recv()
        at = pl.ds(k * span, span)
        both = dense_grad[at].astype(f32) + dense_core[at].astype(f32)
        dense_grad[at] = both.astype(low)
        if k:
            chip_copies.append(copy(dense_grad.at[at], dense_chip.at[k - 1], peer(k)))
            chip_copies[-1].start()
    small_step(0)
    small_copies[1].start()
    small_step(1)
    small_copies[2].start()
    small_step(2)
    for sent in small_copies[3:]:
        sent.start()
    for sent in chip_copies:
        sent.wait_recv()
    line_copies = []
    for n in range(4):
        at = pl.ds(n * width, width)
        both = dense_grad[:span, at].astype(f32)
        for k in range(1, EXPERTS):
            both = both + dense_chip[k - 1, :, at].astype(f32)
        dense_out[:, at] = both[:own]
        for s in range(1, planes):
            dense_send[s, :, at] = both[s * own : (s + 1) * own].astype(low)
    for s in range(1, planes):
        line_copies.append(copy(dense_send.at[s], dense_line.at[s], away(s)))
        line_copies[-1].start()

    def finish(w, buffers):
        @pl.loop(0, EXPERTS)
        def _(k):
            got = terms[w, 0, k].astype(f32)
            for buffer in buffers:
                got = got + buffer[last - 1, w, k].astype(f32)
            mine[w, k] = got.astype(low)

    unit_copies = []
    for w in range(2):
        @pl.when(plane >= 1)
        def _(w=w):
            first_up[last, w].wait_recv()

        @pl.when(plane <= last - 1)
        def _(w=w):
            first_down[last, w].wait_recv()

        @pl.when(plane == 0)
        def _(w=w):
            finish(w, [down])

        @pl.when(plane == last)
        def _(w=w):
            finish(w, [up])

        @pl.when((plane > 0) & (plane < last))
        def _(w=w):
            finish(w, [up, down])

        for k in range(1, EXPERTS):
            unit_copies.append(copy(mine.at[w, k], expert.at[w, chip], peer(k)))
            unit_copies[-1].start()
    kept = pltpu.make_async_copy(mine.at[:, 0], expert.at[:, chip], local.at[0])
    kept.start()
    for sent in line_copies:
        sent.wait_recv()
    for s in range(1, planes):
        dense_out[...] = dense_out[...] + dense_line[s].astype(f32)
    for sent in small_copies[3:]:
        sent.wait_recv()
    every = small[3]
    for s in range(1, planes):
        every = every + small_got[2 + s]
    small_out[...] = every
    for sent in trades + core_copies + small_copies + chip_copies + line_copies:
        sent.wait_send()
    for t in range(1, planes):
        for w in range(2):
            @pl.when(plane <= t - 1)
            def _(t=t, w=w):
                first_up[t, w].wait_send()

            @pl.when(plane >= planes - t)
            def _(t=t, w=w):
                first_down[t, w].wait_send()

    kept.wait()
    for sent in unit_copies:
        sent.wait()


def backward(planes, own, args):
    f32, low = jnp.float32, jnp.bfloat16
    square, width = args[0].shape, args[0].shape[1]
    terms, small_in = args[-2:]
    units = terms.shape[3]
    block = (2, EXPERTS, units, width)
    half, span, wide = planes * EXPERTS * own, planes * own, 4 * width
    spec = pl.BlockSpec(memory_space=pltpu.VMEM)
    shape = jax.ShapeDtypeStruct
    copies = 26 + 8 * planes
    anywhere = pl.BlockSpec(memory_space=pl.ANY)
    return pl.pallas_call(
        functools.partial(backward_kernel, planes),
        out_shape=(
            shape(square, f32),
            shape(square, low),
            shape((own, wide), f32),
            shape(small_in.shape, f32),
            shape(block, low),
        ),
        in_specs=[spec] * (len(args) - 4) + [anywhere] * 2 + [spec] * 2,
        out_specs=(spec,) * 5,
        scratch_shapes=[
            pltpu.VMEM((EXPERTS * SLOTS, width), low),
            pltpu.VMEM((EXPERTS * SLOTS, width), low),
            pltpu.VMEM(square, f32),
            pltpu.VMEM(square, low),
            pltpu.VMEM((square[0], 3 * width), low),
            pltpu.VMEM((2 * half, wide), low),
            pltpu.VMEM((half, wide), low),
            pltpu.VMEM((EXPERTS - 1, span, wide), low),
            pltpu.VMEM((planes, own, wide), low),
            pltpu.VMEM((planes, own, wide), low),
            pltpu.VMEM((planes - 1,) + block, low),
            pltpu.VMEM((planes - 1,) + block, low),
            pltpu.VMEM(block, low),
            pltpu.VMEM((4,) + small_in.shape, f32),
            pltpu.VMEM((2 + planes,) + small_in.shape, f32),
            pltpu.SemaphoreType.DMA((copies,)),
            pltpu.SemaphoreType.DMA((copies,)),
            pltpu.SemaphoreType.DMA((3,)),
        ],
        compiler_params=pltpu.CompilerParams(
            collective_id=3, has_side_effects=True, vmem_limit_bytes=62 * 1024 * 1024
        ),
        cost_estimate=pl.CostEstimate(
            flops=20_000_000_000, bytes_accessed=50_000_000, transcendentals=1_000_000
        ),
    )(*args)


def expert_kernel(
    planes, rows, grads, own_half, other_half, bias_in, bias_out,
    result, slot_grads, terms, grad_bias, total, back, sent, got, send, recv,
):
    f32, low = jnp.float32, jnp.bfloat16
    step = pl.program_id(0)
    core, chip, plane = place()
    other = plane * PLANE + chip * 2 + 1 - core
    count = rows.shape[0]

    @pl.when(step == 0)
    def _():
        barrier = pltpu.get_barrier_semaphore()
        pl.semaphore_signal(
            barrier, inc=1, device_id=(other,), device_id_type=pl.DeviceIdType.MESH
        )
        pl.semaphore_wait(barrier, 1)
        total[...] = jnp.zeros_like(total)
        back[...] = jnp.zeros_like(back)

    def block_terms(weight):
        w_in, w_out = weight[0, 0], weight[1, 0]
        pre = dot_f32(rows[...], w_in, 1, 1) + bias_in[0]
        square = pre * pre
        bend = jnp.tanh(0.7978845608 * pre * (1.0 + 0.044715 * square))
        hidden = (0.5 * pre * (1.0 + bend)).astype(low)
        slope = 0.5 * (1.0 + bend) + 0.5 * pre * (1.0 - bend * bend) * 0.7978845608 * (
            1.0 + 3 * 0.044715 * square
        )
        grad_pre = slope * dot_f32(grads[...], w_out, 1, 1)
        grad_pre = grad_pre.astype(low)
        grad_bias[0] = jnp.sum(grad_pre.astype(f32), axis=0, keepdims=True)
        total[...] += dot_f32(hidden, w_out, 1, 0)
        back[...] += dot_f32(grad_pre, w_in, 1, 0)
        return (
            dot_f32(grad_pre, rows[...], 0, 0),
            dot_f32(hidden, grads[...], 0, 0),
        )

    def swap(n):
        return remote(sent.at[n], got.at[n], send.at[n], recv.at[n], other)

    @pl.when(step < planes)
    def _():
        for w, term in enumerate(block_terms(other_half)):
            sent[step, w] = term.astype(low)
        swap(step).start()

    @pl.when(step >= planes)
    def _():
        mine = block_terms(own_half)
        swap(step - planes).wait()
        for w, term in enumerate(mine):
            terms[w, 0] = (term + got[step - planes, w].astype(f32)).astype(low)

    @pl.when(step == 2 * planes - 1)
    def _():
        result[...] = (total[...] + bias_out[...]).astype(low)
        slot_grads[...] = back[...].astype(low)


def experts_apply(planes, rows, grads, own_half, other_half, bias_in, bias_out):
    f32, low = jnp.float32, jnp.bfloat16
    count, width = rows.shape
    block = own_half.shape[2]
    shape = jax.ShapeDtypeStruct
    whole = pl.BlockSpec((count, width), lambda i: (0, 0))
    bias = pl.BlockSpec((1, 1, block), lambda i: ((i + planes) % (2 * planes), 0, 0))

    def weights(index):
        return pl.BlockSpec((2, 1, block, width), lambda i: (0, index(i), 0, 0))

    own = weights(lambda i: jnp.maximum(i - planes, 0))
    theirs = weights(lambda i: jnp.minimum(i, planes - 1))
    return pl.pallas_call(
        functools.partial(expert_kernel, planes),
        grid=(2 * planes,),
        out_shape=(
            shape((count, width), low),
            shape((count, width), low),
            shape(own_half.shape, low),
            shape(bias_in.shape, f32),
        ),
        in_specs=[
            whole, whole, own, theirs, bias, pl.BlockSpec((1, width), lambda i: (0, 0)),
        ],
        out_specs=(whole, whole, own, bias),
        scratch_shapes=[
            pltpu.VMEM((count, width), f32),
            pltpu.VMEM((count, width), f32),
            pltpu.VMEM((planes, 2, block, width), low),
            pltpu.VMEM((planes, 2, block, width), low),
            pltpu.SemaphoreType.DMA((planes,)),
            pltpu.SemaphoreType.DMA((planes,)),
        ],
        compiler_params=pltpu.CompilerParams(
            collective_id=4, has_side_effects=True, vmem_limit_bytes=60 * 1024 * 1024
        ),
        cost_estimate=pl.CostEstimate(
            flops=30_000_000_000, bytes_accessed=40_000_000, transcendentals=3_000_000
        ),
    )(rows, grads, own_half, other_half, bias_in, bias_out)


def on_device(
    n_dev,
    tokens,
    ln1_gain,
    ln1_shift,
    qkv_weight,
    qv_bias,
    proj_weight,
    proj_bias,
    ln2_gain,
    ln2_shift,
    router_weight,
    expert_in,
    expert_in_bias,
    expert_out,
    expert_out_bias,
    routes,
    out_grad,
):
    highest = lax.Precision.HIGHEST
    f32 = jnp.float32
    low = jnp.bfloat16
    model_width = tokens.shape[1]
    spare = -LEN % 16
    row_count = SEQ_DEV * (LEN + spare)

    def spread_rows(array, fill=0):
        array = array.reshape(SEQ_DEV, LEN, -1)
        array = jnp.pad(array, ((0, 0), (0, spare), (0, 0)), constant_values=fill)
        return array.reshape(row_count, -1)

    def close_rows(array):
        return array.reshape(SEQ_DEV, LEN + spare, -1)[:, :LEN].reshape(SEQ_DEV * LEN, -1)

    tokens = spread_rows(tokens)
    out_grad = spread_rows(out_grad)
    routes = spread_rows(routes, -1)
    own = qkv_weight.shape[0]
    units = expert_in.shape[0]
    planes = n_dev // PLANE
    each = range(EXPERTS)
    wide = 4 * model_width
    here = lax.axis_index("fsdp")
    core = here % 2
    chip = (here // 2) % EXPERTS
    plane = here // PLANE

    def owner_dense(j):
        s, k, c = j % planes, (j // planes) % EXPERTS, j // (planes * EXPERTS)
        return ((plane - s + planes) % planes) * PLANE + (chip ^ k) * 2 + (core ^ c)

    def owner_units(j):
        k, s, c = j % EXPERTS, (j // EXPERTS) % planes, j // (planes * EXPERTS)
        return ((plane - s + planes) % planes) * PLANE + (chip ^ k) * 2 + (core ^ c)

    devices = jnp.arange(n_dev, dtype=jnp.int32)
    sort_dense = (devices[:, None] == owner_dense(devices)[None, :]).astype(low)
    sort_units = (devices[:, None] == owner_units(devices)[None, :]).astype(low)
    features = jnp.arange(model_width, dtype=jnp.int32)
    home = owner_dense(features // own) * own + features % own
    sort_rows = (features[:, None] == home[None, :]).astype(low)

    small_parts = [
        ln1_gain,
        ln1_shift,
        qv_bias.reshape(-1),
        proj_bias,
        ln2_gain,
        ln2_shift,
        router_weight.T.reshape(-1),
        expert_out_bias.reshape(-1),
        expert_in_bias.T.reshape(-1),
    ]
    small_widths = [p.shape[0] for p in small_parts]
    small_total = sum(small_widths)
    small_room = own * LANES
    small_mine = jnp.pad(jnp.concatenate(small_parts), (0, small_room - small_total))
    dense_mine = jnp.concatenate(
        [qkv_weight, proj_weight, small_mine.reshape(own, LANES)], axis=1
    )
    weight_mine = jnp.stack([expert_in.transpose(1, 0, 2), expert_out.transpose(1, 0, 2)])
    dense, own_half = gather_weights(dense_mine, weight_mine, n_dev)
    dense = dense.reshape(model_width, wide + LANES)

    small = dense[:, wide:].reshape(n_dev, small_room)
    small = dot_f32(sort_dense, small, 1, 0).astype(low)
    gain1, shift1, bias_qv, bias_proj, gain2, shift2, w_router, bias_out, bias_in = take_columns(
        small, small_widths
    )
    vecs = [gain1, shift1, bias_qv[:, :own], bias_qv[:, own:], bias_proj, gain2, shift2, shift2]
    vecs = jnp.stack([v.reshape(-1) for v in vecs]).astype(f32)
    w_router = jnp.stack([p.reshape(-1) for p in take_columns(w_router, [own] * EXPERTS)])
    bias_out = jnp.stack([p.reshape(-1) for p in take_columns(bias_out, [own] * EXPERTS)])
    mine = (jnp.arange(EXPERTS, dtype=jnp.int32) == chip).astype(f32)
    bias_out = jnp.sum(bias_out.astype(f32) * mine[:, None], axis=0)
    bias_in = jnp.stack(take_columns(bias_in, [units] * EXPERTS)).astype(f32)
    bias_in = jnp.sum(bias_in * mine[:, None, None], axis=0).astype(low)
    bias_in = dot_f32(sort_units, bias_in, 0, 0).reshape(2 * planes, 1, EXPERTS * units)

    experts = jnp.arange(EXPERTS, dtype=jnp.int32)[None, :]
    pick = [(routes[:, j : j + 1] == experts).astype(f32) for j in range(TOP)]
    picked = pick[0] + pick[1]
    tri = jnp.arange(row_count)[:, None] > jnp.arange(row_count)[None, :]
    before = dot_f32(tri.astype(low), picked.astype(low), 1, 0)
    columns = []
    for j in range(TOP):
        slot = jnp.sum(pick[j] * before, axis=1, keepdims=True).astype(jnp.int32)
        columns.append((routes[:, j : j + 1] ^ chip) * SLOTS + slot)
    columns = jnp.concatenate(columns, axis=1)
    router = jnp.pad(w_router, ((0, LANES - EXPERTS), (0, 0)))
    (
        own_half, other_half, slot_rows, grad_result, dispatch, combine, gates,
        middle, normed2, qkv, normed, attended,
    ) = forward_exchange(
        n_dev,
        (own_half, tokens, dense, vecs, sort_rows, router, out_grad, routes, columns),
    )
    slot_rows = slot_rows.reshape(EXPERTS * SLOTS, model_width)
    grad_result = grad_result.reshape(EXPERTS * SLOTS, model_width)
    blocks = (2, planes, EXPERTS * units, model_width)
    result, grad_slots, terms, grad_bias_in = experts_apply(
        planes,
        slot_rows,
        grad_result,
        own_half.reshape(blocks),
        other_half.reshape(blocks),
        bias_in,
        bias_out[None, :],
    )
    terms = terms.reshape(2, planes, EXPERTS, units, model_width)
    grad_bias_in = jnp.dot(
        sort_units.astype(f32), grad_bias_in.reshape(n_dev, units), precision=highest
    )
    grad_bias_in = mine[:, None] * grad_bias_in.reshape(1, n_dev * units)
    grad_bias_out = mine[:, None] * jnp.sum(grad_result.astype(f32), axis=0)[None, :]
    small_in = jnp.concatenate(
        [
            jnp.zeros((12, model_width), f32),
            grad_bias_out,
            grad_bias_in.reshape(-1, model_width),
        ]
    )
    four = (EXPERTS, SLOTS, model_width)
    tokens_grad, block_out, dense_out, small_out, expert_out_terms = backward(
        planes,
        own,
        (
            tokens, dense, vecs, sort_rows, middle, qkv, normed, attended, out_grad,
            normed2, router, combine, dispatch, gates, routes, columns,
            result.reshape(four), grad_slots.reshape(four), terms, small_in,
        ),
    )
    small = lax.dynamic_slice_in_dim(small_out[:16], here * own, own, axis=1)
    bias_in_mine = lax.dynamic_slice_in_dim(
        small_out[16:].reshape(EXPERTS, n_dev * units), here * units, units, axis=1
    )
    expert_in_mine, expert_out_mine = [
        expert_out_terms[w].transpose(1, 0, 2).astype(f32) for w in range(2)
    ]
    return (
        close_rows(block_out),
        close_rows(tokens_grad),
        small[0],
        small[1],
        dense_out[:, : 3 * model_width],
        small[2:4],
        dense_out[:, 3 * model_width :],
        small[4],
        small[5],
        small[6],
        small[8:12].T,
        expert_in_mine,
        bias_in_mine.T,
        expert_out_mine,
        small[12:16],
    )


def solution(mesh):
    row, flat, wide_row = P("fsdp", None), P("fsdp"), P(None, "fsdp")
    unit = P("fsdp", None, None)
    in_specs = (
        row, flat, flat, row, wide_row, row, flat, flat, flat, row,
        unit, row, unit, wide_row, row, row,
    )
    out_specs = (
        row, row, flat, flat, row, wide_row, row, flat, flat, flat, row,
        unit, row, unit, wide_row,
    )
    return jax.shard_map(
        functools.partial(on_device, mesh.shape["fsdp"]),
        mesh=mesh,
        in_specs=in_specs,
        out_specs=out_specs,
        check_vma=False,
    )
```

```python
import functools

import jax
import jax.numpy as jnp
from jax import lax
from jax.experimental import pallas as pl
from jax.experimental.pallas import tpu as pltpu
from jax.sharding import PartitionSpec as P

HD = 64
EXPERTS = 4
TOP = 2
LEN = 197
SEQ_DEV = 2
SLOTS = 256
PLANE = 2 * EXPERTS
LANES = 128


def take_columns(block, widths):
    pieces, at = [], 0
    for width in widths:
        pieces.append(block[:, at : at + width])
        at += width
    return pieces


def dot_f32(left, right, left_dim, right_dim):
    return lax.dot_general(
        left,
        right,
        (((left_dim,), (right_dim,)), ((), ())),
        preferred_element_type=jnp.float32,
    )


def place():
    here = lax.axis_index("fsdp")
    return here % 2, (here // 2) % EXPERTS, here // PLANE


def chip_apart(chip, k):
    x, y = chip % 2, chip // 2
    x = 1 - x if k % 2 else x
    y = 1 - y if k // 2 else y
    return 2 * y + x


def entry_barrier(planes, shifts):
    core, chip, plane = place()
    barrier = pltpu.get_barrier_semaphore()
    greeted = [plane * PLANE + chip * 2 + 1 - core]
    greeted += [plane * PLANE + chip_apart(chip, k) * 2 + core for k in range(1, EXPERTS)]
    greeted += [(plane + s) % planes * PLANE + chip * 2 + core for s in shifts]
    for device in greeted:
        pl.semaphore_signal(
            barrier, inc=1, device_id=(device,), device_id_type=pl.DeviceIdType.MESH
        )
    pl.semaphore_wait(barrier, len(greeted))


def remote(src, dst, send, recv, device):
    return pltpu.make_async_remote_copy(
        src_ref=src,
        dst_ref=dst,
        send_sem=send,
        recv_sem=recv,
        device_id=(device,),
        device_id_type=pl.DeviceIdType.MESH,
    )


def gather_kernel(
    planes, dense_in, weight_in, dense, weight,
    line_send, line_recv, hop_send, hop_recv, chip_send, chip_recv,
    part_send, part_recv, core_send, core_recv, local,
):
    core, chip, plane = place()
    last = planes - 1
    other = plane * PLANE + chip * 2 + 1 - core
    above = (plane + 1) * PLANE + chip * 2 + core
    below = (plane - 1) * PLANE + chip * 2 + core

    def peer(k):
        return plane * PLANE + chip_apart(chip, k) * 2 + core

    def line(slot, up):
        to = slot + 1 if up else (slot - 1) % planes
        return remote(
            dense.at[0, 0, slot], dense.at[0, 0, to],
            line_send.at[int(up), slot], line_recv.at[to], above if up else below,
        )

    def arrived(slot):
        return remote(
            dense.at[0, 0, slot], dense.at[0, 0, slot],
            line_send.at[0, slot], line_recv.at[slot], other,
        )

    def hop(up):
        to = 1 if up else last
        return remote(
            weight.at[:, 0], weight.at[:, to],
            hop_send.at[int(up)], hop_recv.at[to], above if up else below,
        )

    def hop_arrived(slot):
        return remote(
            weight.at[:, slot], weight.at[:, slot], hop_send.at[0], hop_recv.at[slot], other
        )

    parts = [
        remote(
            weight_in.at[:, chip_apart(chip, k)], weight.at[:, 0, k],
            part_send.at[k], part_recv.at[k], peer(k),
        )
        for k in range(1, EXPERTS)
    ]
    own_dense = pltpu.make_async_copy(dense_in, dense.at[0, 0, 0], local.at[0])
    own_part = pltpu.make_async_copy(weight_in.at[:, chip], weight.at[:, 0, 0], local.at[1])
    own_dense.start()
    own_part.start()
    entry_barrier(planes, (1, planes - 1))
    own_dense.wait()

    @pl.when(plane < last)
    def _():
        line(0, True).start()

    @pl.when(plane > 0)
    def _():
        line(0, False).start()

    for part in parts:
        part.start()

    def direct(slot, k):
        return remote(
            dense.at[0, 0, slot], dense.at[0, k, slot],
            chip_send.at[k, slot], chip_recv.at[k, slot], peer(k),
        )

    def first(slot):
        return 1 + slot % 2

    def onward(slot):
        k = first(slot)
        return remote(
            dense.at[0, k, slot], dense.at[0, 3, slot],
            chip_send.at[3, slot], chip_recv.at[3, slot], peer(3 - k),
        )

    def swap(slot, k):
        return remote(
            dense.at[0, k, slot], dense.at[1, k, slot],
            core_send.at[k, slot], core_recv.at[k, slot], other,
        )

    for d in range(1, planes):
        @pl.when(plane >= d)
        def _(d=d):
            arrived(d).wait_recv()

            @pl.when(plane < last)
            def _():
                line(d, True).start()

        @pl.when(plane <= last - d)
        def _(d=d):
            arrived(planes - d).wait_recv()

            @pl.when(plane > 0)
            def _():
                line(planes - d, False).start()

        if d == 1:
            for k in (1, 2):
                direct(0, k).start()
            swap(0, 0).start()

    for slot in range(1, planes):
        for k in (1, 2):
            direct(slot, k).start()
        swap(slot, 0).start()
    own_part.wait()
    for part in parts:
        part.wait()

    @pl.when(plane < last)
    def _():
        hop(True).start()

    @pl.when(plane > 0)
    def _():
        hop(False).start()

    for slot in range(planes):
        direct(slot, first(slot)).wait_recv()
        onward(slot).start()
        swap(slot, first(slot)).start()
    for slot in range(planes):
        direct(slot, 3 - first(slot)).wait_recv()
        swap(slot, 3 - first(slot)).start()
    for slot in range(planes):
        onward(slot).wait_recv()
        swap(slot, 3).start()
    for slot in range(planes):
        for k in (1, 2):
            direct(slot, k).wait_send()
        onward(slot).wait_send()
        for k in range(EXPERTS):
            swap(slot, k).wait()

    @pl.when(plane < last)
    def _():
        line(0, True).wait_send()
        hop(True).wait_send()
        hop_arrived(last).wait_recv()

    @pl.when(plane > 0)
    def _():
        line(0, False).wait_send()
        hop(False).wait_send()
        hop_arrived(1).wait_recv()

    for d in range(1, planes):
        @pl.when((plane >= d) & (plane < last))
        def _(d=d):
            line(d, True).wait_send()

        @pl.when((plane <= last - d) & (plane > 0))
        def _(d=d):
            line(planes - d, False).wait_send()


def gather_weights(dense_mine, weight_mine, n_dev):
    planes = n_dev // PLANE
    _, _, units, width = weight_mine.shape
    sem = pltpu.SemaphoreType.DMA
    any_spec = pl.BlockSpec(memory_space=pl.ANY)
    return pl.pallas_call(
        functools.partial(gather_kernel, planes),
        out_shape=(
            jax.ShapeDtypeStruct((2, EXPERTS, planes) + dense_mine.shape, dense_mine.dtype),
            jax.ShapeDtypeStruct((2, planes, EXPERTS, units, width), weight_mine.dtype),
        ),
        in_specs=[any_spec] * 2,
        out_specs=(any_spec,) * 2,
        scratch_shapes=[
            sem((2, planes)), sem((planes,)), sem((2,)), sem((planes,)),
            sem((EXPERTS, planes)), sem((EXPERTS, planes)),
            sem((EXPERTS,)), sem((EXPERTS,)),
            sem((EXPERTS, planes)), sem((EXPERTS, planes)), sem((2,)),
        ],
        compiler_params=pltpu.CompilerParams(collective_id=1, has_side_effects=True),
        cost_estimate=pl.CostEstimate(flops=0, bytes_accessed=100_000_000, transcendentals=0),
    )(dense_mine, weight_mine)


def forward_exchange_kernel(
    planes, weight_in, tokens, dense, vecs, sort, router, out_grad, routes, columns,
    weight, theirs, got_rows, got_grads, dispatch, combine, gates,
    middle, normed2, qkv, normed, attended,
    heads, rows, grads, hop_send, hop_recv, core_send, core_recv, row_send, row_recv, local,
):
    f32, low = jnp.float32, jnp.bfloat16
    core, chip, plane = place()
    last = planes - 1
    other = plane * PLANE + chip * 2 + 1 - core
    above = (plane + 1) * PLANE + chip * 2 + core
    below = (plane - 1) * PLANE + chip * 2 + core

    def hop(slot, up):
        to = slot + 1 if up else (slot - 1) % planes
        return remote(
            weight.at[:, slot], weight.at[:, to],
            hop_send.at[slot], hop_recv.at[to], above if up else below,
        )

    def hop_arrived(slot):
        return remote(
            weight.at[:, slot], weight.at[:, slot], hop_send.at[slot], hop_recv.at[slot], other
        )

    def swap(slot):
        return remote(
            weight.at[:, slot], theirs.at[:, slot],
            core_send.at[slot], core_recv.at[slot], other,
        )

    keep = [
        pltpu.make_async_copy(rows.at[0], got_rows.at[0], local.at[0]),
        pltpu.make_async_copy(grads.at[0], got_grads.at[0], local.at[1]),
    ]
    entry_barrier(planes, (1, planes - 1))

    def onward(d, wait):
        @pl.when(plane >= d)
        def _():
            if wait:
                hop_arrived(d).wait_recv()

            @pl.when(plane < last)
            def _():
                hop(d, True).start()

            swap(d).start()

        @pl.when(plane <= last - d)
        def _():
            if wait:
                hop_arrived(planes - d).wait_recv()

            @pl.when(plane > 0)
            def _():
                hop(planes - d, False).start()

            swap(planes - d).start()

    onward(1, False)
    trades = []
    for n, (src, dst) in enumerate(((rows, got_rows), (grads, got_grads))):
        for k in range(1, EXPERTS):
            trades.append(
                remote(
                    src.at[k], dst.at[k], row_send.at[n, k], row_recv.at[n, k],
                    plane * PLANE + chip_apart(chip, k) * 2 + core,
                )
            )
    swap(0).start()
    forward_part(
        tokens, dense, vecs, sort, router, middle, normed2, gates, qkv, normed, attended, heads
    )

    lane = lax.broadcasted_iota(jnp.int32, gates.shape, 1)
    logits = jnp.where(lane < EXPERTS, gates[...], -1e30)
    chance = jnp.exp(logits - jnp.max(logits, axis=-1, keepdims=True))
    chance = chance / jnp.sum(chance, axis=-1, keepdims=True)
    gates[...] = chance
    slot = lax.broadcasted_iota(jnp.int32, dispatch.shape, 1)
    marks, shares = 0.0, 0.0
    for j in range(TOP):
        pick = jnp.where(lane == routes[:, j : j + 1], chance, 0.0)
        chosen = jnp.sum(pick, axis=1, keepdims=True)
        hit = slot == columns[:, j : j + 1]
        marks = marks + jnp.where(hit, 1.0, 0.0)
        shares = shares + jnp.where(hit, chosen, 0.0)
    dispatch[...] = marks.astype(low)
    combine[...] = shares.astype(low)
    for n, (sent, table, source) in enumerate(
        ((rows, dispatch, normed2), (grads, combine, out_grad))
    ):
        for k in (3, 1, 2, 0):
            at = pl.ds(k * SLOTS, SLOTS)
            sent[k] = dot_f32(table[:, at], source[...], 0, 0).astype(low)
            if k:
                trades[n * (EXPERTS - 1) + k - 1].start()
        keep[n].start()
    for d in range(2, planes):
        onward(d, True)
    for trade in trades:
        trade.wait()
    for copy in keep:
        copy.wait()
    for slot in range(planes):
        swap(slot).wait()
    for d in range(1, planes):
        @pl.when((plane >= d) & (plane < last))
        def _(d=d):
            hop(d, True).wait_send()

        @pl.when((plane <= last - d) & (plane > 0))
        def _(d=d):
            hop(planes - d, False).wait_send()


def forward_exchange(n_dev, args):
    planes = n_dev // PLANE
    f32, low = jnp.float32, jnp.bfloat16
    weight, tokens = args[:2]
    count, width = tokens.shape
    sem = pltpu.SemaphoreType.DMA
    anywhere = pl.BlockSpec(memory_space=pl.ANY)
    vmem = pl.BlockSpec(memory_space=pltpu.VMEM)
    shape = jax.ShapeDtypeStruct
    slots = (EXPERTS, SLOTS, width)
    table = shape((count, EXPERTS * SLOTS), low)
    return pl.pallas_call(
        functools.partial(forward_exchange_kernel, planes),
        out_shape=(
            shape(weight.shape, low),
            shape(weight.shape, low),
            shape(slots, low),
            shape(slots, low),
            table,
            table,
            shape((count, LANES), f32),
            shape((count, width), f32),
            shape((count, width), low),
            shape((count, 3 * width), low),
            shape((count, width), low),
            shape((count, width), low),
        ),
        in_specs=[anywhere] + [vmem] * (len(args) - 1),
        out_specs=(anywhere,) * 4 + (vmem,) * 8,
        input_output_aliases={0: 0},
        scratch_shapes=[
            pltpu.VMEM((count, width), low),
            pltpu.VMEM(slots, low),
            pltpu.VMEM(slots, low),
            sem((planes,)), sem((planes,)), sem((planes,)), sem((planes,)),
            sem((2, EXPERTS)), sem((2, EXPERTS)), sem((2,)),
        ],
        compiler_params=pltpu.CompilerParams(
            collective_id=2, has_side_effects=True, vmem_limit_bytes=48 * 1024 * 1024
        ),
        cost_estimate=pl.CostEstimate(
            flops=20_000_000_000, bytes_accessed=100_000_000, transcendentals=1_000_000
        ),
    )(*args)


def row_norm(values):
    centred = values - jnp.mean(values, axis=-1, keepdims=True)
    spread = jnp.mean(centred * centred, axis=-1, keepdims=True)
    return centred, lax.rsqrt(spread + 1e-06)


def norm_back(centred, scale, gain_vec, grad):
    inner = grad * gain_vec
    unit = centred * scale
    shared = jnp.mean(inner, axis=-1, keepdims=True)
    slope = jnp.mean(inner * unit, axis=-1, keepdims=True)
    return scale * (inner - shared - unit * slope), unit * grad


def head_lanes(h):
    lane = lax.broadcasted_iota(jnp.int32, (1, 2 * HD), 1)
    return (lane // HD == h).astype(jnp.float32)


def head_probs(queries, key_rows):
    scores = dot_f32(queries, key_rows, 1, 1)
    key = lax.broadcasted_iota(jnp.int32, scores.shape, 1)
    scores = jnp.where(key < LEN, scores, -1e30)
    scores = jnp.exp(scores - jnp.max(scores, axis=-1, keepdims=True))
    return scores * (1.0 / jnp.sum(scores, axis=-1, keepdims=True))


def forward_part(
    tokens, dense, vecs, sort, router, middle, normed2, logits, qkv, normed, attended, heads
):
    f32, low = jnp.float32, jnp.bfloat16
    width = tokens.shape[1]
    rows = tokens.shape[0] // SEQ_DEV
    inputs = tokens[...].astype(f32)
    centred, scale = row_norm(inputs)
    plain = (centred * scale * vecs[0:1] + vecs[1:2]).astype(low)
    normed[...] = dot_f32(plain, sort[...], 1, 0).astype(low)
    queries = dot_f32(normed[...], dense[:, :width], 1, 0)
    qkv[:, :width] = ((queries + vecs[2:3]) * HD ** (-0.5)).astype(low)
    key_rows = dot_f32(normed[...], dense[:, width : 2 * width], 1, 0)
    qkv[:, width : 2 * width] = key_rows.astype(low)
    values = dot_f32(normed[...], dense[:, 2 * width : 3 * width], 1, 0)
    qkv[:, 2 * width : 3 * width] = (values + vecs[3:4]).astype(low)

    @pl.loop(0, width // (2 * HD))
    def _(pair):
        q_at, k_at, v_at = [
            pl.ds(pl.multiple_of(pair * 2 * HD + n * width, 2 * HD), 2 * HD) for n in range(3)
        ]
        for seq in range(SEQ_DEV):
            at = pl.ds(seq * rows, rows)
            total = 0.0
            for h in range(2):
                lanes = head_lanes(h)
                probs = head_probs(qkv[at, q_at] * lanes.astype(low), qkv[at, k_at])
                total = total + dot_f32(probs.astype(low), qkv[at, v_at], 1, 0) * lanes
            heads[at, q_at] = total.astype(low)

    attended[...] = dot_f32(heads[...], sort[...], 1, 0).astype(low)
    branch = dot_f32(attended[...], dense[:, 3 * width : 4 * width], 1, 0)
    middle[...] = inputs + branch + vecs[4:5]
    centred, scale = row_norm(middle[...])
    normed2[...] = (centred * scale * vecs[5:6] + vecs[6:7]).astype(low)
    logits[...] = dot_f32(normed2[...], router[...], 1, 1)


def backward_kernel(
    planes, tokens, dense, vecs, sort, middle, qkv, normed, attended, out_grad,
    normed2, router, combine, dispatch, gates, routes, columns, result, slot_grads,
    terms, small_in, tokens_grad, block_out, dense_out, small_out, expert,
    got_result, got_slots, grad_mid, heads, grads, dense_grad, dense_core, dense_chip, dense_send, dense_line,
    up, down, mine, small, small_got, send, recv, local,
):
    f32, low = jnp.float32, jnp.bfloat16
    width = tokens.shape[1]
    rows = tokens.shape[0] // SEQ_DEV
    own = dense_out.shape[0]
    half, span = planes * EXPERTS * own, planes * own
    core, chip, plane = place()
    last = planes - 1
    other = plane * PLANE + chip * 2 + 1 - core
    above = (plane + 1) * PLANE + chip * 2 + core
    below = (plane - 1) * PLANE + chip * 2 + core
    used = [0]
    sums = small.at[0]

    def copy(src, dst, device):
        used[0] += 1
        return remote(src, dst, send.at[used[0] - 1], recv.at[used[0] - 1], device)

    def peer(k):
        return plane * PLANE + chip_apart(chip, k) * 2 + core

    def away(s):
        return (plane + planes - s) % planes * PLANE + chip * 2 + core

    def total(rows_of):
        return jnp.sum(rows_of, axis=0, keepdims=True)

    first_up, next_up, first_down, next_down = {}, {}, {}, {}
    for t in range(1, planes):
        for w in range(2):
            first_up[t, w] = copy(terms.at[w, t], up.at[t - 1, w], above)
            first_down[t, w] = copy(terms.at[w, planes - t], down.at[t - 1, w], below)
            n = used[0]
            if t > 1:
                next_up[t, w] = remote(
                    up.at[t - 2, w], up.at[t - 1, w], send.at[n - 2], recv.at[n - 2], above
                )
                next_down[t, w] = remote(
                    down.at[t - 2, w], down.at[t - 1, w], send.at[n - 1], recv.at[n - 1], below
                )

    def add_terms(buffer, w, slot):
        @pl.loop(0, EXPERTS)
        def _(k):
            got = buffer[w, k].astype(f32) + terms[w, slot, k].astype(f32)
            buffer[w, k] = got.astype(low)

    def hop(t):
        for w in range(2):
            @pl.when(plane == 0)
            def _(w=w):
                first_up[t, w].start()

            @pl.when(plane == last)
            def _(w=w):
                first_down[t, w].start()

            if t == 1:
                continue

            @pl.when((plane >= 1) & (plane <= t - 1))
            def _(w=w):
                first_up[t - 1, w].wait_recv()
                add_terms(up.at[t - 2], w, t)
                next_up[t, w].start()

            @pl.when((plane <= last - 1) & (plane >= planes - t))
            def _(w=w):
                first_down[t - 1, w].wait_recv()
                add_terms(down.at[t - 2], w, planes - t)
                next_down[t, w].start()

    core_copies, chip_copies, line_copies = {}, {}, {}

    def columns_of(n):
        return pl.ds(n * width, width)

    def to_core(n):
        at = columns_of(n)
        core_copies[n] = copy(dense_grad.at[pl.ds(half, half), at], dense_core.at[:, at], other)
        core_copies[n].start()

    def to_chips(n):
        at = columns_of(n)
        core_copies[n].wait_recv()
        chip_copies[n] = []
        for k in (1, 2, 3, 0):
            mine_at = pl.ds(k * span, span)
            both = dense_grad[mine_at, at].astype(f32) + dense_core[mine_at, at].astype(f32)
            dense_grad[mine_at, at] = both.astype(low)
            if k:
                sent = copy(
                    dense_grad.at[mine_at, at], dense_chip.at[k - 1, :, at], peer(k)
                )
                sent.start()
                chip_copies[n].append(sent)

    def to_line(n):
        at = columns_of(n)
        for sent in chip_copies[n]:
            sent.wait_recv()
        both = dense_grad[:span, at].astype(f32)
        for k in range(1, EXPERTS):
            both = both + dense_chip[k - 1, :, at].astype(f32)
        dense_out[:, at] = both[:own]
        line_copies[n] = []
        for s in range(1, planes):
            dense_send[n, s] = both[s * own : (s + 1) * own].astype(low)
            sent = copy(dense_send.at[n, s], dense_line.at[n, s], away(s))
            sent.start()
            line_copies[n].append(sent)

    entry_barrier(planes, range(1, planes))
    hop(1)

    trades, keep = [], []
    for n, (mine_of, got) in enumerate(((result, got_result), (slot_grads, got_slots))):
        for k in range(1, EXPERTS):
            trades.append(copy(mine_of.at[k], got.at[pl.ds(k * SLOTS, SLOTS)], peer(k)))
            if n == 0:
                trades[-1].start()
        keep.append(
            pltpu.make_async_copy(mine_of.at[0], got.at[pl.ds(0, SLOTS)], local.at[1 + n])
        )
        keep[-1].start()

    def trade_done(n):
        keep[n].wait()
        for k in range(EXPERTS - 1):
            trades[n * (EXPERTS - 1) + k].wait_recv()

    trade_done(0)
    for trade in trades[EXPERTS - 1 :]:
        trade.start()
    mixed = dot_f32(combine[...], got_result[...], 1, 0)
    block_out[...] = (middle[...] + mixed).astype(low)
    slot_dots = dot_f32(out_grad[...], got_result[...], 1, 1)
    lane = lax.broadcasted_iota(jnp.int32, gates.shape, 1)
    slot = lax.broadcasted_iota(jnp.int32, slot_dots.shape, 1)
    grad_gates = 0.0
    for j in range(TOP):
        picked = jnp.where(slot == columns[:, j : j + 1], slot_dots, 0.0)
        picked = jnp.sum(picked, axis=1, keepdims=True)
        grad_gates = grad_gates + jnp.where(lane == routes[:, j : j + 1], picked, 0.0)
    chance = gates[...]
    shared = jnp.sum(chance * grad_gates, axis=1, keepdims=True)
    grad_logits = chance * (grad_gates - shared)
    upper = grad_logits.astype(low)
    lower = (grad_logits - upper.astype(f32)).astype(low)
    grad_router = dot_f32(upper, normed2[...], 0, 0) + dot_f32(lower, normed2[...], 0, 0)
    grad = dot_f32(upper, router[...], 1, 0) + dot_f32(lower, router[...], 1, 0)
    trade_done(1)
    grad = grad + dot_f32(dispatch[...], got_slots[...], 1, 0)
    for t in range(2, planes - 1):
        hop(t)
    centred, scale = row_norm(middle[...])
    back, gain_terms = norm_back(centred, scale, vecs[5:6], grad)
    sums[5:6] = total(gain_terms)
    sums[6:7] = total(grad)
    sums[7:8] = jnp.zeros((1, width), f32)
    sums[8:12] = grad_router[:EXPERTS]
    sums[12:] = small_in[12:]
    grad_mid[...] = out_grad[...].astype(f32) + back
    branch = grad_mid[...].astype(low)
    sums[4:5] = total(branch.astype(f32))
    dense_grad[:, 3 * width : 4 * width] = dot_f32(attended[...], branch, 0, 0).astype(low)
    to_core(3)
    grad_att = dot_f32(branch, dense[:, 3 * width : 4 * width], 1, 1).astype(low)
    heads[...] = dot_f32(grad_att, sort[...], 1, 1).astype(low)

    @pl.loop(0, width // (2 * HD))
    def _(pair):
        q_at, k_at, v_at = [
            pl.ds(pl.multiple_of(pair * 2 * HD + n * width, 2 * HD), 2 * HD) for n in range(3)
        ]
        for seq in range(SEQ_DEV):
            at = pl.ds(seq * rows, rows)
            queries, key_rows, values = qkv[at, q_at], qkv[at, k_at], qkv[at, v_at]
            grad_out = heads[at, q_at]
            grad_q, grad_k, grad_v = 0.0, 0.0, 0.0
            for h in range(2):
                lanes = head_lanes(h)
                probs = head_probs(queries * lanes.astype(low), key_rows)
                grad_probs = dot_f32(grad_out * lanes.astype(low), values, 1, 1)
                grad_v = grad_v + dot_f32(probs.astype(low), grad_out, 0, 0) * lanes
                shared = jnp.sum(probs * grad_probs, axis=-1, keepdims=True)
                scores = (probs * (grad_probs - shared)).astype(low)
                grad_q = grad_q + dot_f32(scores, key_rows, 1, 0) * lanes
                grad_k = grad_k + dot_f32(scores, queries, 0, 0) * lanes
            grads[at, q_at] = (grad_q.astype(low).astype(f32) * HD ** (-0.5)).astype(low)
            grads[at, k_at] = grad_k.astype(low)
            grads[at, v_at] = grad_v.astype(low)

    to_chips(3)
    for n in range(3):
        at = columns_of(n)
        dense_grad[:, at] = dot_f32(normed[...], grads[:, at], 0, 0).astype(low)
        to_core(n)
    for n in range(3):
        to_chips(n)
    if planes > 2:
        hop(last)
    to_line(3)
    sums[2:3] = total(grads[:, :width].astype(f32))
    sums[3:4] = total(grads[:, 2 * width :].astype(f32))
    grad = dot_f32(grads[...], dense[:, : 3 * width], 1, 1)
    upper = grad.astype(low)
    lower = (grad - upper.astype(f32)).astype(low)
    grad = dot_f32(upper, sort[...], 1, 1) + dot_f32(lower, sort[...], 1, 1)
    centred, scale = row_norm(tokens[...].astype(f32))
    back, gain_terms = norm_back(centred, scale, vecs[0:1], grad)
    sums[0:1] = total(gain_terms)
    sums[1:2] = total(grad)
    tokens_grad[...] = grad_mid[...] + back

    small_copies = [copy(small.at[0], small_got.at[0], other)]
    small_copies += [copy(small.at[k], small_got.at[k], peer(k)) for k in (1, 2)]
    small_copies += [
        copy(small.at[3], small_got.at[2 + s], away(s)) for s in range(1, planes)
    ]

    def small_step(n):
        small_copies[n].wait_recv()
        small[n + 1] = small[n] + small_got[n]

    small_copies[0].start()
    small_step(0)
    small_copies[1].start()
    small_step(1)
    small_copies[2].start()
    small_step(2)
    for sent in small_copies[3:]:
        sent.start()
    for n in range(3):
        to_line(n)

    def finish(w, buffers):
        @pl.loop(0, EXPERTS)
        def _(k):
            got = terms[w, 0, k].astype(f32)
            for buffer in buffers:
                got = got + buffer[last - 1, w, k].astype(f32)
            mine[w, k] = got.astype(low)

    unit_copies = []
    for w in range(2):
        @pl.when(plane >= 1)
        def _(w=w):
            first_up[last, w].wait_recv()

        @pl.when(plane <= last - 1)
        def _(w=w):
            first_down[last, w].wait_recv()

        @pl.when(plane == 0)
        def _(w=w):
            finish(w, [down])

        @pl.when(plane == last)
        def _(w=w):
            finish(w, [up])

        @pl.when((plane > 0) & (plane < last))
        def _(w=w):
            finish(w, [up, down])

        for k in range(1, EXPERTS):
            unit_copies.append(copy(mine.at[w, k], expert.at[w, chip], peer(k)))
            unit_copies[-1].start()
    kept = pltpu.make_async_copy(mine.at[:, 0], expert.at[:, chip], local.at[0])
    kept.start()
    for n in range(4):
        got = dense_out[:, columns_of(n)]
        for s in range(1, planes):
            line_copies[n][s - 1].wait_recv()
            got = got + dense_line[n, s].astype(f32)
        dense_out[:, columns_of(n)] = got
    for sent in small_copies[3:]:
        sent.wait_recv()
    every = small[3]
    for s in range(1, planes):
        every = every + small_got[2 + s]
    small_out[...] = every
    for n in range(4):
        for sent in [core_copies[n]] + chip_copies[n] + line_copies[n]:
            sent.wait_send()
    for sent in trades + small_copies:
        sent.wait_send()
    for t in range(1, planes):
        for w in range(2):
            @pl.when(plane <= t - 1)
            def _(t=t, w=w):
                first_up[t, w].wait_send()

            @pl.when(plane >= planes - t)
            def _(t=t, w=w):
                first_down[t, w].wait_send()

    kept.wait()
    for sent in unit_copies:
        sent.wait()


def backward(planes, own, args):
    f32, low = jnp.float32, jnp.bfloat16
    square, width = args[0].shape, args[0].shape[1]
    terms, small_in = args[-2:]
    units = terms.shape[3]
    block = (2, EXPERTS, units, width)
    half, span, wide = planes * EXPERTS * own, planes * own, 4 * width
    spec = pl.BlockSpec(memory_space=pltpu.VMEM)
    shape = jax.ShapeDtypeStruct
    copies = 40 + 12 * planes
    anywhere = pl.BlockSpec(memory_space=pl.ANY)
    return pl.pallas_call(
        functools.partial(backward_kernel, planes),
        out_shape=(
            shape(square, f32),
            shape(square, low),
            shape((own, wide), f32),
            shape(small_in.shape, f32),
            shape(block, low),
        ),
        in_specs=[spec] * (len(args) - 4) + [anywhere] * 2 + [spec] * 2,
        out_specs=(spec,) * 5,
        scratch_shapes=[
            pltpu.VMEM((EXPERTS * SLOTS, width), low),
            pltpu.VMEM((EXPERTS * SLOTS, width), low),
            pltpu.VMEM(square, f32),
            pltpu.VMEM(square, low),
            pltpu.VMEM((square[0], 3 * width), low),
            pltpu.VMEM((2 * half, wide), low),
            pltpu.VMEM((half, wide), low),
            pltpu.VMEM((EXPERTS - 1, span, wide), low),
            pltpu.VMEM((4, planes, own, width), low),
            pltpu.VMEM((4, planes, own, width), low),
            pltpu.VMEM((planes - 1,) + block, low),
            pltpu.VMEM((planes - 1,) + block, low),
            pltpu.VMEM(block, low),
            pltpu.VMEM((4,) + small_in.shape, f32),
            pltpu.VMEM((2 + planes,) + small_in.shape, f32),
            pltpu.SemaphoreType.DMA((copies,)),
            pltpu.SemaphoreType.DMA((copies,)),
            pltpu.SemaphoreType.DMA((3,)),
        ],
        compiler_params=pltpu.CompilerParams(
            collective_id=3, has_side_effects=True, vmem_limit_bytes=62 * 1024 * 1024
        ),
        cost_estimate=pl.CostEstimate(
            flops=20_000_000_000, bytes_accessed=50_000_000, transcendentals=1_000_000
        ),
    )(*args)


def expert_kernel(
    planes, rows, grads, own_half, other_half, bias_in, bias_out,
    result, slot_grads, terms, grad_bias, total, back, sent, got, send, recv,
):
    f32, low = jnp.float32, jnp.bfloat16
    step = pl.program_id(0)
    core, chip, plane = place()
    other = plane * PLANE + chip * 2 + 1 - core
    count = rows.shape[0]

    @pl.when(step == 0)
    def _():
        barrier = pltpu.get_barrier_semaphore()
        pl.semaphore_signal(
            barrier, inc=1, device_id=(other,), device_id_type=pl.DeviceIdType.MESH
        )
        pl.semaphore_wait(barrier, 1)
        total[...] = jnp.zeros_like(total)
        back[...] = jnp.zeros_like(back)

    def block_terms(weight):
        w_in, w_out = weight[0, 0], weight[1, 0]
        pre = dot_f32(rows[...], w_in, 1, 1) + bias_in[0]
        square = pre * pre
        bend = jnp.tanh(0.7978845608 * pre * (1.0 + 0.044715 * square))
        hidden = (0.5 * pre * (1.0 + bend)).astype(low)
        slope = 0.5 * (1.0 + bend) + 0.5 * pre * (1.0 - bend * bend) * 0.7978845608 * (
            1.0 + 3 * 0.044715 * square
        )
        grad_pre = slope * dot_f32(grads[...], w_out, 1, 1)
        grad_pre = grad_pre.astype(low)
        grad_bias[0] = jnp.sum(grad_pre.astype(f32), axis=0, keepdims=True)
        total[...] += dot_f32(hidden, w_out, 1, 0)
        back[...] += dot_f32(grad_pre, w_in, 1, 0)
        return (
            dot_f32(grad_pre, rows[...], 0, 0),
            dot_f32(hidden, grads[...], 0, 0),
        )

    def swap(n):
        return remote(sent.at[n], got.at[n], send.at[n], recv.at[n], other)

    @pl.when(step < planes)
    def _():
        for w, term in enumerate(block_terms(other_half)):
            sent[step, w] = term.astype(low)
        swap(step).start()

    @pl.when(step >= planes)
    def _():
        mine = block_terms(own_half)
        swap(step - planes).wait()
        for w, term in enumerate(mine):
            terms[w, 0] = (term + got[step - planes, w].astype(f32)).astype(low)

    @pl.when(step == 2 * planes - 1)
    def _():
        result[...] = (total[...] + bias_out[...]).astype(low)
        slot_grads[...] = back[...].astype(low)


def experts_apply(planes, rows, grads, own_half, other_half, bias_in, bias_out):
    f32, low = jnp.float32, jnp.bfloat16
    count, width = rows.shape
    block = own_half.shape[2]
    shape = jax.ShapeDtypeStruct
    whole = pl.BlockSpec((count, width), lambda i: (0, 0))
    bias = pl.BlockSpec((1, 1, block), lambda i: ((i + planes) % (2 * planes), 0, 0))

    def weights(index):
        return pl.BlockSpec((2, 1, block, width), lambda i: (0, index(i), 0, 0))

    own = weights(lambda i: jnp.maximum(i - planes, 0))
    theirs = weights(lambda i: jnp.minimum(i, planes - 1))
    return pl.pallas_call(
        functools.partial(expert_kernel, planes),
        grid=(2 * planes,),
        out_shape=(
            shape((count, width), low),
            shape((count, width), low),
            shape(own_half.shape, low),
            shape(bias_in.shape, f32),
        ),
        in_specs=[
            whole, whole, own, theirs, bias, pl.BlockSpec((1, width), lambda i: (0, 0)),
        ],
        out_specs=(whole, whole, own, bias),
        scratch_shapes=[
            pltpu.VMEM((count, width), f32),
            pltpu.VMEM((count, width), f32),
            pltpu.VMEM((planes, 2, block, width), low),
            pltpu.VMEM((planes, 2, block, width), low),
            pltpu.SemaphoreType.DMA((planes,)),
            pltpu.SemaphoreType.DMA((planes,)),
        ],
        compiler_params=pltpu.CompilerParams(
            collective_id=4, has_side_effects=True, vmem_limit_bytes=60 * 1024 * 1024
        ),
        cost_estimate=pl.CostEstimate(
            flops=30_000_000_000, bytes_accessed=40_000_000, transcendentals=3_000_000
        ),
    )(rows, grads, own_half, other_half, bias_in, bias_out)


def on_device(
    n_dev,
    tokens,
    ln1_gain,
    ln1_shift,
    qkv_weight,
    qv_bias,
    proj_weight,
    proj_bias,
    ln2_gain,
    ln2_shift,
    router_weight,
    expert_in,
    expert_in_bias,
    expert_out,
    expert_out_bias,
    routes,
    out_grad,
):
    highest = lax.Precision.HIGHEST
    f32 = jnp.float32
    low = jnp.bfloat16
    model_width = tokens.shape[1]
    spare = -LEN % 16
    row_count = SEQ_DEV * (LEN + spare)

    def spread_rows(array, fill=0):
        array = array.reshape(SEQ_DEV, LEN, -1)
        array = jnp.pad(array, ((0, 0), (0, spare), (0, 0)), constant_values=fill)
        return array.reshape(row_count, -1)

    def close_rows(array):
        return array.reshape(SEQ_DEV, LEN + spare, -1)[:, :LEN].reshape(SEQ_DEV * LEN, -1)

    tokens = spread_rows(tokens)
    out_grad = spread_rows(out_grad)
    routes = spread_rows(routes, -1)
    own = qkv_weight.shape[0]
    units = expert_in.shape[0]
    planes = n_dev // PLANE
    each = range(EXPERTS)
    wide = 4 * model_width
    here = lax.axis_index("fsdp")
    core = here % 2
    chip = (here // 2) % EXPERTS
    plane = here // PLANE

    def owner_dense(j):
        s, k, c = j % planes, (j // planes) % EXPERTS, j // (planes * EXPERTS)
        return ((plane - s + planes) % planes) * PLANE + (chip ^ k) * 2 + (core ^ c)

    def owner_units(j):
        k, s, c = j % EXPERTS, (j // EXPERTS) % planes, j // (planes * EXPERTS)
        return ((plane - s + planes) % planes) * PLANE + (chip ^ k) * 2 + (core ^ c)

    devices = jnp.arange(n_dev, dtype=jnp.int32)
    sort_dense = (devices[:, None] == owner_dense(devices)[None, :]).astype(low)
    sort_units = (devices[:, None] == owner_units(devices)[None, :]).astype(low)
    features = jnp.arange(model_width, dtype=jnp.int32)
    home = owner_dense(features // own) * own + features % own
    sort_rows = (features[:, None] == home[None, :]).astype(low)

    small_parts = [
        ln1_gain,
        ln1_shift,
        qv_bias.reshape(-1),
        proj_bias,
        ln2_gain,
        ln2_shift,
        router_weight.T.reshape(-1),
        expert_out_bias.reshape(-1),
        expert_in_bias.T.reshape(-1),
    ]
    small_widths = [p.shape[0] for p in small_parts]
    small_total = sum(small_widths)
    small_room = own * LANES
    small_mine = jnp.pad(jnp.concatenate(small_parts), (0, small_room - small_total))
    dense_mine = jnp.concatenate(
        [qkv_weight, proj_weight, small_mine.reshape(own, LANES)], axis=1
    )
    weight_mine = jnp.stack([expert_in.transpose(1, 0, 2), expert_out.transpose(1, 0, 2)])
    dense, own_half = gather_weights(dense_mine, weight_mine, n_dev)
    dense = dense.reshape(model_width, wide + LANES)

    small = dense[:, wide:].reshape(n_dev, small_room)
    small = dot_f32(sort_dense, small, 1, 0).astype(low)
    gain1, shift1, bias_qv, bias_proj, gain2, shift2, w_router, bias_out, bias_in = take_columns(
        small, small_widths
    )
    vecs = [gain1, shift1, bias_qv[:, :own], bias_qv[:, own:], bias_proj, gain2, shift2, shift2]
    vecs = jnp.stack([v.reshape(-1) for v in vecs]).astype(f32)
    w_router = jnp.stack([p.reshape(-1) for p in take_columns(w_router, [own] * EXPERTS)])
    bias_out = jnp.stack([p.reshape(-1) for p in take_columns(bias_out, [own] * EXPERTS)])
    mine = (jnp.arange(EXPERTS, dtype=jnp.int32) == chip).astype(f32)
    bias_out = jnp.sum(bias_out.astype(f32) * mine[:, None], axis=0)
    bias_in = jnp.stack(take_columns(bias_in, [units] * EXPERTS)).astype(f32)
    bias_in = jnp.sum(bias_in * mine[:, None, None], axis=0).astype(low)
    bias_in = dot_f32(sort_units, bias_in, 0, 0).reshape(2 * planes, 1, EXPERTS * units)

    experts = jnp.arange(EXPERTS, dtype=jnp.int32)[None, :]
    pick = [(routes[:, j : j + 1] == experts).astype(f32) for j in range(TOP)]
    picked = pick[0] + pick[1]
    tri = jnp.arange(row_count)[:, None] > jnp.arange(row_count)[None, :]
    before = dot_f32(tri.astype(low), picked.astype(low), 1, 0)
    columns = []
    for j in range(TOP):
        slot = jnp.sum(pick[j] * before, axis=1, keepdims=True).astype(jnp.int32)
        columns.append((routes[:, j : j + 1] ^ chip) * SLOTS + slot)
    columns = jnp.concatenate(columns, axis=1)
    router = jnp.pad(w_router, ((0, LANES - EXPERTS), (0, 0)))
    (
        own_half, other_half, slot_rows, grad_result, dispatch, combine, gates,
        middle, normed2, qkv, normed, attended,
    ) = forward_exchange(
        n_dev,
        (own_half, tokens, dense, vecs, sort_rows, router, out_grad, routes, columns),
    )
    slot_rows = slot_rows.reshape(EXPERTS * SLOTS, model_width)
    grad_result = grad_result.reshape(EXPERTS * SLOTS, model_width)
    blocks = (2, planes, EXPERTS * units, model_width)
    result, grad_slots, terms, grad_bias_in = experts_apply(
        planes,
        slot_rows,
        grad_result,
        own_half.reshape(blocks),
        other_half.reshape(blocks),
        bias_in,
        bias_out[None, :],
    )
    terms = terms.reshape(2, planes, EXPERTS, units, model_width)
    grad_bias_in = jnp.dot(
        sort_units.astype(f32), grad_bias_in.reshape(n_dev, units), precision=highest
    )
    grad_bias_in = mine[:, None] * grad_bias_in.reshape(1, n_dev * units)
    grad_bias_out = mine[:, None] * jnp.sum(grad_result.astype(f32), axis=0)[None, :]
    small_in = jnp.concatenate(
        [
            jnp.zeros((12, model_width), f32),
            grad_bias_out,
            grad_bias_in.reshape(-1, model_width),
        ]
    )
    four = (EXPERTS, SLOTS, model_width)
    tokens_grad, block_out, dense_out, small_out, expert_out_terms = backward(
        planes,
        own,
        (
            tokens, dense, vecs, sort_rows, middle, qkv, normed, attended, out_grad,
            normed2, router, combine, dispatch, gates, routes, columns,
            result.reshape(four), grad_slots.reshape(four), terms, small_in,
        ),
    )
    small = lax.dynamic_slice_in_dim(small_out[:16], here * own, own, axis=1)
    bias_in_mine = lax.dynamic_slice_in_dim(
        small_out[16:].reshape(EXPERTS, n_dev * units), here * units, units, axis=1
    )
    expert_in_mine, expert_out_mine = [
        expert_out_terms[w].transpose(1, 0, 2).astype(f32) for w in range(2)
    ]
    return (
        close_rows(block_out),
        close_rows(tokens_grad),
        small[0],
        small[1],
        dense_out[:, : 3 * model_width],
        small[2:4],
        dense_out[:, 3 * model_width :],
        small[4],
        small[5],
        small[6],
        small[8:12].T,
        expert_in_mine,
        bias_in_mine.T,
        expert_out_mine,
        small[12:16],
    )


def solution(mesh):
    row, flat, wide_row = P("fsdp", None), P("fsdp"), P(None, "fsdp")
    unit = P("fsdp", None, None)
    in_specs = (
        row, flat, flat, row, wide_row, row, flat, flat, flat, row,
        unit, row, unit, wide_row, row, row,
    )
    out_specs = (
        row, row, flat, flat, row, wide_row, row, flat, flat, flat, row,
        unit, row, unit, wide_row,
    )
    return jax.shard_map(
        functools.partial(on_device, mesh.shape["fsdp"]),
        mesh=mesh,
        in_specs=in_specs,
        out_specs=out_specs,
        check_vma=False,
    )
```
